128 devices in a mesh: ctx: 8 (over y, x_lo), fsdp: 16 (over x_hi, z, core).
Axes of the slice: x: 4 (x_hi: 2, x_lo: 2; x = x_hi * 2 + x_lo), y: 4, z: 4, core: 2. Of those that a mesh axis runs over, the one named last changes fastest.
Arguments:
- hidden_in: bfloat16 [16, 1024, 1536], P('fsdp', 'ctx'), may hold values from -6 to 6
- block_order: int32 [16, 16], P('fsdp'), may hold values from 0 to 15, as said below
- attn_gain: bfloat16 [1536], P('fsdp'), may hold values from 0.099609375 to 1.8984375
- w_qkv: bfloat16 [1536, 2048], P('fsdp'), may hold values from -0.21875 to 0.21875
- b_qkv: bfloat16 [2048], P('fsdp'), may hold values from -3 to 3
- w_out: bfloat16 [1536, 1536], P('fsdp'), may hold values from -0.625 to 0.625
- mlp_gain: bfloat16 [1536], P('fsdp'), may hold values from 0.099609375 to 1.8984375
- w_gate_up: bfloat16 [1536, 17920], P('fsdp'), may hold values from -0.15625 to 0.15625
- w_down: bfloat16 [8960, 1536], P('fsdp'), may hold values from -0.09375 to 0.09375
- cotangent: bfloat16 [16, 1024, 1536], P('fsdp', 'ctx'), may hold values from -6 to 6
Outputs:
- hidden_out: float32 [16, 1024, 1536], P('fsdp', 'ctx')
- grad_in: float32 [16, 1024, 1536], P('fsdp', 'ctx')
- grad_attn_gain: float32 [1536], P('fsdp')
- grad_w_qkv: float32 [1536, 2048], P('fsdp')
- grad_b_qkv: float32 [2048], P('fsdp')
- grad_w_out: float32 [1536, 1536], P('fsdp')
- grad_mlp_gain: float32 [1536], P('fsdp')
- grad_w_gate_up: float32 [1536, 17920], P('fsdp')
- grad_w_down: float32 [8960, 1536], P('fsdp')
The draws below stay inside these ranges and needn't reach their ends.
Inputs may be any that keep to these rules, and one draw needn't show every extreme that they name: `block_order`: each row holds every number 0 to 15 once, and columns 2 c and 2 c + 1 hold two numbers that add up to 15.
All inputs are finite; a program needn't handle non-finite values.
Results may differ from the reference program's by a relative error of at most 0.025.
Values may be sent and summed in bfloat16 or wider, within the bound.
No kernel may reach another device: no remote copies, remote signals or barrier semaphores. Data moves between devices by JAX's collectives and lax.ppermute only.
A program may use at most 448 MiB of HBM per device.

```python
import math
import jax
import jax.numpy as jnp
from jax import lax

D = 1536
H = 12
KVH = 2
HD = 128
FF = 8960
LEN = 1024
QKV = 2048
SEQS = 16
BLOCKS = 16
BLOCK_ROWS = 64
QB = 512


def draw_block_order(key, part):
    key = jax.random.fold_in(key, 11)
    order_key, flip_key = jax.random.split(key)
    pair_count = BLOCKS // 2
    orders = jax.vmap(lambda sub_key: jax.random.permutation(sub_key, pair_count))(jax.random.split(order_key, SEQS))
    flip_bits = jax.random.randint(flip_key, (SEQS, pair_count), 0, 2)
    leading = jnp.where(flip_bits == 1, BLOCKS - 1 - orders, orders)
    trailing = BLOCKS - 1 - leading
    return jnp.stack([leading, trailing], axis=-1).reshape(SEQS, BLOCKS).astype(jnp.int32)


def block_scale(key, extent, cuts, low, high):
    level, own = 1.0, jax.random.fold_in(key, 6)
    for dim, blocks in cuts:
        draws = jnp.exp(jax.random.uniform(jax.random.fold_in(own, dim), (blocks,), jnp.float32, low / len(cuts), high / len(cuts)))
        level = level * jnp.repeat(draws, extent[dim] // blocks).reshape([-1 if axis == dim else 1 for axis in range(len(extent))])
    return level


def scatter_about(own_key, extent, spread, bound, cuts=(), kind=jnp.bfloat16):
    drawn = jax.random.normal(own_key, extent, jnp.float32) * spread
    if len(cuts) > 0:
        drawn = block_scale(own_key, extent, cuts, -0.22, 0.18) * drawn
    return jnp.clip(drawn, min=-bound, max=bound).astype(kind)


def setup_inputs(seed: int = 0) -> dict:
    keys = jax.random.split(jax.random.key(seed), 11)
    return {
        "hidden_in": scatter_about(keys[0], (SEQS, LEN, D), 1.0, 6.0, ((0, 16), (1, 8))),
        "block_order": draw_block_order(jax.random.fold_in(keys[10], 71), 0),
        "attn_gain": jnp.clip(1.0 + 0.18 * jax.random.normal(keys[2], (D,), jnp.float32), 0.099609375, 1.8984375).astype(jnp.bfloat16),
        "w_qkv": scatter_about(keys[3], (D, QKV), (D // 2) ** -0.5, 0.21875, ((0, 16),)),
        "b_qkv": scatter_about(keys[4], (QKV,), 0.5, 3.0, ((0, 16),)),
        "w_out": scatter_about(keys[5], (D, D), (D // 16) ** -0.5, 0.625, ((0, 16),)),
        "mlp_gain": jnp.clip(1.0 + 0.18 * jax.random.normal(keys[6], (D,), jnp.float32), 0.099609375, 1.8984375).astype(jnp.bfloat16),
        "w_gate_up": scatter_about(keys[7], (D, 2 * FF), D ** -0.5, 0.15625, ((0, 16),)),
        "w_down": scatter_about(keys[8], (FF, D), (FF // 2) ** -0.5, 0.09375, ((0, 16),)),
        "cotangent": scatter_about(keys[9], (SEQS, LEN, D), 1.0, 6.0, ((0, 16), (1, 8))),
    }


@jax.custom_vjp
def low(v):
    return lax.optimization_barrier(v.astype(jnp.bfloat16)).astype(jnp.float32)

@jax.custom_vjp
def low_back(v):
    return v

def low_keep(v):
    return (low(v), None)

def low_pass(kept, grad):
    return (grad,)

def back_keep(v):
    return (v, None)

def back_low(kept, grad):
    return (low(grad),)
low.defvjp(low_keep, low_pass)
low_back.defvjp(back_keep, back_low)
eps = 1e-06
rope_base = 1000000.0
masked_value = -1e+30

def highest(left, right):
    return jnp.dot(left, right, precision=lax.Precision.HIGHEST)

def normed(values, gain):
    return values * lax.rsqrt(lax.optimization_barrier(jnp.mean(values * values, axis=-1, keepdims=True)) + eps) * gain

def angles_of(positions, head_size):
    frequency = jnp.exp(jnp.arange(0, head_size, 2, dtype=jnp.float32) * (-math.log(rope_base) / head_size))
    return positions.astype(jnp.float32)[:, None] * frequency[None, :]

def rotate(field, angles):
    half_size = field.shape[-1] // 2
    cosine = jnp.cos(angles)[:, None, :]
    sine_part = jnp.sin(angles)[:, None, :]
    first_half = field[..., :half_size]
    second = field[..., half_size:]
    return jnp.concatenate([first_half * cosine - second * sine_part, second * cosine + first_half * sine_part], axis=-1)

def layer(resid, attn_gain, w_qkv, b_qkv, w_out, mlp_gain, w_gate_up, w_down, positions):
    kv_width = KVH * HD
    normed_in = low(normed(resid, attn_gain))
    projected = low_back(highest(normed_in, w_qkv) + b_qkv)
    angles = angles_of(positions, HD)
    queries = low(rotate(projected[:, :D].reshape(LEN, H, HD), angles))
    keys_rot = low(rotate(projected[:, D:D + kv_width].reshape(LEN, KVH, HD), angles))
    values_all = low(projected[:, D + kv_width:].reshape(LEN, KVH, HD))
    keys_wide = jnp.repeat(keys_rot, H // KVH, axis=1)
    values_wide = jnp.repeat(values_all, H // KVH, axis=1)
    score_scale = 1.0 / math.sqrt(HD)

    def attend_pair(operands):
        query_block, query_pos = operands
        scores = low_back(jnp.einsum('qhd,khd->hqk', query_block, keys_wide, precision=lax.Precision.HIGHEST) * score_scale)
        scores = jnp.where(query_pos[None, :, None] >= positions[None, None, :], scores, masked_value)
        row_max = lax.optimization_barrier(jnp.max(scores, axis=-1, keepdims=True))
        exponent = jnp.exp(scores - row_max)
        probability = low(exponent / lax.optimization_barrier(jnp.sum(exponent, axis=-1, keepdims=True)))
        return jnp.einsum('hqk,khd->qhd', probability, values_wide, precision=lax.Precision.HIGHEST)
    block_count = LEN // QB
    attended = lax.map(jax.checkpoint(attend_pair), (queries.reshape(block_count, QB, H, HD), positions.reshape(block_count, QB)))
    attended = low(low_back(attended.reshape(LEN, D)))
    middle = resid + low_back(highest(attended, w_out))
    normed_mid = low(normed(middle, mlp_gain))
    gate_up = low_back(highest(normed_mid, w_gate_up))
    hidden = low(jax.nn.silu(gate_up[:, :FF]) * gate_up[:, FF:])
    return middle + low_back(highest(hidden, w_down))

def reference(hidden_in, block_order, attn_gain, w_qkv, b_qkv, w_out, mlp_gain, w_gate_up, w_down, cotangent):
    params = tuple((param.astype(jnp.float32) for param in (attn_gain, w_qkv, b_qkv, w_out, mlp_gain, w_gate_up, w_down)))
    offsets = jnp.arange(BLOCK_ROWS, dtype=jnp.int32)
    positions = (block_order[:, :, None] * BLOCK_ROWS + offsets[None, None, :]).reshape(SEQS, LEN)

    def one_sequence(totals, operands):
        resid, grad_out, seq_pos = operands

        def forward(resid_in, *weights):
            return layer(resid_in, *weights, seq_pos)
        output, pull_back = jax.vjp(forward, resid.astype(jnp.float32), *params)
        gradients = pull_back(grad_out.astype(jnp.float32))
        totals = tuple((summed + gradient for summed, gradient in zip(totals, gradients[1:])))
        return (totals, (output, gradients[0]))
    start_totals = tuple((jnp.zeros_like(param) for param in params))
    totals, outputs = lax.scan(one_sequence, start_totals, (hidden_in, cotangent, positions))
    return (outputs[0], outputs[1], totals[0], totals[1], totals[2], totals[3], totals[4], totals[5], totals[6])
```

```python
import math

import jax
import jax.numpy as jnp
from jax import lax
from jax.sharding import Mesh, PartitionSpec as P

D = 1536
H = 12
KVH = 2
HD = 128
FF = 8960
SLICE = FF // 8
WIDE = 1152

CTX = ("y", "xl")
FSDP = ("xh", "z", "core")

eps = 1e-06
rope_base = 1000000.0
masked_value = -1e30
bf16 = jnp.bfloat16
f32 = jnp.float32


def moved(block, ring, pair, step, flip):
    size = lax.axis_size(ring)
    if step == 0:
        return lax.ppermute(block, pair, [(0, 1), (1, 0)])
    return lax.ppermute(block, ring, [(i, (i + step) % size) for i in range(size)])


def gather_eight(block, ring, pair):
    rows = block.shape[0]
    half = rows // 2
    across = moved(block, ring, pair, 0, 1)
    before = moved(block, ring, pair, 1, 0)
    after = moved(block, ring, pair, -1, 0)
    far_first = moved(before[:half], ring, pair, 1, 0)
    far_second = moved(after[half:], ring, pair, -1, 0)
    across_before = moved(across, ring, pair, 1, 0)
    across_after = moved(across, ring, pair, -1, 0)
    across_far_first = moved(far_first, ring, pair, 0, 1)
    across_far_second = moved(far_second, ring, pair, 0, 1)
    return [
        (0, 0, 0, block),
        (0, 1, 0, across),
        (-1, 0, 0, before),
        (1, 0, 0, after),
        (-1, 1, 0, across_before),
        (1, 1, 0, across_after),
        (2, 0, 0, far_first),
        (2, 0, half, far_second),
        (2, 1, 0, across_far_first),
        (2, 1, half, across_far_second),
    ]


def place(ring, pair, ring_major, step, flip):
    size = lax.axis_size(ring)
    r = (lax.axis_index(ring) + step) % size
    q = lax.axis_index(pair)
    q = 1 - q if flip else q
    return r * 2 + q if ring_major else q * size + r


def gathered(block, ring, pair, ring_major):
    rows = block.shape[0]
    whole = jnp.zeros((8 * rows,) + block.shape[1:], block.dtype)
    for step, flip, first, piece in gather_eight(block, ring, pair):
        at = place(ring, pair, ring_major, step, flip) * rows + first
        whole = lax.dynamic_update_slice_in_dim(whole, piece, at, 0)
    return whole


def scattered(parts, ring, pair, ring_major):
    half = parts.shape[1] // 2

    def part(step, flip):
        at = place(ring, pair, ring_major, step, flip)
        return lax.dynamic_index_in_dim(parts, at, 0, keepdims=False)

    def add(a, b):
        return (a.astype(f32) + b.astype(f32)).astype(bf16)

    far_across = moved(part(2, 1), ring, pair, 0, 1)
    from_after = moved(part(-1, 1), ring, pair, -1, 0)
    from_before = moved(part(1, 1), ring, pair, 1, 0)
    far = part(2, 0)
    far_first = moved(add(far[:half], far_across[:half]), ring, pair, -1, 0)
    far_second = moved(add(far[half:], far_across[half:]), ring, pair, 1, 0)
    across = part(0, 1)
    across = (across.astype(f32) + from_after.astype(f32) + from_before.astype(f32)).astype(bf16)
    got_across = moved(across, ring, pair, 0, 1)
    back = part(-1, 0)
    back = jnp.concatenate([add(back[:half], far_first), back[half:]], axis=0)
    ahead = part(1, 0)
    ahead = jnp.concatenate([ahead[:half], add(ahead[half:], far_second)], axis=0)
    got_back = moved(back, ring, pair, -1, 0)
    got_ahead = moved(ahead, ring, pair, 1, 0)
    return (
        part(0, 0).astype(f32)
        + got_across.astype(f32)
        + got_back.astype(f32)
        + got_ahead.astype(f32)
    )


def swap_core(block):
    return lax.ppermute(block, "core", [(0, 1), (1, 0)])


def gathered_fsdp(block):
    rows, columns = block.shape
    own = gathered(block, "z", "xh", False)
    other = swap_core(own)
    own = own.reshape(8, rows, columns)
    other = other.reshape(8, rows, columns)
    first = lax.axis_index("core") == 0
    return jnp.stack(
        [jnp.where(first, own, other), jnp.where(first, other, own)], axis=1
    ).reshape(16 * rows, columns)


def scattered_fsdp(parts):
    _, rows, columns = parts.shape
    core = lax.axis_index("core")
    pairs = parts.reshape(8, 2, rows, columns)
    given = lax.dynamic_index_in_dim(pairs, 1 - core, 1, keepdims=False)
    kept = lax.dynamic_index_in_dim(pairs, core, 1, keepdims=False)
    got = swap_core(given)
    both = (kept.astype(f32) + got.astype(f32)).astype(bf16)
    return scattered(both, "z", "xh", False)


def scattered_ctx(part):
    pieces = lax.all_to_all(part.reshape(8, 128, D), CTX, 0, 0, tiled=True)
    return jnp.sum(pieces.astype(f32), axis=0)


def rotate(field, cosine, sine):
    half = field.shape[-1] // 2
    a, b = field[..., :half], field[..., half:]
    return jnp.concatenate([a * cosine - b * sine, b * cosine + a * sine], axis=-1)


def unrotate(field, cosine, sine):
    half = field.shape[-1] // 2
    a, b = field[..., :half], field[..., half:]
    return jnp.concatenate([a * cosine + b * sine, b * cosine - a * sine], axis=-1)


def mm(a, b):
    return jnp.dot(a, b, preferred_element_type=f32)


def mm_nt(a, b):
    return jnp.einsum("ik,jk->ij", a, b, preferred_element_type=f32)


def mm_tn(a, b):
    return jnp.einsum("ki,kj->ij", a, b, preferred_element_type=f32)


def own_half(rows, half):
    n = rows.shape[-1]
    return lax.dynamic_index_in_dim(
        rows.reshape(8, 2, 64, n), half, 1, keepdims=False
    ).reshape(512, n)


def shards(
    hidden_in, block_order, attn_gain, w_qkv, b_qkv, w_out, mlp_gain, w_gate_up, w_down, cotangent
):
    yi, qi = lax.axis_index("y"), lax.axis_index("xl")
    ci = 2 * yi + qi
    fi = lax.axis_index(FSDP)
    group = yi // 2
    x_own = hidden_in[0]
    cot_own = cotangent[0]

    starts = (
        HD * (3 * yi + 2 * qi),
        HD * (3 * yi + 1),
        D + HD * group,
        D + HD * (KVH + group),
    )

    def my_columns(array):
        return jnp.concatenate(
            [lax.dynamic_slice_in_dim(array, s, HD, array.ndim - 1) for s in starts], axis=-1
        )

    bias_low = jnp.concatenate([b_qkv[:96, None], jnp.pad(b_qkv[96:], (0, 64))[:, None]], axis=1)
    extra = jnp.concatenate([attn_gain[:, None], mlp_gain[:, None], bias_low], axis=1)
    extra = jnp.pad(extra, ((0, 0), (0, 124)))
    packed = jnp.concatenate([my_columns(w_qkv), w_out, extra], axis=1)

    x_all = gathered(x_own, "y", "xl", True)
    packed_all = gathered_fsdp(packed)

    pad = jnp.zeros((96, WIDE - SLICE), bf16)
    gu_own = jnp.concatenate(
        [
            lax.dynamic_slice_in_dim(w_gate_up, SLICE * ci, SLICE, 1),
            pad,
            lax.dynamic_slice_in_dim(w_gate_up, FF + SLICE * ci, SLICE, 1),
            pad,
        ],
        axis=1,
    )
    w_gu = lax.all_gather(gu_own, FSDP, axis=0, tiled=True)
    whole = CTX + FSDP
    route = [
        ((s % 8) * 16 + 2 * c + s // 8, c * 16 + s) for c in range(8) for s in range(16)
    ]
    wd_own = lax.ppermute(lax.dynamic_slice_in_dim(w_down, 70 * ci, 70, 0), whole, route)
    w_dn = lax.all_gather(wd_own, FSDP, axis=0, tiled=True)
    w_qkv_all = lax.all_gather(w_qkv, FSDP, axis=0, tiled=True)
    cot_all = gathered(cot_own, "y", "xl", True)

    w_mine = packed_all[:, :512]
    w_out_all = packed_all[:, 512 : 512 + D]
    extras = packed_all[:, 512 + D :].astype(f32)
    gain_one = extras[:, 0]
    gain_two = extras[:, 1]
    bias_rows = extras.reshape(16, 96, 128)
    bias_all = jnp.concatenate([bias_rows[:, :, 2], bias_rows[:, :32, 3]], axis=1).reshape(2048)
    bias_mine = my_columns(bias_all)

    order = block_order[0]
    positions = (order[:, None] * 64 + jnp.arange(64, dtype=jnp.int32)[None, :]).reshape(1024)
    frequency = jnp.exp(jnp.arange(0, HD, 2, dtype=f32) * (-math.log(rope_base) / HD))
    angles = positions.astype(f32)[:, None] * frequency[None, :]
    cosine, sine = jnp.cos(angles), jnp.sin(angles)
    score_scale = 1.0 / math.sqrt(HD)

    resid_all = x_all.astype(f32)
    inv_all = lax.rsqrt(jnp.mean(resid_all * resid_all, axis=-1, keepdims=True) + eps)
    normed_all = (resid_all * inv_all * gain_one).astype(bf16)
    projected = mm(normed_all, w_mine) + bias_mine
    q_a = rotate(projected[:, :HD], cosine, sine).astype(bf16)
    q_b = rotate(projected[:, HD : 2 * HD], cosine, sine).astype(bf16)
    keys = rotate(projected[:, 2 * HD : 3 * HD], cosine, sine).astype(bf16)
    values = projected[:, 3 * HD :].astype(bf16)
    queries = jnp.concatenate([q_a, own_half(q_b, qi)], axis=0)
    q_pos = jnp.concatenate(
        [positions, lax.dynamic_index_in_dim(positions.reshape(8, 2, 64), qi, 1, False).reshape(512)]
    )
    scores = mm_nt(queries, keys) * score_scale
    scores = jnp.where(q_pos[:, None] >= positions[None, :], scores, masked_value)
    row_max = jnp.max(scores, axis=-1, keepdims=True)
    exponent = jnp.exp(scores - row_max)
    probs = exponent / jnp.sum(exponent, axis=-1, keepdims=True)
    probability = probs.astype(bf16)
    att_mine = mm(probability, values).astype(bf16)

    def to_rows(head_a, head_b):
        return jnp.concatenate([head_a.reshape(8, 128, HD), head_b.reshape(8, 64, HD)], axis=1)

    def rows_of(got):
        got = got.reshape(4, 2, 192, HD)
        first, last = got[:, 0, :128], got[:, 1, :128]
        mid = got[:, :, 128:].reshape(4, 128, HD)
        return jnp.stack([first, mid, last], axis=1).transpose(2, 0, 1, 3).reshape(128, D)

    got = lax.all_to_all(to_rows(att_mine[:1024], att_mine[1024:]), CTX, 0, 0, tiled=True)
    attended = rows_of(got)

    resid = x_own.astype(f32)
    inv_first = lax.rsqrt(jnp.mean(resid * resid, axis=-1, keepdims=True) + eps)
    middle = resid + mm(attended, w_out_all)
    inv_second = lax.rsqrt(jnp.mean(middle * middle, axis=-1, keepdims=True) + eps)
    normed_mid = (middle * inv_second * gain_two).astype(bf16)
    nm_all = gathered(normed_mid, "y", "xl", True)

    gate_up = mm(nm_all, w_gu)
    gate, up = gate_up[:, :SLICE], gate_up[:, WIDE : WIDE + SLICE]
    sigmoid_gate = jax.nn.sigmoid(gate)
    silu_gate = gate * sigmoid_gate
    hidden = (silu_gate * up).astype(bf16)
    grad_act = mm_nt(cot_all, w_dn)
    grad_gate = grad_act * up * sigmoid_gate * (1.0 + gate * (1.0 - sigmoid_gate))
    grad_up = grad_act * silu_gate
    zero = jnp.zeros((1024, WIDE - SLICE), bf16)
    grad_gu = jnp.concatenate([grad_gate.astype(bf16), zero, grad_up.astype(bf16), zero], axis=1)
    hn_part = mm_nt(grad_gu, w_gu).astype(bf16)
    out_part = mm(hidden, w_dn).astype(bf16)

    grad_hn = scattered_ctx(hn_part)
    hidden_sum = lax.psum_scatter(out_part, CTX, scatter_dimension=0, tiled=True)
    hidden_out = middle + hidden_sum.astype(f32)

    gw_dn = mm_tn(hidden, cot_all).astype(bf16)
    gw_gu = mm_tn(nm_all, grad_gu).astype(bf16)

    grad_out = cot_own.astype(f32)
    scaled = grad_hn * gain_two
    grad_middle = (
        grad_out
        + inv_second * scaled
        - middle * (inv_second**3) * jnp.mean(middle * scaled, axis=-1, keepdims=True)
    )
    grad_attn = grad_middle.astype(bf16)
    grad_attended = mm_nt(grad_attn, w_out_all).astype(bf16)
    by_head = grad_attended.reshape(128, 4, 3, HD)
    send_a = by_head[:, :, ::2].transpose(1, 2, 0, 3)
    send_b = by_head.reshape(2, 64, 4, 3, HD)[:, :, :, 1].transpose(2, 0, 1, 3)
    send = jnp.concatenate([send_a, send_b], axis=2).reshape(8, 192, HD)
    got = lax.all_to_all(send, CTX, 0, 0, tiled=True)
    grad_heads = jnp.concatenate(
        [got[:, :128].reshape(1024, HD), got[:, 128:].reshape(512, HD)], axis=0
    )

    grad_prob = mm_nt(grad_heads, values)
    grad_scores = (
        probs * (grad_prob - jnp.sum(probs * grad_prob, axis=-1, keepdims=True))
    ).astype(bf16)
    grad_q = mm(grad_scores, keys) * score_scale
    grad_k = mm_tn(grad_scores, queries) * score_scale
    grad_v = mm_tn(probability, grad_heads)
    half_cos = lax.dynamic_index_in_dim(cosine.reshape(8, 2, 64, 64), qi, 1, False).reshape(512, 64)
    half_sin = lax.dynamic_index_in_dim(sine.reshape(8, 2, 64, 64), qi, 1, False).reshape(512, 64)
    gp_a = unrotate(grad_q[:1024], cosine, sine).astype(bf16)
    gp_b = unrotate(grad_q[1024:], half_cos, half_sin).astype(bf16)
    gp_k = unrotate(grad_k, cosine, sine).astype(bf16)
    gp_v = grad_v.astype(bf16)

    send = jnp.concatenate(
        [
            to_rows(gp_a, gp_b),
            gp_k.reshape(8, 128, HD),
            gp_v.reshape(8, 128, HD),
        ],
        axis=1,
    )
    got = lax.all_to_all(send, CTX, 0, 0, tiled=True)
    gq_rows = rows_of(got[:, :192])
    gkv = jnp.sum(got[:, 192:].astype(f32).reshape(2, 4, 2, 128, HD), axis=1).astype(bf16)
    gkv_rows = gkv.transpose(2, 1, 0, 3).reshape(128, 4 * HD)
    gp_rows = jnp.concatenate([gq_rows, gkv_rows], axis=1)
    grad_xn = mm_nt(gp_rows, w_qkv_all)
    scaled = grad_xn * gain_one
    grad_in = (
        grad_middle
        + inv_first * scaled
        - resid * (inv_first**3) * jnp.mean(resid * scaled, axis=-1, keepdims=True)
    )

    here = (jnp.arange(2) == qi)[None, :, None, None]
    gp_b_all = jnp.where(here, gp_b.reshape(8, 1, 64, HD), jnp.zeros((), bf16)).reshape(1024, HD)
    gp_mine = jnp.concatenate([gp_a, gp_b_all, gp_k, gp_v], axis=1)
    gw_mine = mm_tn(normed_all, gp_mine).astype(bf16)
    gb_mine = jnp.sum(gp_mine.astype(f32), axis=0).astype(bf16)
    qkv_parts = jnp.concatenate(
        [gw_mine.reshape(16, 96, 512), jnp.broadcast_to(gb_mine, (16, 16, 512))], axis=1
    )
    qkv_sum = scattered_fsdp(qkv_parts).astype(bf16)

    gw_out = mm_tn(attended, grad_attn).astype(bf16)
    out_sum = scattered_fsdp(gw_out.reshape(16, 96, D)).astype(bf16)
    out_pieces = lax.all_to_all(
        out_sum.reshape(96, 8, 192).transpose(1, 0, 2), CTX, 0, 0, tiled=True
    )
    out_mine = jnp.sum(out_pieces.astype(f32), axis=0).astype(bf16)

    gu_sum = scattered_fsdp(gw_gu.reshape(16, 96, 2 * WIDE)).astype(bf16)
    dn_sum = lax.psum_scatter(gw_dn, FSDP, scatter_dimension=0, tiled=True)
    dn_mine = lax.ppermute(dn_sum, whole, [(b, a) for a, b in route])
    grad_w_down = lax.all_gather(dn_mine, CTX, axis=0, tiled=True).astype(f32)

    gu_all = gathered(gu_sum, "y", "xl", True).reshape(8, 96, 2 * WIDE)
    grad_w_gate_up = jnp.concatenate(
        [gu_all[c, :, :SLICE] for c in range(8)]
        + [gu_all[c, :, WIDE : WIDE + SLICE] for c in range(8)],
        axis=1,
    ).astype(f32)
    grad_mlp_gain = jnp.sum(grad_w_gate_up * w_gate_up.astype(f32), axis=1) / mlp_gain.astype(f32)

    tail = jnp.concatenate([qkv_sum, jnp.pad(out_mine, ((0, 16), (0, 64)))], axis=1)
    tail_all = gathered(tail, "y", "xl", True).reshape(8, 112, 768)
    grad_w_out = tail_all[:, :96, 512:704].transpose(1, 0, 2).reshape(96, D).astype(f32)
    qkv_all = tail_all[:, :, :512].astype(f32).reshape(4, 2, 112, 4, HD)
    head_first = qkv_all[:, 0, :, 0]
    head_last = qkv_all[:, 1, :, 0]
    head_mid = qkv_all[:, 0, :, 1] + qkv_all[:, 1, :, 1]
    gq = jnp.stack([head_first, head_mid, head_last], axis=1).reshape(12, 112, HD)
    gk = jnp.sum(qkv_all[:, :, :, 2].reshape(2, 4, 112, HD), axis=1)
    gv = jnp.sum(qkv_all[:, :, :, 3].reshape(2, 4, 112, HD), axis=1)
    heads = jnp.concatenate([gq, gk, gv], axis=0)
    grad_w_qkv = heads[:, :96].transpose(1, 0, 2).reshape(96, 2048)
    grad_b_qkv = lax.dynamic_index_in_dim(heads[:, 96], fi, 0, keepdims=False)
    grad_attn_gain = jnp.sum(grad_w_qkv * w_qkv.astype(f32), axis=1) / attn_gain.astype(f32)

    return (
        hidden_out[None],
        grad_in[None],
        grad_attn_gain,
        grad_w_qkv,
        grad_b_qkv,
        grad_w_out,
        grad_mlp_gain,
        grad_w_gate_up,
        grad_w_down,
    )


def solution(mesh):
    fine = Mesh(mesh.devices.reshape(4, 2, 2, 4, 2), CTX + FSDP)
    rows = P(FSDP, CTX, None)
    vector = P(FSDP)
    matrix = P(FSDP, None)
    return jax.shard_map(
        shards,
        mesh=fine,
        in_specs=(rows, matrix, vector, matrix, vector, matrix, vector, matrix, matrix, rows),
        out_specs=(rows, rows, vector, matrix, vector, matrix, vector, matrix, matrix),
        check_vma=False,
    )
```

```python
import math

import jax
import jax.numpy as jnp
from jax import lax
from jax.experimental import pallas as pl
from jax.experimental.pallas import tpu as pltpu
from jax.sharding import Mesh, PartitionSpec as P

D = 1536
H = 12
KVH = 2
HD = 128
FF = 8960
PART = FF // 128
WIDE = 1152
MINE = 896

CTX = ("y", "xl")
FSDP = ("xh", "z", "core")

eps = 1e-06
rope_base = 1000000.0
masked_value = -1e30
bf16 = jnp.bfloat16
f32 = jnp.float32


def moved(block, ring, pair, step, flip):
    size = lax.axis_size(ring)
    if step == 0:
        return lax.ppermute(block, pair, [(0, 1), (1, 0)])
    return lax.ppermute(block, ring, [(i, (i + step) % size) for i in range(size)])


def halfway(rows):
    return rows // 32 * 16


def gather_stages(block, ring, pair):
    half = halfway(block.shape[0])
    across, before, after_ = yield (
        moved(block, ring, pair, 0, 1),
        moved(block, ring, pair, 1, 0),
        moved(block, ring, pair, -1, 0),
    )
    far_first, far_second, across_before, across_after = yield (
        moved(before[:half], ring, pair, 1, 0),
        moved(after_[half:], ring, pair, -1, 0),
        moved(across, ring, pair, 1, 0),
        moved(across, ring, pair, -1, 0),
    )
    across_far_first, across_far_second = yield (
        moved(far_first, ring, pair, 0, 1),
        moved(far_second, ring, pair, 0, 1),
    )
    yield [
        (0, 0, 0, block),
        (0, 1, 0, across),
        (-1, 0, 0, before),
        (1, 0, 0, after_),
        (-1, 1, 0, across_before),
        (1, 1, 0, across_after),
        (2, 0, 0, far_first),
        (2, 0, half, far_second),
        (2, 1, 0, across_far_first),
        (2, 1, half, across_far_second),
    ]


def in_step(*gathers):
    states = [next(g) for g in gathers]
    for _ in range(3):
        if len(gathers) > 1:
            states = lax.optimization_barrier(states)
        states = [g.send(state) for g, state in zip(gathers, states)]
    return states


def gather_eight(block, ring, pair):
    return in_step(gather_stages(block, ring, pair))[0]


def place(ring, pair, ring_major, step, flip):
    size = lax.axis_size(ring)
    r = (lax.axis_index(ring) + step) % size
    q = lax.axis_index(pair)
    q = 1 - q if flip else q
    return r * 2 + q if ring_major else q * size + r


def place_kernel(firsts, at_ref, *refs):
    pieces, out = refs[:-1], refs[-1]
    for i, (first, piece) in enumerate(zip(firsts, pieces)):
        out[at_ref[i], first : first + piece.shape[0]] = piece[...]


def placed(got, ring, pair, ring_major):
    pieces, firsts = [g[3] for g in got], [g[2] for g in got]
    places = [place(ring, pair, ring_major, step, flip) for step, flip, _, _ in got]
    rows, columns = pieces[0].shape
    size = 8 * rows * columns * pieces[0].dtype.itemsize
    return pl.pallas_call(
        lambda *refs: place_kernel(firsts, *refs),
        grid_spec=pltpu.PrefetchScalarGridSpec(
            num_scalar_prefetch=1,
            grid=(1,),
            in_specs=[pl.BlockSpec(p.shape, lambda i, at: (0, 0)) for p in pieces],
            out_specs=pl.BlockSpec((8, rows, columns), lambda i, at: (0, 0, 0)),
        ),
        out_shape=jax.ShapeDtypeStruct((8, rows, columns), pieces[0].dtype),
        compiler_params=pltpu.CompilerParams(vmem_limit_bytes=32 * 1024 * 1024),
        cost_estimate=pl.CostEstimate(flops=0, bytes_accessed=2 * size, transcendentals=0),
    )(jnp.stack(places).astype(jnp.int32), *pieces)


def gathered(block, ring, pair, ring_major):
    return placed(gather_eight(block, ring, pair), ring, pair, ring_major)


def weave_kernel(widths, at_ref, own, other, *outs):
    core = at_ref[0]
    at = 0
    for width, out in zip(widths, outs):
        out[0, core] = own[0, :, at : at + width]
        out[0, 1 - core] = other[0, :, at : at + width]
        at += width


def woven(own, *widths):
    _, _, rows, columns = own.shape
    own = own.reshape(8, rows, columns)
    other = swap_core(own)
    block = pl.BlockSpec((1, rows, columns), lambda i, at: (i, 0, 0))

    def place_of(i, at):
        side = jnp.where(i % 2 == 0, at[1], 1 - at[1])
        return side * 4 + i // 2, 0, 0, 0

    at = jnp.stack([lax.axis_index("core"), lax.axis_index("xh")]).astype(jnp.int32)
    outs = call(
        lambda *refs: weave_kernel(widths, *refs),
        [shaped((8, 2, rows, width), own.dtype) for width in widths],
        (8,),
        [(own, block), (other, block)],
        [pl.BlockSpec((1, 2, rows, width), place_of) for width in widths],
        scalars=(at,),
        bytes_accessed=32 * rows * columns * own.dtype.itemsize,
    )
    return [out.reshape(16 * rows, -1) for out in outs]


def pick_kernel(at_ref, weights, out):
    for c in range(8):

        @pl.when(at_ref[0] == c)
        def _():
            for part in range(2):
                for s in range(16):
                    start, to = part * FF + 560 * s + PART * c, part * WIDE + 72 * s
                    out[:, to : to + PART] = weights[:, start : start + PART]
                    out[:, to + PART : to + 72] = jnp.zeros((96, 2), bf16)


def picked(slice_index, weights):
    return call(
        pick_kernel,
        shaped((96, 2 * WIDE), bf16),
        (1,),
        [(weights, fixed(96, 2 * FF))],
        fixed(96, 2 * WIDE),
        scalars=(slice_index.astype(jnp.int32)[None],),
        bytes_accessed=4 * 1024 * 1024,
    )


def folded(rows):
    rest = rows[:, WIDE:]
    rest = jnp.concatenate([rest[24 * k : 24 * (k + 1)] for k in range(3)], axis=1)
    return jnp.concatenate([rows[:, :WIDE], rest], axis=0)


def unfolded(rows):
    rest = jnp.concatenate([rows[72:, 384 * k : 384 * (k + 1)] for k in range(3)], axis=0)
    return jnp.concatenate([rows[:72], rest], axis=1)


def unfold_kernel(weights, out):
    out[0] = unfolded(weights[...].astype(f32)).astype(bf16)


def down_weights(w_ffn):
    return call(
        unfold_kernel,
        shaped((16, 72, D), bf16),
        (16,),
        [(w_ffn, pl.BlockSpec((96, WIDE), lambda s: (s, 2)))],
        pl.BlockSpec((1, 72, D), lambda s: (s, 0, 0)),
        bytes_accessed=8 * 1024 * 1024,
    ).reshape(WIDE, D)


def last_kernel(at_ref, *refs):
    pieces, weights, weights_qkv = refs[:10], refs[10], refs[11]
    out, gain, out_qkv, gain_qkv, out_out, bias, blocks = refs[12:]
    step = pl.program_id(0)
    for i in range(6):
        blocks[at_ref[i]] = pieces[i][...]
    for i in (6, 8):
        blocks[at_ref[i]] = jnp.where(step < 3, pieces[i][...], pieces[i + 1][...])
    total = jnp.zeros((16, 1), f32)
    for part in range(2):
        for s in range(16):
            start = part * WIDE + 72 * s
            row = jnp.concatenate(
                [blocks[c, :, start : start + PART].astype(f32) for c in range(8)], axis=1
            )
            out[:, part * FF + 560 * s : part * FF + 560 * (s + 1)] = row
    for at in range(0, 2 * FF, 1792):
        lanes = slice(at, at + 1792)
        total = total + jnp.sum(
            out[:, lanes] * weights[:, lanes].astype(f32), axis=1, keepdims=True
        )
    gain[...] = jnp.broadcast_to(total, (16, HD))

    def whole(c, at, rows=slice(0, 16)):
        start = 3 * WIDE + at * HD
        return blocks[c, rows, start : start + HD].astype(f32)

    def heads(term):
        for y in range(4):
            yield 3 * y, term(2 * y, 0)
            yield 3 * y + 1, term(2 * y, 1) + term(2 * y + 1, 1)
            yield 3 * y + 2, term(2 * y + 1, 0)
        for kind in range(2):
            for group in range(2):
                yield 12 + 2 * kind + group, sum(term(4 * group + i, 2 + kind) for i in range(4))

    total = jnp.zeros((16, 1), f32)
    for h, value in heads(whole):
        lanes = slice(h * HD, (h + 1) * HD)
        out_qkv[:, lanes] = value
        total = total + jnp.sum(
            value * weights_qkv[:, lanes].astype(f32), axis=1, keepdims=True
        )
    gain_qkv[...] = jnp.broadcast_to(total, (16, HD))
    for y in range(4):
        at = 3 * y * HD
        out_out[:, at : at + HD] = whole(2 * y, 4)
        out_out[:, at + HD : at + 2 * HD] = whole(2 * y, 5) + whole(2 * y + 1, 5)
        out_out[:, at + 2 * HD : at + 3 * HD] = whole(2 * y + 1, 4)

    @pl.when(step == 0)
    def _():
        for h, value in heads(lambda c, kind: whole(c, 6)[kind : kind + 1]):
            bias[h : h + 1] = value


def last_down_kernel(at_ref, *refs):
    pieces, out, blocks = refs[:10], refs[10], refs[11]
    for i in range(6):
        blocks[at_ref[i]] = pieces[i][...].astype(f32)
    for i in (6, 8):
        blocks[at_ref[i], :48] = pieces[i][...].astype(f32)
        blocks[at_ref[i], 48:] = pieces[i + 1][...].astype(f32)
    for c in range(8):
        out[PART * c : PART * (c + 1)] = unfolded(blocks[c])[:PART]


def weight_gradients(got, weights, weights_qkv):
    pieces = [g[3] for g in got]
    places = [place("y", "xl", True, step, flip) for step, flip, _, _ in got]
    places = jnp.stack(places).astype(jnp.int32)
    width = 3 * WIDE + MINE

    def rows(i, at):
        return i, 0

    maps = [rows] * 6 + [
        lambda i, at: (jnp.minimum(i, 2), 0),
        lambda i, at: (jnp.maximum(i - 3, 0), 0),
    ] * 2
    outs = call(
        last_kernel,
        [
            shaped((96, 2 * FF), f32),
            shaped((96, HD), f32),
            shaped((96, 2048), f32),
            shaped((96, HD), f32),
            shaped((96, D), f32),
            shaped((16, HD), f32),
        ],
        (6,),
        [(p, pl.BlockSpec((16, width), m)) for p, m in zip(pieces, maps)]
        + [
            (weights, pl.BlockSpec((16, 2 * FF), rows)),
            (weights_qkv, pl.BlockSpec((16, 2048), rows)),
        ],
        [
            pl.BlockSpec((16, 2 * FF), rows),
            pl.BlockSpec((16, HD), rows),
            pl.BlockSpec((16, 2048), rows),
            pl.BlockSpec((16, HD), rows),
            pl.BlockSpec((16, D), rows),
            pl.BlockSpec((16, HD), lambda i, at: (0, 0)),
        ],
        scalars=(places,),
        scratch=[pltpu.VMEM((8, 16, width), bf16)],
        bytes_accessed=96 * 2 * FF * 8,
    )
    w_gate_up, gain, w_qkv, gain_qkv, w_out, bias = outs
    w_down = call(
        last_down_kernel,
        shaped((560, D), f32),
        (1,),
        [(p, pl.BlockSpec((p.shape[0], WIDE), lambda i, at: (0, 2))) for p in pieces],
        fixed(560, D),
        scalars=(places,),
        scratch=[pltpu.VMEM((8, 96, WIDE), f32)],
        bytes_accessed=6 * 1024 * 1024,
    )
    return w_gate_up, w_down, w_qkv, w_out, bias, gain[:, 0], gain_qkv[:, 0]


def turned(field, cos_ref, sin_ref):
    return field * cos_ref + pltpu.roll(field, HD // 2, 1) * sin_ref


def nt(a, b):
    return lax.dot_general(a, b, (((1,), (1,)), ((), ())), preferred_element_type=f32)


def tn(a, b):
    return lax.dot_general(a, b, (((0,), (0,)), ((), ())), preferred_element_type=f32)


SCALE = 1.0 / math.sqrt(HD)


def attend_kernel(half_ref, proj, cos, sin, pos_col, pos_row, att, queries, lse, keys, values):
    c, half = pl.program_id(0), half_ref[0]

    @pl.when(c == 0)
    def _():
        keys[...] = turned(proj[:, 2 * HD : 3 * HD], cos[...], sin[...]).astype(bf16)
        values[...] = proj[:, 3 * HD :].astype(bf16)

    rows = pl.ds(pl.multiple_of(c * 128, 128), 128)
    part = pl.ds(pl.multiple_of(c * 128 + half * 64, 64), 64)
    query = jnp.concatenate(
        [
            turned(proj[rows, :HD], cos[rows], sin[rows]),
            turned(proj[part, HD : 2 * HD], cos[part], sin[part]),
        ],
        axis=0,
    ).astype(bf16)
    queries[...] = query
    scores = nt(query, keys[...]) * SCALE
    seen = jnp.concatenate([pos_col[rows], pos_col[part]], axis=0) >= pos_row[...]
    scores = jnp.where(seen, scores, masked_value)
    row_max = jnp.max(scores, axis=1, keepdims=True)
    exponent = jnp.exp(scores - row_max)
    total = jnp.sum(exponent, axis=1, keepdims=True)
    probability = (exponent / total).astype(bf16)
    att[...] = jnp.dot(probability, values[...], preferred_element_type=f32).astype(bf16)
    lse[...] = jnp.broadcast_to(row_max + jnp.log(total), (192, HD))


def attend(half, projected, cos, sin, pos_col, pos_row):
    block = pl.BlockSpec((192, HD), lambda c, half: (c, 0))
    return call(
        attend_kernel,
        [
            shaped((1536, HD), bf16),
            shaped((1536, HD), bf16),
            shaped((1536, HD), f32),
            shaped((1024, HD), bf16),
            shaped((1024, HD), bf16),
        ],
        (8,),
        [
            (projected, fixed(1024, 4 * HD)),
            (cos, fixed(1024, HD)),
            (sin, fixed(1024, HD)),
            (pos_col, fixed(1024, 1)),
            (pos_row, fixed(1, 1024)),
        ],
        [block, block, block, fixed(1024, HD), fixed(1024, HD)],
        scalars=(half,),
        flops=4 * 1536 * 1024 * HD,
        bytes_accessed=6 * 1024 * 1024,
        exps=1536 * 1024,
    )


def attend_back_kernel(
    half_ref, got, queries, lse, keys, values, cos, sin, pos_col, pos_row, grads, columns, gk, gv
):
    c, half = pl.program_id(0), half_ref[0]

    @pl.when(c == 0)
    def _():
        gk[...] = jnp.zeros_like(gk)
        gv[...] = jnp.zeros_like(gv)

    rows = pl.ds(pl.multiple_of(c * 128, 128), 128)
    part = pl.ds(pl.multiple_of(c * 128 + half * 64, 64), 64)
    rest = pl.ds(pl.multiple_of(c * 128 + (1 - half) * 64, 64), 64)
    out = got[0, :192]
    query = queries[...]
    scores = nt(query, keys[...]) * SCALE
    seen = jnp.concatenate([pos_col[rows], pos_col[part]], axis=0) >= pos_row[...]
    scores = jnp.where(seen, scores, masked_value)
    probs = jnp.exp(scores - lse[:, :1])
    grad_prob = nt(out, values[...])
    inner = jnp.sum(probs * grad_prob, axis=1, keepdims=True)
    grad_scores = (probs * (grad_prob - inner)).astype(bf16)
    grad_query = jnp.dot(grad_scores, keys[...], preferred_element_type=f32) * SCALE
    gk[...] += tn(grad_scores, query)
    gv[...] += tn(probs.astype(bf16), out)
    grads[rows, :HD] = turned(grad_query[:128], cos[rows], -sin[rows]).astype(bf16)
    grads[part, HD : 2 * HD] = turned(grad_query[128:], cos[part], -sin[part]).astype(bf16)
    grads[rest, HD : 2 * HD] = jnp.zeros((64, HD), bf16)
    columns[:, :HD] = got[0, 192:320]
    columns[pl.ds(pl.multiple_of(half * 64, 64), 64), HD:] = got[0, 320:]
    columns[pl.ds(pl.multiple_of((1 - half) * 64, 64), 64), HD:] = jnp.zeros((64, HD), bf16)

    @pl.when(c == 7)
    def _():
        grads[:, 2 * HD : 3 * HD] = turned(gk[...] * SCALE, cos[...], -sin[...]).astype(bf16)
        grads[:, 3 * HD :] = gv[...].astype(bf16)


def attend_back(half, got, queries, lse, keys, values, cos, sin, pos_col, pos_row):
    block = pl.BlockSpec((192, HD), lambda c, half: (c, 0))
    return call(
        attend_back_kernel,
        [shaped((1024, 4 * HD), bf16), shaped((1024, 2 * HD), bf16)],
        (8,),
        [
            (got, pl.BlockSpec((1, 384, HD), lambda c, half: (c, 0, 0))),
            (queries, block),
            (lse, block),
            (keys, fixed(1024, HD)),
            (values, fixed(1024, HD)),
            (cos, fixed(1024, HD)),
            (sin, fixed(1024, HD)),
            (pos_col, fixed(1024, 1)),
            (pos_row, fixed(1, 1024)),
        ],
        [fixed(1024, 4 * HD), pl.BlockSpec((128, 2 * HD), lambda c, half: (c, 0))],
        scalars=(half,),
        scratch=[pltpu.VMEM((1024, HD), f32), pltpu.VMEM((1024, HD), f32)],
        flops=10 * 1536 * 1024 * HD,
        bytes_accessed=6 * 1024 * 1024,
        exps=1536 * 1024,
    )


def middle_kernel(got, w_out, x, gain, attended, middle, normed, inverse):
    for y in range(4):
        for q in range(2):
            whole, split = HD * (3 * y + 2 * q), HD * (3 * y + 1)
            attended[:, whole : whole + HD] = got[2 * y + q, :128]
            attended[64 * q : 64 * (q + 1), split : split + HD] = got[2 * y + q, 128:]
    mid = x[...].astype(f32) + jnp.dot(attended[...], w_out[...], preferred_element_type=f32)
    inv = lax.rsqrt(jnp.mean(mid * mid, axis=1, keepdims=True) + eps)
    middle[...] = mid
    normed[...] = (mid * inv * gain[...]).astype(bf16)
    inverse[...] = jnp.broadcast_to(inv, (128, HD))


def to_middle(got, w_out, x, gain):
    return call(
        middle_kernel,
        [
            shaped((128, D), bf16),
            shaped((128, D), f32),
            shaped((128, D), bf16),
            shaped((128, HD), f32),
        ],
        (1,),
        [
            (got, fixed(8, 192, HD)),
            (w_out, fixed(D, D)),
            (x, fixed(128, D)),
            (gain, fixed(1, D)),
        ],
        [fixed(128, D), fixed(128, D), fixed(128, D), fixed(128, HD)],
        flops=2 * 128 * D * D,
        bytes_accessed=8 * 1024 * 1024,
    )


def middle_back_kernel(a, b, c, d, middle, inverse, gain, cot, w_out, grad_middle, send):
    grad_hn = a[...].astype(f32) + b[...].astype(f32) + c[...].astype(f32) + d[...].astype(f32)
    inv, mid = inverse[:, :1], middle[...]
    scaled = grad_hn * gain[...]
    inner = jnp.mean(mid * scaled, axis=1, keepdims=True)
    grad = cot[...].astype(f32) + inv * scaled - mid * (inv * inv * inv * inner)
    grad_middle[...] = grad
    grad_attn = grad.astype(bf16)
    heads = nt(grad_attn, w_out[...]).astype(bf16)
    for y in range(4):
        for q in range(2):
            whole, split = HD * (3 * y + 2 * q), HD * (3 * y + 1)
            half = slice(64 * q, 64 * (q + 1))
            send[2 * y + q, :128] = heads[:, whole : whole + HD]
            send[2 * y + q, 128:192] = heads[half, split : split + HD]
            send[2 * y + q, 192:320] = grad_attn[:, whole : whole + HD]
            send[2 * y + q, 320:] = grad_attn[half, split : split + HD]


def middle_back(parts, middle, inverse, gain, cot, w_out):
    row = fixed(128, D)
    return call(
        middle_back_kernel,
        [shaped((128, D), f32), shaped((8, 384, HD), bf16)],
        (1,),
        [(p, row) for p in parts]
        + [
            (middle, row),
            (inverse, fixed(128, HD)),
            (gain, fixed(1, D)),
            (cot, row),
            (w_out, fixed(D, D)),
        ],
        [row, fixed(8, 384, HD)],
        flops=2 * 128 * D * D,
        bytes_accessed=10 * 1024 * 1024,
    )


def down_product_kernel(*refs):
    hidden, cot, out, total = refs[:2], refs[2:4], refs[4], refs[5]
    step = pl.program_id(0)
    product = tn(hidden[0][...], cot[0][...]) + tn(hidden[1][...], cot[1][...])

    for k in range(3):

        @pl.when(step == k)
        def _():
            for s in range(16):
                total[s, :72, 384 * k : 384 * (k + 1)] = product[72 * s : 72 * (s + 1)]

    @pl.when(step == 3)
    def _():
        for s in range(16):
            for k in range(3):
                total[s, 72:, 384 * k : 384 * (k + 1)] = product[
                    72 * s + 24 * k : 72 * s + 24 * (k + 1)
                ]
        out[...] = total[...].astype(bf16)


def gate_up_product_kernel(*refs):
    nm, rhs, out = refs[:2], refs[2:6], refs[7]

    def work(right):
        total = tn(nm[0][...], right[0][...]) + tn(nm[1][...], right[1][...])
        for i in range(4):
            out[i] = total[96 * i : 96 * (i + 1)].astype(bf16)

    for j in range(2):
        pl.when(pl.program_id(0) == j)(lambda j=j: work(rhs[2 * j : 2 * j + 2]))


def feed_forward_products(nm, cot, gate, up, hidden):
    parts = call(
        down_product_kernel,
        shaped((16, 96, 3 * WIDE), bf16),
        (4,),
        [(a, fixed(512, WIDE)) for a in hidden]
        + [(a, pl.BlockSpec((512, 384), lambda t: (0, t))) for a in cot],
        pl.BlockSpec((16, 96, WIDE), lambda t: (0, 0, 2)),
        scratch=[pltpu.VMEM((16, 96, WIDE), f32)],
        flops=2 * 1024 * D * WIDE,
        bytes_accessed=10 * 1024 * 1024,
    )
    return call(
        gate_up_product_kernel,
        shaped((16, 96, 3 * WIDE), bf16),
        (2, 4),
        [(a, pl.BlockSpec((512, 384), lambda j, g: (0, g))) for a in nm]
        + [(a, fixed(512, WIDE)) for pair in (gate, up) for a in pair]
        + [(parts, pl.BlockSpec(memory_space=pl.ANY))],
        pl.BlockSpec((4, 96, WIDE), lambda j, g: (g, 0, j)),
        aliases={6: 0},
        flops=2 * 1024 * D * 2 * WIDE,
        bytes_accessed=20 * 1024 * 1024,
    )


def feed_forward_kernel(n, *refs):
    nm_pieces, cot_pieces = refs[:n], refs[n : 2 * n]
    w_gate, w_up, w_dn = refs[2 * n : 2 * n + 3]
    nm, cot, hidden, grad_gate, grad_up, hn, total = refs[2 * n + 3 :]
    step = pl.program_id(0)

    @pl.when(step == 0)
    def _():
        for pieces, out in ((nm_pieces, nm), (cot_pieces, cot)):
            at = 0
            for piece in pieces:
                out[at : at + piece.shape[0]] = piece[...]
                at += piece.shape[0]

    gate = jnp.dot(nm[...], w_gate[...], preferred_element_type=f32)
    up = jnp.dot(nm[...], w_up[...], preferred_element_type=f32)
    act = nt(cot[...], w_dn[...])
    sigmoid_gate = jax.nn.sigmoid(gate)
    silu_gate = gate * sigmoid_gate
    hidden[...] = (silu_gate * up).astype(bf16)
    to_gate = (act * up * (sigmoid_gate * (1.0 + gate * (1.0 - sigmoid_gate)))).astype(bf16)
    to_up = (act * silu_gate).astype(bf16)
    grad_gate[...] = to_gate
    grad_up[...] = to_up
    term = nt(to_gate, w_gate[...]) + nt(to_up, w_up[...])

    @pl.when(step == 0)
    def _():
        total[...] = term

    @pl.when(step > 0)
    def _():
        total[...] += term

    @pl.when(step == 2)
    def _():
        hn[...] = total[...].astype(bf16)


def feed_forward(nm, cot, w_ffn, w_dn):
    whole, column = fixed(512, D), pl.BlockSpec((512, 384), lambda j: (0, j))
    wide, narrow = shaped((512, D), bf16), shaped((512, WIDE), bf16)
    return call(
        lambda *refs: feed_forward_kernel(len(nm), *refs),
        [wide, wide, narrow, narrow, narrow, wide],
        (3,),
        [(p, fixed(*p.shape)) for p in (*nm, *cot)]
        + [
            (w_ffn, pl.BlockSpec((D, 384), lambda j: (0, j))),
            (w_ffn, pl.BlockSpec((D, 384), lambda j: (0, 3 + j))),
            (w_dn, pl.BlockSpec((384, D), lambda j: (j, 0))),
        ],
        [whole, whole, column, column, column, whole],
        scratch=[pltpu.VMEM((512, D), f32)],
        flops=2 * 512 * D * 5 * WIDE,
        bytes_accessed=20 * 1024 * 1024,
        exps=512 * WIDE,
    )


def add(a, *others):
    total = a.astype(f32)
    for other in others:
        total = total + other.astype(f32)
    return total.astype(bf16)


def scattered(part, ring, pair):
    away = part(2, 1)
    half = halfway(away.shape[0])
    got = (
        moved(away, ring, pair, 0, 1),
        moved(part(-1, 1), ring, pair, -1, 0),
        moved(part(1, 1), ring, pair, 1, 0),
    )
    away, from_after, from_before = got
    away = add(part(2, 0), away)
    got = (
        moved(away[:half], ring, pair, -1, 0),
        moved(away[half:], ring, pair, 1, 0),
        moved(add(part(0, 1), from_after, from_before), ring, pair, 0, 1),
    )
    away_first, away_second, got_across = got
    back, ahead = part(-1, 0), part(1, 0)
    back = jnp.concatenate([add(back[:half], away_first), back[half:]], axis=0)
    ahead = jnp.concatenate([ahead[:half], add(ahead[half:], away_second)], axis=0)
    got = (moved(back, ring, pair, -1, 0), moved(ahead, ring, pair, 1, 0))
    return part(0, 0), got_across, *got


NEAR_FAR = [(0, 0), (0, 1), (-1, 0), (1, 0), (-1, 1), (1, 1), (2, 0), (2, 1)]


def parts_of(near, far):
    rows = near.shape[0] // 4

    def part(step, flip):
        i = NEAR_FAR.index((step, flip))
        array = near if i < 4 else far
        return array[i % 4 * rows : (i % 4 + 1) * rows]

    return part


def tied(*values):
    return lax.optimization_barrier(values)


def call(
    kernel, out, grid, ins, outs, scalars=(), scratch=(), aliases=None, flops=0, bytes_accessed=0, exps=0
):
    return pl.pallas_call(
        kernel,
        grid_spec=pltpu.PrefetchScalarGridSpec(
            num_scalar_prefetch=len(scalars),
            grid=grid,
            in_specs=[spec for _, spec in ins],
            out_specs=outs,
            scratch_shapes=scratch,
        ),
        out_shape=out,
        input_output_aliases=aliases or {},
        compiler_params=pltpu.CompilerParams(vmem_limit_bytes=50 * 1024 * 1024),
        cost_estimate=pl.CostEstimate(
            flops=flops, bytes_accessed=bytes_accessed, transcendentals=exps
        ),
    )(*scalars, *[array for array, _ in ins])


def fixed(*shape):
    return pl.BlockSpec(shape, lambda *_: (0,) * len(shape))


def shaped(shape, dtype):
    return jax.ShapeDtypeStruct(shape, dtype)


def exchanged(blocks, axes):
    return lax.all_to_all(blocks, axes, 0, 0, tiled=True)


def swap_core(block):
    return lax.ppermute(block, "core", [(0, 1), (1, 0)])


def summed(pieces):
    return jnp.sum(pieces.astype(f32), axis=0)


def mm(a, b):
    return jnp.dot(a, b, preferred_element_type=f32)


def mm_nt(a, b):
    return jnp.einsum("ik,jk->ij", a, b, preferred_element_type=f32)


def mm_tn(a, b):
    return jnp.einsum("ki,kj->ij", a, b, preferred_element_type=f32)


def shards(
    hidden_in, block_order, attn_gain, w_qkv, b_qkv, w_out, mlp_gain, w_gate_up, w_down, cotangent
):
    yi, qi = lax.axis_index("y"), lax.axis_index("xl")
    ci = 2 * yi + qi
    fi = lax.axis_index(FSDP)
    core = lax.axis_index("core")
    group = yi // 2
    half = qi.astype(jnp.int32)[None]
    x_own, cot_own = hidden_in[0], cotangent[0]

    down = lax.dynamic_slice_in_dim(w_down, PART * ci, PART, 0)
    down = folded(jnp.concatenate([down, jnp.zeros((2, D), bf16)], axis=0))
    ffn_own = jnp.concatenate([picked(ci, w_gate_up), down], axis=1)
    w_ffn = lax.all_gather(ffn_own, FSDP, axis=0, tiled=True)

    starts = (
        HD * (3 * yi + 2 * qi),
        HD * (3 * yi + 1),
        D + HD * group,
        D + HD * (KVH + group),
    )

    def my_columns(array):
        return jnp.concatenate(
            [lax.dynamic_slice_in_dim(array, s, HD, array.ndim - 1) for s in starts], axis=-1
        )

    bias_low = jnp.concatenate([b_qkv[:96, None], jnp.pad(b_qkv[96:], (0, 64))[:, None]], axis=1)
    extra = jnp.concatenate([attn_gain[:, None], mlp_gain[:, None], bias_low], axis=1)
    extra = jnp.pad(extra, ((0, 0), (0, 124)))
    packed = jnp.concatenate([my_columns(w_qkv), extra, w_out], axis=1)
    packed = jnp.stack([packed, lax.ppermute(packed, "xh", [(0, 1), (1, 0)])])
    own = exchanged(jnp.broadcast_to(packed[:, :, :640], (4, 2, 96, 640)), ("z",))
    x_all = gathered(x_own, "y", "xl", True).reshape(1024, D)
    own, x_all, cot_own, packed = tied(own, x_all, cot_own, packed)
    w_mine, extras = woven(own, 512, 128)
    own_out = exchanged(jnp.broadcast_to(packed[:, :, 640:], (4, 2, 96, D)), ("z",))
    cot_gather = gather_stages(cot_own, "y", "xl")
    cot_state = next(cot_gather)

    extras = extras.astype(f32)
    gain_one = extras[:, 0][None]
    gain_two = extras[:, 1][None]
    bias_rows = extras.reshape(16, 96, 128)
    bias_all = jnp.concatenate([bias_rows[:, :, 2], bias_rows[:, :32, 3]], axis=1).reshape(2048)
    bias_mine = my_columns(bias_all)

    order = block_order[0]
    positions = (order[:, None] * 64 + jnp.arange(64, dtype=jnp.int32)[None, :]).reshape(1024)
    frequency = jnp.exp(jnp.arange(0, HD, 2, dtype=f32) * (-math.log(rope_base) / HD))
    angles = positions.astype(f32)[:, None] * frequency[None, :]
    cosine, sine = jnp.cos(angles), jnp.sin(angles)
    cosine = jnp.concatenate([cosine, cosine], axis=1)
    sine = jnp.concatenate([-sine, sine], axis=1)
    pos_col, pos_row = positions[:, None], positions[None, :]

    resid_all = x_all.astype(f32)
    inv_all = lax.rsqrt(jnp.mean(resid_all * resid_all, axis=-1, keepdims=True) + eps)
    normed_all = (resid_all * inv_all * gain_one).astype(bf16)
    projected = mm(normed_all, w_mine) + bias_mine
    att_mine, queries, lse, keys, values = attend(half, projected, cosine, sine, pos_col, pos_row)
    att_mine, own_out, *cot_state = tied(att_mine, own_out, *cot_state)
    (w_out_all,) = woven(own_out, D)
    cot_state = cot_gather.send(cot_state)
    got = exchanged(att_mine.reshape(8, 192, HD), CTX)
    got, *cot_state = tied(got, *cot_state)
    cot = [g[3] for g in cot_gather.send(cot_gather.send(cot_state))]
    attended, middle, normed_mid, inv_second = to_middle(got, w_out_all, x_own, gain_two)
    nm = [g[3] for g in gather_eight(normed_mid, "y", "xl")]
    attended_all = lax.all_gather(attended, CTX, axis=0, tiled=True)

    w_dn = down_weights(w_ffn)
    nm_near, cot_near, hidden_near, gg_near, gu_near, hn_near = feed_forward(
        nm[:4], cot[:4], w_ffn, w_dn
    )
    nm_far, cot_far, hidden_far, gg_far, gu_far, hn_far = feed_forward(
        nm[4:], cot[4:], w_ffn, w_dn
    )
    operands = (nm_near, nm_far, cot_near, cot_far, gg_near, gg_far, gu_near, gu_far)
    hn_near, hn_far, hidden_near, hidden_far, *operands = tied(
        hn_near, hn_far, hidden_near, hidden_far, *operands
    )
    hn_parts = scattered(parts_of(hn_near, hn_far), "y", "xl")
    ffn_parts = feed_forward_products(
        *(operands[i : i + 2] for i in range(0, 8, 2)), (hidden_near, hidden_far)
    )
    ffn_sum = lax.psum_scatter(ffn_parts, FSDP, scatter_dimension=0, tiled=True)[0]

    grad_middle, send = middle_back(hn_parts, middle, inv_second, gain_two, cot_own, w_out_all)
    got = exchanged(send, CTX)
    gp_mine, columns = attend_back(
        half, got, queries, lse, keys, values, cosine, sine, pos_col, pos_row
    )
    xn_parts = mm_nt(gp_mine, w_mine).astype(bf16).reshape(8, 128, D)
    out_part = parts_of(
        mm(hidden_near, w_dn).astype(bf16), mm(hidden_far, w_dn).astype(bf16)
    )

    def xn_out_part(step, flip):
        at = place("y", "xl", True, step, flip)
        xn = lax.dynamic_index_in_dim(xn_parts, at, 0, keepdims=False)
        return jnp.concatenate([xn, out_part(step, flip)], axis=1)

    xn_parts, gp_mine, columns = tied(xn_parts, gp_mine, columns)
    gb_mine = jnp.sum(gp_mine.astype(f32), axis=0).astype(bf16).reshape(4, HD)
    gb_mine = jnp.broadcast_to(jnp.pad(gb_mine, ((0, 92), (0, 0))), (16, 96, HD))
    mine_parts = jnp.concatenate(
        [
            mm_tn(normed_all, gp_mine).astype(bf16).reshape(16, 96, 512),
            mm_tn(attended_all, columns).astype(bf16).reshape(16, 96, 256),
            gb_mine,
        ],
        axis=2,
    )
    pairs = mine_parts.reshape(8, 2, 96, MINE)
    mine_both = add(
        lax.dynamic_index_in_dim(pairs, core, 1, keepdims=False),
        swap_core(lax.dynamic_index_in_dim(pairs, 1 - core, 1, keepdims=False)),
    )
    mine_sum = summed(exchanged(mine_both, ("xh", "z"))).astype(bf16)

    xn_out = scattered(xn_out_part, "y", "xl")
    xn_out = sum(term.astype(f32) for term in xn_out)
    grad_xn = xn_out[:, :D]
    hidden_out = middle + xn_out[:, D:]
    resid = x_own.astype(f32)
    inv_first = lax.rsqrt(jnp.mean(resid * resid, axis=-1, keepdims=True) + eps)
    scaled = grad_xn * gain_one
    grad_in = (
        grad_middle
        + inv_first * scaled
        - resid * (inv_first**3) * jnp.mean(resid * scaled, axis=-1, keepdims=True)
    )

    grad_w_gate_up, grad_w_down, grad_w_qkv, grad_w_out, grad_bias, gain_sum, gain_sum_qkv = (
        weight_gradients(
            gather_eight(jnp.concatenate([ffn_sum, mine_sum], axis=1), "y", "xl"), w_gate_up, w_qkv
        )
    )
    grad_mlp_gain = gain_sum / mlp_gain.astype(f32)
    grad_attn_gain = gain_sum_qkv / attn_gain.astype(f32)
    grad_b_qkv = lax.dynamic_index_in_dim(grad_bias, fi, 0, keepdims=False)

    return (
        hidden_out[None],
        grad_in[None],
        grad_attn_gain,
        grad_w_qkv,
        grad_b_qkv,
        grad_w_out,
        grad_mlp_gain,
        grad_w_gate_up,
        grad_w_down,
    )


def solution(mesh):
    fine = Mesh(mesh.devices.reshape(4, 2, 2, 4, 2), CTX + FSDP)
    rows = P(FSDP, CTX, None)
    vector = P(FSDP)
    matrix = P(FSDP, None)
    return jax.shard_map(
        shards,
        mesh=fine,
        in_specs=(rows, matrix, vector, matrix, vector, matrix, vector, matrix, matrix, rows),
        out_specs=(rows, rows, vector, matrix, vector, matrix, vector, matrix, matrix),
        check_vma=False,
    )
```

```python
import math

import jax
import jax.numpy as jnp
from jax import lax
from jax.experimental import pallas as pl
from jax.experimental.pallas import tpu as pltpu
from jax.sharding import Mesh, PartitionSpec as P

D = 1536
H = 12
KVH = 2
HD = 128
FF = 8960
PART = FF // 128
WIDE = 1152
MINE = 896

CTX = ("y", "xl")
FSDP = ("xh", "z", "core")

eps = 1e-06
rope_base = 1000000.0
masked_value = -1e30
bf16 = jnp.bfloat16
f32 = jnp.float32


def moved(block, ring, pair, step, flip):
    size = lax.axis_size(ring)
    if step == 0:
        return lax.ppermute(block, pair, [(0, 1), (1, 0)])
    return lax.ppermute(block, ring, [(i, (i + step) % size) for i in range(size)])


def halfway(rows):
    return rows // 32 * 16


def gather_stages(block, ring, pair, by_ring=False):
    half = halfway(block.shape[0])
    across, before, after_ = yield (
        moved(block, ring, pair, 0, 1),
        moved(block, ring, pair, 1, 0),
        moved(block, ring, pair, -1, 0),
    )
    far_first, far_second, across_before, across_after = yield (
        moved(before[:half], ring, pair, 1, 0),
        moved(after_[half:], ring, pair, -1, 0),
        moved(across, ring, pair, 1, 0),
        moved(across, ring, pair, -1, 0),
    )
    if by_ring:
        last = (
            moved(across_before[:half], ring, pair, 1, 0),
            moved(across_after[half:], ring, pair, -1, 0),
        )
    else:
        last = (moved(far_first, ring, pair, 0, 1), moved(far_second, ring, pair, 0, 1))
    across_far_first, across_far_second = yield last
    yield [
        (0, 0, 0, block),
        (0, 1, 0, across),
        (-1, 0, 0, before),
        (1, 0, 0, after_),
        (-1, 1, 0, across_before),
        (1, 1, 0, across_after),
        (2, 0, 0, far_first),
        (2, 0, half, far_second),
        (2, 1, 0, across_far_first),
        (2, 1, half, across_far_second),
    ]


def in_step(*gathers):
    states = [next(g) for g in gathers]
    for _ in range(3):
        if len(gathers) > 1:
            states = lax.optimization_barrier(states)
        states = [g.send(state) for g, state in zip(gathers, states)]
    return states


def gather_eight(block, ring, pair):
    return in_step(gather_stages(block, ring, pair))[0]


def place(ring, pair, ring_major, step, flip):
    size = lax.axis_size(ring)
    r = (lax.axis_index(ring) + step) % size
    q = lax.axis_index(pair)
    q = 1 - q if flip else q
    return r * 2 + q if ring_major else q * size + r


def places_of(got, ring, pair, ring_major):
    return [place(ring, pair, ring_major, step, flip) for step, flip, _, _ in got]


def pick_kernel(at_ref, weights, out):
    for c in range(8):

        @pl.when(at_ref[0] == c)
        def _():
            for part in range(2):
                for s in range(16):
                    start, to = part * FF + 560 * s + PART * c, part * WIDE + 72 * s
                    out[:, to : to + PART] = weights[:, start : start + PART]
                    out[:, to + PART : to + 72] = jnp.zeros((96, 2), bf16)


def picked(slice_index, weights):
    return call(
        pick_kernel,
        shaped((96, 2 * WIDE), bf16),
        (1,),
        [(weights, fixed(96, 2 * FF))],
        fixed(96, 2 * WIDE),
        mib=12,
        scalars=(slice_index.astype(jnp.int32)[None],),
        bytes_accessed=4 * 1024 * 1024,
    )


def folded(rows):
    rest = rows[:, WIDE:]
    rest = jnp.concatenate([rest[24 * k : 24 * (k + 1)] for k in range(3)], axis=1)
    return jnp.concatenate([rows[:, :WIDE], rest], axis=0)


def unfolded(rows):
    rest = jnp.concatenate([rows[72:, 384 * k : 384 * (k + 1)] for k in range(3)], axis=0)
    return jnp.concatenate([rows[:72], rest], axis=1)


def unfold_kernel(weights, out):
    out[0] = unfolded(weights[...].astype(f32)).astype(bf16)


def down_weights(w_ffn):
    return call(
        unfold_kernel,
        shaped((16, 72, D), bf16),
        (16,),
        [(w_ffn, pl.BlockSpec((96, WIDE), lambda s: (s, 2)))],
        pl.BlockSpec((1, 72, D), lambda s: (s, 0, 0)),
        bytes_accessed=8 * 1024 * 1024,
    ).reshape(WIDE, D)


def last_kernel(at_ref, *refs):
    pieces, weights, weights_qkv, gains = refs[:10], *refs[10:13]
    out, out_qkv, out_out, vectors, blocks, sums, bias = refs[13:]
    step = pl.program_id(0)
    for i in range(6):
        blocks[at_ref[i]] = pieces[i][...]
    for i in (6, 8):
        blocks[at_ref[i]] = jnp.where(step < 3, pieces[i][...], pieces[i + 1][...])
    total = jnp.zeros((16, 1), f32)
    for part in range(2):
        for s in range(16):
            start = part * WIDE + 72 * s
            row = jnp.concatenate(
                [blocks[c, :, start : start + PART] for c in range(8)], axis=1
            )
            out[:, part * FF + 560 * s : part * FF + 560 * (s + 1)] = row.astype(f32)
    for at in range(0, 2 * FF, 1792):
        lanes = slice(at, at + 1792)
        total = total + jnp.sum(
            out[:, lanes] * weights[:, lanes].astype(f32), axis=1, keepdims=True
        )
    rows = pl.ds(pl.multiple_of(step * 16, 16), 16)
    sums[0, rows] = jnp.broadcast_to(total, (16, HD))

    def whole(c, at, rows=slice(0, 16)):
        start = 3 * WIDE + at * HD
        return blocks[c, rows, start : start + HD].astype(f32)

    def heads(term):
        for y in range(4):
            yield 3 * y, term(2 * y, 0)
            yield 3 * y + 1, term(2 * y, 1) + term(2 * y + 1, 1)
            yield 3 * y + 2, term(2 * y + 1, 0)
        for kind in range(2):
            for group in range(2):
                yield 12 + 2 * kind + group, sum(term(4 * group + i, 2 + kind) for i in range(4))

    total = jnp.zeros((16, 1), f32)
    for h, value in heads(whole):
        lanes = slice(h * HD, (h + 1) * HD)
        out_qkv[:, lanes] = value
        total = total + jnp.sum(
            value * weights_qkv[:, lanes].astype(f32), axis=1, keepdims=True
        )
    sums[1, rows] = jnp.broadcast_to(total, (16, HD))
    for y in range(4):
        at = 3 * y * HD
        out_out[:, at : at + HD] = whole(2 * y, 4)
        out_out[:, at + HD : at + 2 * HD] = whole(2 * y, 5) + whole(2 * y + 1, 5)
        out_out[:, at + 2 * HD : at + 3 * HD] = whole(2 * y + 1, 4)

    @pl.when(step == 0)
    def _():
        for h, value in heads(lambda c, kind: whole(c, 6)[kind : kind + 1]):
            bias[h : h + 1] = value

    @pl.when(step == 5)
    def _():
        vectors[...] = jnp.zeros_like(vectors)
        for i in range(2):
            vectors[i : i + 1, :96] = sums[i].T[:1, :96] / gains[i : i + 1, :96]
        vectors[2:3] = bias[pl.ds(at_ref[10], 1)]


def last_down_kernel(at_ref, *refs):
    pieces, out, blocks = refs[:10], refs[10], refs[11]
    for i in range(6):
        blocks[at_ref[i]] = pieces[i][...].astype(f32)
    for i in (6, 8):
        blocks[at_ref[i], :48] = pieces[i][...].astype(f32)
        blocks[at_ref[i], 48:] = pieces[i + 1][...].astype(f32)
    for c in range(8):
        out[PART * c : PART * (c + 1)] = unfolded(blocks[c])[:PART]


def weight_gradients(got, weights, weights_qkv, gains, head):
    pieces = [g[3] for g in got]
    places = jnp.stack([*places_of(got, "y", "xl", True), head]).astype(jnp.int32)
    width = 3 * WIDE + MINE

    def rows(i, at):
        return i, 0

    maps = [rows] * 6 + [
        lambda i, at: (jnp.minimum(i, 2), 0),
        lambda i, at: (jnp.maximum(i - 3, 0), 0),
    ] * 2
    w_gate_up, w_qkv, w_out, vectors = call(
        last_kernel,
        [
            shaped((96, 2 * FF), f32),
            shaped((96, 2048), f32),
            shaped((96, D), f32),
            shaped((8, HD), f32),
        ],
        (6,),
        [(p, pl.BlockSpec((16, width), m)) for p, m in zip(pieces, maps)]
        + [
            (weights, pl.BlockSpec((16, 2 * FF), rows)),
            (weights_qkv, pl.BlockSpec((16, 2048), rows)),
            (gains, fixed(8, HD)),
        ],
        [
            pl.BlockSpec((16, 2 * FF), rows),
            pl.BlockSpec((16, 2048), rows),
            pl.BlockSpec((16, D), rows),
            fixed(8, HD),
        ],
        scalars=(places,),
        scratch=[
            pltpu.VMEM((8, 16, width), bf16),
            pltpu.VMEM((2, 96, HD), f32),
            pltpu.VMEM((16, HD), f32),
        ],
        mib=24,
        bytes_accessed=96 * 2 * FF * 8,
    )
    w_down = call(
        last_down_kernel,
        shaped((560, D), f32),
        (1,),
        [(p, pl.BlockSpec((p.shape[0], WIDE), lambda i, at: (0, 2))) for p in pieces],
        fixed(560, D),
        scalars=(places,),
        scratch=[pltpu.VMEM((8, 96, WIDE), f32)],
        mib=24,
        bytes_accessed=6 * 1024 * 1024,
    )
    return w_gate_up, w_down, w_qkv, w_out, vectors


def pack_kernel(at, weights, vectors, out):
    for i in range(4):
        out[:, i * HD : (i + 1) * HD] = weights[:, pl.ds(pl.multiple_of(at[i] * HD, HD), HD)]
    out[:, 4 * HD :] = jnp.concatenate([vectors[...], jnp.zeros((80, HD), bf16)], axis=0)


def packed_columns(heads, weights, vectors):
    rows = jnp.concatenate([jnp.stack(vectors), jnp.zeros((13, HD), bf16)], axis=0)
    return call(
        pack_kernel,
        shaped((96, 640), bf16),
        (1,),
        [(weights, fixed(96, 2048)), (rows, fixed(16, HD))],
        fixed(96, 640),
        scalars=(jnp.stack(heads).astype(jnp.int32),),
        bytes_accessed=2 * 1024 * 1024,
    )


def turned(field, cos_ref, sin_ref):
    return field * cos_ref + pltpu.roll(field, HD // 2, 1) * sin_ref


def nt(a, b):
    return lax.dot_general(a, b, (((1,), (1,)), ((), ())), preferred_element_type=f32)


def tn(a, b):
    return lax.dot_general(a, b, (((0,), (0,)), ((), ())), preferred_element_type=f32)


SCALE = 1.0 / math.sqrt(HD)


def attend_kernel(*refs):
    at, pieces, own, other, cos, sin, pos_col, pos_row = refs[0], refs[1:11], *refs[11:17]
    att, queries, lse, keys, values, normed, weights, gains, x, woven, proj = refs[17:]
    c, core, half = pl.program_id(0), at[10], at[11]

    @pl.when(c == 0)
    def _():
        for i, piece in enumerate(pieces):
            first = 64 if i in (7, 9) else 0
            x[at[i], first : first + piece.shape[0]] = piece[...]
        for i in range(8):
            index = 4 * (at[16] if i % 2 == 0 else 1 - at[16]) + i // 2
            woven[index, core] = own[i]
            woven[index, 1 - core] = other[i]
        gains[...] = jnp.zeros_like(gains)
        for s in range(16):
            weights[96 * s : 96 * (s + 1)] = woven[s // 2, s % 2, :, :512]
            rows = woven[s // 2, s % 2, :16, 512:].astype(f32)
            gains[0:2, 96 * s : 96 * (s + 1)] = rows[0:2, :96]
        bias = jnp.concatenate(
            [
                woven[at[12 + i] // 2, at[12 + i] % 2, :16, 512:].astype(f32)[2:3]
                for i in range(4)
            ],
            axis=1,
        )
        for i in range(8):
            rows = x[i].astype(f32)
            inv = lax.rsqrt(jnp.mean(rows * rows, axis=1, keepdims=True) + eps)
            normed[128 * i : 128 * (i + 1)] = (rows * inv * gains[0:1]).astype(bf16)
        proj[...] = jnp.dot(normed[...], weights[...], preferred_element_type=f32) + bias
        keys[...] = turned(proj[:, 2 * HD : 3 * HD], cos[...], sin[...]).astype(bf16)
        values[...] = proj[:, 3 * HD :].astype(bf16)

    rows = pl.ds(pl.multiple_of(c * 128, 128), 128)
    part = pl.ds(pl.multiple_of(c * 128 + half * 64, 64), 64)
    query = jnp.concatenate(
        [
            turned(proj[rows, :HD], cos[rows], sin[rows]),
            turned(proj[part, HD : 2 * HD], cos[part], sin[part]),
        ],
        axis=0,
    ).astype(bf16)
    queries[...] = query
    scores = nt(query, keys[...]) * SCALE
    seen = jnp.concatenate([pos_col[rows], pos_col[part]], axis=0) >= pos_row[...]
    scores = jnp.where(seen, scores, masked_value)
    row_max = jnp.max(scores, axis=1, keepdims=True)
    exponent = jnp.exp(scores - row_max)
    total = jnp.sum(exponent, axis=1, keepdims=True)
    probability = (exponent / total).astype(bf16)
    att[...] = jnp.dot(probability, values[...], preferred_element_type=f32).astype(bf16)
    lse[...] = jnp.broadcast_to(row_max + jnp.log(total), (192, HD))


def attend(x_got, own, core, half, heads, cos, sin, pos_col, pos_row):
    block = pl.BlockSpec((192, HD), lambda c, at: (c, 0))
    at = [*places_of(x_got, "y", "xl", True), core, half, *heads, lax.axis_index("xh")]
    at = jnp.stack(at).astype(jnp.int32)
    own = own.reshape(8, 96, 640)
    return call(
        attend_kernel,
        [
            shaped((1536, HD), bf16),
            shaped((1536, HD), bf16),
            shaped((1536, HD), f32),
            shaped((1024, HD), bf16),
            shaped((1024, HD), bf16),
            shaped((1024, D), bf16),
            shaped((D, 512), bf16),
            shaped((8, D), f32),
            shaped((8, 128, D), bf16),
        ],
        (8,),
        [(g[3], fixed(g[3].shape[0], D)) for g in x_got]
        + [
            (own, fixed(8, 96, 640)),
            (swap_core(own), fixed(8, 96, 640)),
            (cos, fixed(1024, HD)),
            (sin, fixed(1024, HD)),
            (pos_col, fixed(1024, 1)),
            (pos_row, fixed(1, 1024)),
        ],
        [
            block,
            block,
            block,
            fixed(1024, HD),
            fixed(1024, HD),
            fixed(1024, D),
            fixed(D, 512),
            fixed(8, D),
            fixed(8, 128, D),
        ],
        scalars=(at,),
        scratch=[
            pltpu.VMEM((8, 2, 96, 640), bf16),
            pltpu.VMEM((1024, 512), f32),
        ],
        mib=40,
        flops=4 * 1536 * 1024 * HD + 2 * 1024 * D * 512,
        bytes_accessed=14 * 1024 * 1024,
        exps=1536 * 1024,
    )


def attend_back_kernel(
    half_ref, got, queries, lse, keys, values, cos, sin, pos_col, pos_row, grads, columns, gk, gv
):
    c, half = pl.program_id(0), half_ref[0]

    @pl.when(c == 0)
    def _():
        gk[...] = jnp.zeros_like(gk)
        gv[...] = jnp.zeros_like(gv)

    rows = pl.ds(pl.multiple_of(c * 128, 128), 128)
    part = pl.ds(pl.multiple_of(c * 128 + half * 64, 64), 64)
    rest = pl.ds(pl.multiple_of(c * 128 + (1 - half) * 64, 64), 64)
    out = got[0, :192]
    query = queries[...]
    scores = nt(query, keys[...]) * SCALE
    seen = jnp.concatenate([pos_col[rows], pos_col[part]], axis=0) >= pos_row[...]
    scores = jnp.where(seen, scores, masked_value)
    probs = jnp.exp(scores - lse[:, :1])
    grad_prob = nt(out, values[...])
    inner = jnp.sum(probs * grad_prob, axis=1, keepdims=True)
    grad_scores = (probs * (grad_prob - inner)).astype(bf16)
    grad_query = jnp.dot(grad_scores, keys[...], preferred_element_type=f32) * SCALE
    gk[...] += tn(grad_scores, query)
    gv[...] += tn(probs.astype(bf16), out)
    grads[rows, :HD] = turned(grad_query[:128], cos[rows], -sin[rows]).astype(bf16)
    grads[part, HD : 2 * HD] = turned(grad_query[128:], cos[part], -sin[part]).astype(bf16)
    grads[rest, HD : 2 * HD] = jnp.zeros((64, HD), bf16)
    columns[:, :HD] = got[0, 192:320]
    columns[pl.ds(pl.multiple_of(half * 64, 64), 64), HD:] = got[0, 320:]
    columns[pl.ds(pl.multiple_of((1 - half) * 64, 64), 64), HD:] = jnp.zeros((64, HD), bf16)

    @pl.when(c == 7)
    def _():
        grads[:, 2 * HD : 3 * HD] = turned(gk[...] * SCALE, cos[...], -sin[...]).astype(bf16)
        grads[:, 3 * HD :] = gv[...].astype(bf16)


def attend_back(half, got, queries, lse, keys, values, cos, sin, pos_col, pos_row):
    block = pl.BlockSpec((192, HD), lambda c, half: (c, 0))
    return call(
        attend_back_kernel,
        [shaped((1024, 4 * HD), bf16), shaped((1024, 2 * HD), bf16)],
        (8,),
        [
            (got, pl.BlockSpec((1, 384, HD), lambda c, half: (c, 0, 0))),
            (queries, block),
            (lse, block),
            (keys, fixed(1024, HD)),
            (values, fixed(1024, HD)),
            (cos, fixed(1024, HD)),
            (sin, fixed(1024, HD)),
            (pos_col, fixed(1024, 1)),
            (pos_row, fixed(1, 1024)),
        ],
        [fixed(1024, 4 * HD), pl.BlockSpec((128, 2 * HD), lambda c, half: (c, 0))],
        scalars=(half,),
        scratch=[pltpu.VMEM((1024, HD), f32), pltpu.VMEM((1024, HD), f32)],
        mib=50,
        flops=10 * 1536 * 1024 * HD,
        bytes_accessed=6 * 1024 * 1024,
        exps=1536 * 1024,
    )


def place_kernel(*refs):
    pieces, out = refs[:10], refs[10]
    for i, piece in enumerate(pieces):
        at = 128 * (i if i < 6 else 6 + (i - 6) // 2) + (64 if i in (7, 9) else 0)
        out[at : at + piece.shape[0]] = piece[...]


def placed(got):
    return call(
        place_kernel,
        shaped((1024, D), bf16),
        (1,),
        [(g[3], pl.BlockSpec((g[3].shape[0], D), lambda i: (0, 1))) for g in got],
        fixed(1024, D),
        bytes_accessed=4 * 1024 * D,
    )


def middle_kernel(at, *refs):
    pieces, own, other, x, gains = refs[:10], *refs[10:14]
    attended, normed, middle, inverse, w_out, heads = refs[14:]
    step, core, side = pl.program_id(0), at[10], at[11]

    @pl.when(step == 0)
    def _():
        for i in range(8):
            index = 2 * (4 * (side if i % 2 == 0 else 1 - side) + i // 2)
            w_out[index + core] = own[i]
            w_out[index + 1 - core] = other[i]
        for i, piece in enumerate(pieces):
            first = 768 if i in (7, 9) else 0
            heads[at[i], first : first + piece.shape[0]] = piece[...]

    block = at[12 + step]
    rows = pl.ds(pl.multiple_of(block * 192, 64), 128)
    part = pl.ds(pl.multiple_of(block * 192 + 128, 64), 64)
    for y in range(4):
        for q in range(2):
            whole, split = HD * (3 * y + 2 * q), HD * (3 * y + 1)
            attended[:, whole : whole + HD] = heads[2 * y + q, rows]
            attended[64 * q : 64 * (q + 1), split : split + HD] = heads[2 * y + q, part]
    weights = w_out[...].reshape(D, D)
    mid = x[0].astype(f32) + jnp.dot(attended[...], weights, preferred_element_type=f32)
    inv = lax.rsqrt(jnp.mean(mid * mid, axis=1, keepdims=True) + eps)
    normed[...] = (mid * inv * gains[1:2]).astype(bf16)

    @pl.when(step == 0)
    def _():
        middle[...] = mid
        inverse[...] = jnp.broadcast_to(inv, (128, HD))


def to_middle(got, own, core, side, x, gains):
    own = own.reshape(8, 96, D)
    order = [place("y", "xl", True, step, flip) for step, flip in ORDER]
    *outs, w_out = call(
        middle_kernel,
        [
            shaped((1024, D), bf16),
            shaped((1024, D), bf16),
            shaped((128, D), f32),
            shaped((128, HD), f32),
            shaped((16, 96, D), bf16),
        ],
        (8,),
        [(g[3], fixed(*g[3].shape)) for g in got]
        + [
            (own, fixed(8, 96, D)),
            (swap_core(own), fixed(8, 96, D)),
            (x, pl.BlockSpec((1, 128, D), lambda b, at: (at[12 + b], 0, 0))),
            (gains, fixed(8, D)),
        ],
        [
            pl.BlockSpec((128, D), lambda b, at: (at[12 + b], 0)),
            pl.BlockSpec((128, D), lambda b, at: (b, 0)),
            fixed(128, D),
            fixed(128, HD),
            fixed(16, 96, D),
        ],
        scalars=(
            jnp.stack([*places_of(got, "y", "xl", True), core, side, *order]).astype(jnp.int32),
        ),
        scratch=[pltpu.VMEM((8, 1536, HD), bf16)],
        mib=40,
        flops=2 * 1024 * D * D,
        bytes_accessed=20 * 1024 * 1024,
    )
    return *outs, w_out.reshape(D, D)


def middle_back_kernel(a, b, c, d, middle, inverse, gain, cot, w_out, grad_middle, send):
    grad_hn = a[...].astype(f32) + b[...].astype(f32) + c[...].astype(f32) + d[...].astype(f32)
    inv, mid = inverse[:, :1], middle[...]
    scaled = grad_hn * gain[1:2]
    inner = jnp.mean(mid * scaled, axis=1, keepdims=True)
    grad = cot[...].astype(f32) + inv * scaled - mid * (inv * inv * inv * inner)
    grad_middle[...] = grad
    grad_attn = grad.astype(bf16)
    heads = nt(grad_attn, w_out[...]).astype(bf16)
    for y in range(4):
        for q in range(2):
            whole, split = HD * (3 * y + 2 * q), HD * (3 * y + 1)
            half = slice(64 * q, 64 * (q + 1))
            send[2 * y + q, :128] = heads[:, whole : whole + HD]
            send[2 * y + q, 128:192] = heads[half, split : split + HD]
            send[2 * y + q, 192:320] = grad_attn[:, whole : whole + HD]
            send[2 * y + q, 320:] = grad_attn[half, split : split + HD]


def middle_back(parts, middle, inverse, gain, cot, w_out):
    row = fixed(128, D)
    return call(
        middle_back_kernel,
        [shaped((128, D), f32), shaped((8, 384, HD), bf16)],
        (1,),
        [(p, row) for p in parts]
        + [
            (middle, row),
            (inverse, fixed(128, HD)),
            (gain, fixed(8, D)),
            (cot, row),
            (w_out, fixed(D, D)),
        ],
        [row, fixed(8, 384, HD)],
        mib=50,
        flops=2 * 128 * D * D,
        bytes_accessed=10 * 1024 * 1024,
    )


def down_product_kernel(*refs):
    hidden, cot, out, total = refs[:2], refs[2:4], refs[4], refs[5]
    step = pl.program_id(0)
    product = tn(hidden[0][...], cot[0][...]) + tn(hidden[1][...], cot[1][...])

    for k in range(3):

        @pl.when(step == k)
        def _():
            for s in range(16):
                total[s, :72, 384 * k : 384 * (k + 1)] = product[72 * s : 72 * (s + 1)]

    @pl.when(step == 3)
    def _():
        for s in range(16):
            for k in range(3):
                total[s, 72:, 384 * k : 384 * (k + 1)] = product[
                    72 * s + 24 * k : 72 * s + 24 * (k + 1)
                ]
        for s in range(16):
            out[s % 8, s // 8] = total[s].astype(bf16)


def gate_up_product_kernel(*refs):
    nm, rhs, out = refs[:2], refs[2:6], refs[7]

    def work(right):
        total = tn(nm[0][...], right[0][...]) + tn(nm[1][...], right[1][...])
        for i in range(4):
            out[i, 0] = total[96 * i : 96 * (i + 1)].astype(bf16)

    for j in range(2):
        pl.when(pl.program_id(0) == j)(lambda j=j: work(rhs[2 * j : 2 * j + 2]))


def down_product(cot, hidden):
    return call(
        down_product_kernel,
        shaped((8, 2, 96, 3 * WIDE), bf16),
        (4,),
        [(a, fixed(512, WIDE)) for a in hidden]
        + [
            (cot, pl.BlockSpec((512, 384), lambda t: (0, t))),
            (cot, pl.BlockSpec((512, 384), lambda t: (1, t))),
        ],
        pl.BlockSpec((8, 2, 96, WIDE), lambda t: (0, 0, 0, 2)),
        scratch=[pltpu.VMEM((16, 96, WIDE), f32)],
        mib=56,
        flops=2 * 1024 * D * WIDE,
        bytes_accessed=10 * 1024 * 1024,
    )


def gate_up_product(nm, gate, up, parts):
    return call(
        gate_up_product_kernel,
        shaped((8, 2, 96, 3 * WIDE), bf16),
        (2, 4),
        [
            (nm, pl.BlockSpec((512, 384), lambda j, g: (0, g))),
            (nm, pl.BlockSpec((512, 384), lambda j, g: (1, g))),
        ]
        + [(a, fixed(512, WIDE)) for pair in (gate, up) for a in pair]
        + [(parts, pl.BlockSpec(memory_space=pl.ANY))],
        pl.BlockSpec((4, 1, 96, WIDE), lambda j, g: (g % 2, g // 2, 0, j)),
        aliases={6: 0},
        mib=56,
        flops=2 * 1024 * D * 2 * WIDE,
        bytes_accessed=20 * 1024 * 1024,
    )


def feed_forward_kernel(
    nm, cot, w_gate, w_up, w_dn, hidden, grad_gate, grad_up, hn, total
):
    step = pl.program_id(0)
    gate = jnp.dot(nm[...], w_gate[...], preferred_element_type=f32)
    up = jnp.dot(nm[...], w_up[...], preferred_element_type=f32)
    act = nt(cot[...], w_dn[...])
    sigmoid_gate = jax.nn.sigmoid(gate)
    silu_gate = gate * sigmoid_gate
    hidden[...] = (silu_gate * up).astype(bf16)
    to_gate = (act * up * (sigmoid_gate * (1.0 + gate * (1.0 - sigmoid_gate)))).astype(bf16)
    to_up = (act * silu_gate).astype(bf16)
    grad_gate[...] = to_gate
    grad_up[...] = to_up
    term = nt(to_gate, w_gate[...]) + nt(to_up, w_up[...])

    @pl.when(step == 0)
    def _():
        total[...] = term

    @pl.when(step > 0)
    def _():
        total[...] += term

    @pl.when(step == 2)
    def _():
        hn[...] = total[...].astype(bf16)


def feed_forward(nm, cot, w_ffn, w_dn, half):
    whole, column = fixed(512, D), pl.BlockSpec((512, 384), lambda j: (0, j))
    narrow = shaped((512, WIDE), bf16)
    rows = pl.BlockSpec((512, D), lambda j: (half, 0))
    return call(
        feed_forward_kernel,
        [narrow, narrow, narrow, shaped((512, D), bf16)],
        (3,),
        [
            (nm, rows),
            (cot, rows),
            (w_ffn, pl.BlockSpec((D, 384), lambda j: (0, j))),
            (w_ffn, pl.BlockSpec((D, 384), lambda j: (0, 3 + j))),
            (w_dn, pl.BlockSpec((384, D), lambda j: (j, 0))),
        ],
        [column, column, column, whole],
        scratch=[pltpu.VMEM((512, D), f32)],
        mib=36,
        flops=2 * 512 * D * 5 * WIDE,
        bytes_accessed=20 * 1024 * 1024,
        exps=512 * WIDE,
    )


def add(a, *others):
    total = a.astype(f32)
    for other in others:
        total = total + other.astype(f32)
    return total.astype(bf16)


def scatter_stages(part, ring, pair):
    away = part(2, 1)
    half = halfway(away.shape[0])
    away, from_after, from_before = yield (
        moved(away, ring, pair, 0, 1),
        moved(part(-1, 1), ring, pair, -1, 0),
        moved(part(1, 1), ring, pair, 1, 0),
    )
    away = add(part(2, 0), away)
    away_first, away_second, got_across = yield (
        moved(away[:half], ring, pair, -1, 0),
        moved(away[half:], ring, pair, 1, 0),
        moved(add(part(0, 1), from_after, from_before), ring, pair, 0, 1),
    )
    back, ahead = part(-1, 0), part(1, 0)
    back = jnp.concatenate([add(back[:half], away_first), back[half:]], axis=0)
    ahead = jnp.concatenate([ahead[:half], add(ahead[half:], away_second)], axis=0)
    got = yield moved(back, ring, pair, -1, 0), moved(ahead, ring, pair, 1, 0)
    yield part(0, 0), got_across, *got


def scattered(part, ring, pair):
    stages = scatter_stages(part, ring, pair)
    state = next(stages)
    for _ in range(3):
        state = stages.send(state)
    return state


ORDER = [(0, 0), (0, 1), (-1, 0), (1, 0), (-1, 1), (1, 1), (2, 0), (2, 1)]


def rows_part(array):
    def part(step, flip):
        at = place("y", "xl", True, step, flip)
        return lax.dynamic_slice_in_dim(array, at * 128, 128, 0)

    return part


def ordered_part(near, far):
    def part(step, flip):
        i = ORDER.index((step, flip))
        return (near, far)[i // 4][i % 4 * 128 : (i % 4 + 1) * 128]

    return part


def tied(*values):
    return lax.optimization_barrier(values)


def call(
    kernel,
    out,
    grid,
    ins,
    outs,
    scalars=(),
    scratch=(),
    aliases=None,
    mib=16,
    flops=0,
    bytes_accessed=0,
    exps=0,
):
    return pl.pallas_call(
        kernel,
        grid_spec=pltpu.PrefetchScalarGridSpec(
            num_scalar_prefetch=len(scalars),
            grid=grid,
            in_specs=[spec for _, spec in ins],
            out_specs=outs,
            scratch_shapes=scratch,
        ),
        out_shape=out,
        input_output_aliases=aliases or {},
        compiler_params=pltpu.CompilerParams(vmem_limit_bytes=mib * 1024 * 1024),
        cost_estimate=pl.CostEstimate(
            flops=flops, bytes_accessed=bytes_accessed, transcendentals=exps
        ),
    )(*scalars, *[array for array, _ in ins])


def fixed(*shape):
    return pl.BlockSpec(shape, lambda *_: (0,) * len(shape))


def shaped(shape, dtype):
    return jax.ShapeDtypeStruct(shape, dtype)


def exchanged(blocks, axes):
    return lax.all_to_all(blocks, axes, 0, 0, tiled=True)


def swap_core(block):
    return lax.ppermute(block, "core", [(0, 1), (1, 0)])


def summed(pieces):
    return jnp.sum(pieces.astype(f32), axis=0)


def mm(a, b):
    return jnp.dot(a, b, preferred_element_type=f32)


def mm_nt(a, b):
    return jnp.einsum("ik,jk->ij", a, b, preferred_element_type=f32)


def mm_tn(a, b):
    return jnp.einsum("ki,kj->ij", a, b, preferred_element_type=f32)


def shards(
    hidden_in, block_order, attn_gain, w_qkv, b_qkv, w_out, mlp_gain, w_gate_up, w_down, cotangent
):
    yi, qi = lax.axis_index("y"), lax.axis_index("xl")
    ci = 2 * yi + qi
    fi = lax.axis_index(FSDP)
    core = lax.axis_index("core")
    group = yi // 2
    half = qi.astype(jnp.int32)[None]
    x_own, cot_own = hidden_in[0], cotangent[0]

    heads = [3 * yi + 2 * qi, 3 * yi + 1, H + group, H + KVH + group]
    vectors = [jnp.pad(attn_gain, (0, 32)), jnp.pad(mlp_gain, (0, 32)), b_qkv]
    packed = packed_columns(heads, w_qkv, vectors)

    order = block_order[0]
    positions = (order[:, None] * 64 + jnp.arange(64, dtype=jnp.int32)[None, :]).reshape(1024)
    frequency = jnp.exp(jnp.arange(0, HD, 2, dtype=f32) * (-math.log(rope_base) / HD))
    angles = positions.astype(f32)[:, None] * frequency[None, :]
    cosine, sine = jnp.cos(angles), jnp.sin(angles)
    cosine = jnp.concatenate([cosine, cosine], axis=1)
    sine = jnp.concatenate([-sine, sine], axis=1)
    pos_col, pos_row = positions[:, None], positions[None, :]

    def both_sides(block):
        return jnp.stack([block, lax.ppermute(block, "xh", [(0, 1), (1, 0)])])

    def along_z(sides):
        return exchanged(jnp.broadcast_to(sides, (4,) + sides.shape), ("z",))

    packed = both_sides(packed)
    w_out = both_sides(w_out)
    x_gather = gather_stages(jnp.concatenate([x_own, cot_own], axis=1), "y", "xl", True)
    *x_state, packed, w_out, w_down, w_gate_up_later, cosine, sine = tied(
        *next(x_gather), packed, w_out, w_down, w_gate_up, cosine, sine
    )
    own = along_z(packed)
    *x_state, own, w_out = tied(*x_gather.send(x_state), own, w_out)
    own_out = along_z(w_out)
    x_got = x_gather.send(x_gather.send(x_state))

    down = lax.dynamic_slice_in_dim(w_down, PART * ci, PART, 0)
    down = folded(jnp.concatenate([down, jnp.zeros((2, D), bf16)], axis=0))
    ffn_own = jnp.concatenate([picked(ci, w_gate_up_later), down], axis=1)
    w_ffn = lax.all_gather(ffn_own, FSDP, axis=0, tiled=True)

    att_mine, queries, lse, keys, values, normed_all, w_mine, gains, x_all = attend(
        x_got, own, core, qi, heads, cosine, sine, pos_col, pos_row
    )
    att_gather = gather_stages(att_mine, "y", "xl")
    *att_state, own_out = tied(*next(att_gather), own_out)
    att_got = att_gather.send(att_gather.send(att_gather.send(att_state)))
    attended_all, nm_all, middle, inv_second, w_out_all = to_middle(
        att_got, own_out, core, lax.axis_index("xh"), x_all, gains
    )
    cot_all = placed(x_got)

    w_dn = down_weights(w_ffn)
    hidden_far, gate_far, up_far, hn_far = feed_forward(nm_all, cot_all, w_ffn, w_dn, 1)
    hidden_near, gate_near, up_near, hn_near = feed_forward(nm_all, cot_all, w_ffn, w_dn, 0)
    hn_stages = scatter_stages(ordered_part(hn_near, hn_far), "y", "xl")
    *state, cot_all, hidden_near, hidden_far = tied(
        *next(hn_stages), cot_all, hidden_near, hidden_far
    )
    ffn_parts = down_product(cot_all, (hidden_near, hidden_far))
    *state, nm_all, gate_near, gate_far, up_near, up_far = tied(
        *hn_stages.send(state), nm_all, gate_near, gate_far, up_near, up_far
    )
    ffn_parts = gate_up_product(nm_all, (gate_near, gate_far), (up_near, up_far), ffn_parts)
    hn_parts = hn_stages.send(hn_stages.send(state))
    ffn_sides = lax.psum_scatter(ffn_parts, ("z", "core"), scatter_dimension=0, tiled=True)[0]
    grad_middle, send = middle_back(hn_parts, middle, inv_second, gains, cot_own, w_out_all)
    got = exchanged(send, CTX)
    gp_mine, columns = attend_back(
        half, got, queries, lse, keys, values, cosine, sine, pos_col, pos_row
    )
    gb_mine = jnp.sum(gp_mine.astype(f32), axis=0).astype(bf16).reshape(4, HD)
    gb_mine = jnp.broadcast_to(jnp.pad(gb_mine, ((0, 92), (0, 0))), (16, 96, HD))
    mine_parts = jnp.concatenate(
        [
            mm_tn(normed_all, gp_mine).astype(bf16).reshape(16, 96, 512),
            mm_tn(attended_all, columns).astype(bf16).reshape(16, 96, 256),
            gb_mine,
        ],
        axis=2,
    )
    pairs = mine_parts.reshape(2, 4, 2, 96, MINE)
    mine_both = add(
        lax.dynamic_index_in_dim(pairs, core, 2, keepdims=False),
        swap_core(lax.dynamic_index_in_dim(pairs, 1 - core, 2, keepdims=False)),
    )
    mine_both, xn_part, out_near, out_far = tied(
        mine_both,
        mm_nt(gp_mine, w_mine).astype(bf16),
        mm(hidden_near, w_dn).astype(bf16),
        mm(hidden_far, w_dn).astype(bf16),
    )
    mine_sides = summed(exchanged(mine_both.transpose(1, 0, 2, 3), ("z",))).astype(bf16)
    xn_of, out_of = rows_part(xn_part), ordered_part(out_near, out_far)
    xn_out = scattered(
        lambda step, flip: jnp.concatenate([xn_of(step, flip), out_of(step, flip)], axis=1),
        "y",
        "xl",
    )
    xn_out = sum(term.astype(f32) for term in xn_out)
    grad_xn = xn_out[:, :D]
    hidden_out = middle + xn_out[:, D:]
    sides = jnp.concatenate([ffn_sides, mine_sides], axis=2)
    side = lax.axis_index("xh")
    weight_sum = add(
        lax.dynamic_index_in_dim(sides, side, 0, keepdims=False),
        lax.ppermute(
            lax.dynamic_index_in_dim(sides, 1 - side, 0, keepdims=False), "xh", [(0, 1), (1, 0)]
        ),
    )
    resid = x_own.astype(f32)
    inv_first = lax.rsqrt(jnp.mean(resid * resid, axis=-1, keepdims=True) + eps)
    scaled = grad_xn * gains[:1]
    grad_in = (
        grad_middle
        + inv_first * scaled
        - resid * (inv_first**3) * jnp.mean(resid * scaled, axis=-1, keepdims=True)
    )

    own_gains = jnp.stack([jnp.pad(g.astype(f32), (0, 32)) for g in (mlp_gain, attn_gain)])
    grad_w_gate_up, grad_w_down, grad_w_qkv, grad_w_out, vectors = weight_gradients(
        gather_eight(weight_sum, "y", "xl"),
        w_gate_up,
        w_qkv,
        jnp.pad(own_gains, ((0, 6), (0, 0)), constant_values=1.0),
        fi,
    )
    grad_mlp_gain, grad_attn_gain, grad_b_qkv = vectors[0, :96], vectors[1, :96], vectors[2]

    return (
        hidden_out[None],
        grad_in[None],
        grad_attn_gain,
        grad_w_qkv,
        grad_b_qkv,
        grad_w_out,
        grad_mlp_gain,
        grad_w_gate_up,
        grad_w_down,
    )


def solution(mesh):
    fine = Mesh(mesh.devices.reshape(4, 2, 2, 4, 2), CTX + FSDP)
    rows = P(FSDP, CTX, None)
    vector = P(FSDP)
    matrix = P(FSDP, None)
    return jax.shard_map(
        shards,
        mesh=fine,
        in_specs=(rows, matrix, vector, matrix, vector, matrix, vector, matrix, matrix, rows),
        out_specs=(rows, rows, vector, matrix, vector, matrix, vector, matrix, matrix),
        check_vma=False,
    )
```

```python
import math

import jax
import jax.numpy as jnp
from jax import lax
from jax.experimental import pallas as pl
from jax.experimental.pallas import tpu as pltpu
from jax.sharding import Mesh, PartitionSpec as P

D = 1536
H = 12
KVH = 2
HD = 128
FF = 8960
PART = FF // 128
WIDE = 1152
MINE = 896

CTX = ("y", "xl")
FSDP = ("xh", "z", "core")

eps = 1e-06
rope_base = 1000000.0
masked_value = -1e30
bf16 = jnp.bfloat16
f32 = jnp.float32


def moved(block, ring, pair, step, flip):
    size = lax.axis_size(ring)
    if step == 0:
        return lax.ppermute(block, pair, [(0, 1), (1, 0)])
    return lax.ppermute(block, ring, [(i, (i + step) % size) for i in range(size)])


def halfway(rows):
    return rows // 32 * 16


def gather_stages(block, ring, pair, by_ring=False):
    half = halfway(block.shape[0])
    across, before, after_ = yield (
        moved(block, ring, pair, 0, 1),
        moved(block, ring, pair, 1, 0),
        moved(block, ring, pair, -1, 0),
    )
    far_first, far_second, across_before, across_after = yield (
        moved(before[:half], ring, pair, 1, 0),
        moved(after_[half:], ring, pair, -1, 0),
        moved(across, ring, pair, 1, 0),
        moved(across, ring, pair, -1, 0),
    )
    if by_ring:
        last = (
            moved(across_before[:half], ring, pair, 1, 0),
            moved(across_after[half:], ring, pair, -1, 0),
        )
    else:
        last = (moved(far_first, ring, pair, 0, 1), moved(far_second, ring, pair, 0, 1))
    across_far_first, across_far_second = yield last
    yield [
        (0, 0, 0, block),
        (0, 1, 0, across),
        (-1, 0, 0, before),
        (1, 0, 0, after_),
        (-1, 1, 0, across_before),
        (1, 1, 0, across_after),
        (2, 0, 0, far_first),
        (2, 0, half, far_second),
        (2, 1, 0, across_far_first),
        (2, 1, half, across_far_second),
    ]


def in_step(*gathers):
    states = [next(g) for g in gathers]
    for _ in range(3):
        if len(gathers) > 1:
            states = lax.optimization_barrier(states)
        states = [g.send(state) for g, state in zip(gathers, states)]
    return states


def gather_eight(block, ring, pair):
    return in_step(gather_stages(block, ring, pair))[0]


def place(ring, pair, ring_major, step, flip):
    size = lax.axis_size(ring)
    r = (lax.axis_index(ring) + step) % size
    q = lax.axis_index(pair)
    q = 1 - q if flip else q
    return r * 2 + q if ring_major else q * size + r


def places_of(got, ring, pair, ring_major):
    return [place(ring, pair, ring_major, step, flip) for step, flip, _, _ in got]


def pick_kernel(at_ref, weights, out):
    for c in range(8):

        @pl.when(at_ref[0] == c)
        def _():
            for part in range(2):
                for s in range(16):
                    start, to = part * FF + 560 * s + PART * c, part * WIDE + 72 * s
                    out[:, to : to + PART] = weights[:, start : start + PART]
                    out[:, to + PART : to + 72] = jnp.zeros((96, 2), bf16)


def picked(slice_index, weights):
    return call(
        pick_kernel,
        shaped((96, 2 * WIDE), bf16),
        (1,),
        [(weights, fixed(96, 2 * FF))],
        fixed(96, 2 * WIDE),
        mib=12,
        scalars=(slice_index.astype(jnp.int32)[None],),
        bytes_accessed=4 * 1024 * 1024,
    )


def folded(rows):
    rest = rows[:, WIDE:]
    rest = jnp.concatenate([rest[24 * k : 24 * (k + 1)] for k in range(3)], axis=1)
    return jnp.concatenate([rows[:, :WIDE], rest], axis=0)


def unfolded(rows):
    rest = jnp.concatenate([rows[72:, 384 * k : 384 * (k + 1)] for k in range(3)], axis=0)
    return jnp.concatenate([rows[:72], rest], axis=1)


def unfold_kernel(weights, out):
    out[0] = unfolded(weights[...].astype(f32)).astype(bf16)


def down_weights(w_ffn):
    return call(
        unfold_kernel,
        shaped((16, 72, D), bf16),
        (16,),
        [(w_ffn, pl.BlockSpec((96, WIDE), lambda s: (s, 2)))],
        pl.BlockSpec((1, 72, D), lambda s: (s, 0, 0)),
        bytes_accessed=8 * 1024 * 1024,
    ).reshape(WIDE, D)


def last_kernel(at_ref, *refs):
    pieces, weights, weights_qkv, gains = refs[:10], *refs[10:13]
    out, out_qkv, out_out, vectors, blocks, sums, bias = refs[13:]
    step = pl.program_id(0)
    for i in range(6):
        blocks[at_ref[i]] = pieces[i][...]
    for i in (6, 8):
        blocks[at_ref[i]] = jnp.where(step < 3, pieces[i][...], pieces[i + 1][...])
    total = jnp.zeros((16, 1), f32)
    for part in range(2):
        for s in range(16):
            start = part * WIDE + 72 * s
            row = jnp.concatenate(
                [blocks[c, :, start : start + PART] for c in range(8)], axis=1
            )
            out[:, part * FF + 560 * s : part * FF + 560 * (s + 1)] = row.astype(f32)
    for at in range(0, 2 * FF, 1792):
        lanes = slice(at, at + 1792)
        total = total + jnp.sum(
            out[:, lanes] * weights[:, lanes].astype(f32), axis=1, keepdims=True
        )
    rows = pl.ds(pl.multiple_of(step * 16, 16), 16)
    sums[0, rows] = jnp.broadcast_to(total, (16, HD))

    def whole(c, at, rows=slice(0, 16)):
        start = 3 * WIDE + at * HD
        return blocks[c, rows, start : start + HD].astype(f32)

    def heads(term):
        for y in range(4):
            yield 3 * y, term(2 * y, 0)
            yield 3 * y + 1, term(2 * y, 1) + term(2 * y + 1, 1)
            yield 3 * y + 2, term(2 * y + 1, 0)
        for kind in range(2):
            for group in range(2):
                yield 12 + 2 * kind + group, sum(term(4 * group + i, 2 + kind) for i in range(4))

    total = jnp.zeros((16, 1), f32)
    for h, value in heads(whole):
        lanes = slice(h * HD, (h + 1) * HD)
        out_qkv[:, lanes] = value
        total = total + jnp.sum(
            value * weights_qkv[:, lanes].astype(f32), axis=1, keepdims=True
        )
    sums[1, rows] = jnp.broadcast_to(total, (16, HD))
    for y in range(4):
        at = 3 * y * HD
        out_out[:, at : at + HD] = whole(2 * y, 4)
        out_out[:, at + HD : at + 2 * HD] = whole(2 * y, 5) + whole(2 * y + 1, 5)
        out_out[:, at + 2 * HD : at + 3 * HD] = whole(2 * y + 1, 4)

    @pl.when(step == 0)
    def _():
        for h, value in heads(lambda c, kind: whole(c, 6)[kind : kind + 1]):
            bias[h : h + 1] = value

    @pl.when(step == 5)
    def _():
        vectors[...] = jnp.zeros_like(vectors)
        for i in range(2):
            vectors[i : i + 1, :96] = sums[i].T[:1, :96] / gains[i : i + 1, :96]
        vectors[2:3] = bias[pl.ds(at_ref[10], 1)]


def last_down_kernel(at_ref, *refs):
    pieces, out, blocks = refs[:10], refs[10], refs[11]
    for i in range(6):
        blocks[at_ref[i]] = pieces[i][...].astype(f32)
    for i in (6, 8):
        blocks[at_ref[i], :48] = pieces[i][...].astype(f32)
        blocks[at_ref[i], 48:] = pieces[i + 1][...].astype(f32)
    for c in range(8):
        out[PART * c : PART * (c + 1)] = unfolded(blocks[c])[:PART]


def weight_gradients(got, weights, weights_qkv, gains, head):
    pieces = [g[3] for g in got]
    places = jnp.stack([*places_of(got, "y", "xl", True), head]).astype(jnp.int32)
    width = 3 * WIDE + MINE

    def rows(i, at):
        return i, 0

    maps = [rows] * 6 + [
        lambda i, at: (jnp.minimum(i, 2), 0),
        lambda i, at: (jnp.maximum(i - 3, 0), 0),
    ] * 2
    w_gate_up, w_qkv, w_out, vectors = call(
        last_kernel,
        [
            shaped((96, 2 * FF), f32),
            shaped((96, 2048), f32),
            shaped((96, D), f32),
            shaped((8, HD), f32),
        ],
        (6,),
        [(p, pl.BlockSpec((16, width), m)) for p, m in zip(pieces, maps)]
        + [
            (weights, pl.BlockSpec((16, 2 * FF), rows)),
            (weights_qkv, pl.BlockSpec((16, 2048), rows)),
            (gains, fixed(8, HD)),
        ],
        [
            pl.BlockSpec((16, 2 * FF), rows),
            pl.BlockSpec((16, 2048), rows),
            pl.BlockSpec((16, D), rows),
            fixed(8, HD),
        ],
        scalars=(places,),
        scratch=[
            pltpu.VMEM((8, 16, width), bf16),
            pltpu.VMEM((2, 96, HD), f32),
            pltpu.VMEM((16, HD), f32),
        ],
        mib=24,
        bytes_accessed=96 * 2 * FF * 8,
    )
    w_down = call(
        last_down_kernel,
        shaped((560, D), f32),
        (1,),
        [(p, pl.BlockSpec((p.shape[0], WIDE), lambda i, at: (0, 2))) for p in pieces],
        fixed(560, D),
        scalars=(places,),
        scratch=[pltpu.VMEM((8, 96, WIDE), f32)],
        mib=24,
        bytes_accessed=6 * 1024 * 1024,
    )
    return w_gate_up, w_down, w_qkv, w_out, vectors


def mine_kernel(at, normed, attended, grads, columns, given, kept):
    core = at[0]
    left = tn(normed[...], grads[...])
    right = tn(attended[...], columns[...])
    sums = jnp.sum(grads[...].astype(f32), axis=0, keepdims=True)
    bias = jnp.concatenate(
        [sums[:, i * HD : (i + 1) * HD] for i in range(4)] + [jnp.zeros((92, HD), f32)], axis=0
    )
    total = jnp.concatenate([left, right], axis=1).astype(bf16)
    bias = bias.astype(bf16)
    for p in range(2):
        even = total[192 * p : 192 * p + 96]
        odd = total[192 * p + 96 : 192 * (p + 1)]
        kept[p, 0, :, :768] = jnp.where(core == 0, even, odd)
        given[p, 0, :, :768] = jnp.where(core == 0, odd, even)
        kept[p, 0, :, 768:] = bias
        given[p, 0, :, 768:] = bias


def attention_products(core, normed, attended, grads, columns):
    out = pl.BlockSpec((2, 1, 96, MINE), lambda g, at: (g % 2, g // 2, 0, 0))
    return call(
        mine_kernel,
        [shaped((4, 2, 96, MINE), bf16)] * 2,
        (4,),
        [
            (normed, pl.BlockSpec((1024, 384), lambda g, at: (0, g))),
            (attended, pl.BlockSpec((1024, 384), lambda g, at: (0, g))),
            (grads, fixed(1024, 512)),
            (columns, fixed(1024, 256)),
        ],
        [out, out],
        scalars=(core.astype(jnp.int32)[None],),
        mib=24,
        flops=2 * 1024 * D * 768,
        bytes_accessed=10 * 1024 * 1024,
    )


def pack_kernel(at, weights, vectors, out):
    for i in range(4):
        out[:, i * HD : (i + 1) * HD] = weights[:, pl.ds(pl.multiple_of(at[i] * HD, HD), HD)]
    out[:, 4 * HD :] = jnp.concatenate([vectors[...], jnp.zeros((80, HD), bf16)], axis=0)


def packed_columns(heads, weights, vectors):
    rows = jnp.concatenate([jnp.stack(vectors), jnp.zeros((13, HD), bf16)], axis=0)
    return call(
        pack_kernel,
        shaped((96, 640), bf16),
        (1,),
        [(weights, fixed(96, 2048)), (rows, fixed(16, HD))],
        fixed(96, 640),
        scalars=(jnp.stack(heads).astype(jnp.int32),),
        bytes_accessed=2 * 1024 * 1024,
    )


def turned(field, cos_ref, sin_ref):
    return field * cos_ref + pltpu.roll(field, HD // 2, 1) * sin_ref


def nt(a, b):
    return lax.dot_general(a, b, (((1,), (1,)), ((), ())), preferred_element_type=f32)


def tn(a, b):
    return lax.dot_general(a, b, (((0,), (0,)), ((), ())), preferred_element_type=f32)


SCALE = 1.0 / math.sqrt(HD)


def attend_kernel(*refs):
    at, pieces, own, other, cos, sin, pos_col, pos_row = refs[0], refs[1:11], *refs[11:17]
    att, queries, lse, keys, values, normed, weights, gains, x, woven, proj = refs[17:]
    c, core, half = pl.program_id(0), at[10], at[11]

    @pl.when(c == 0)
    def _():
        for i, piece in enumerate(pieces):
            first = 64 if i in (7, 9) else 0
            x[at[i], first : first + piece.shape[0]] = piece[...]
        for i in range(8):
            index = 4 * (at[16] if i % 2 == 0 else 1 - at[16]) + i // 2
            woven[index, core] = own[i]
            woven[index, 1 - core] = other[i]
        gains[...] = jnp.zeros_like(gains)
        for s in range(16):
            weights[96 * s : 96 * (s + 1)] = woven[s // 2, s % 2, :, :512]
            rows = woven[s // 2, s % 2, :16, 512:].astype(f32)
            gains[0:2, 96 * s : 96 * (s + 1)] = rows[0:2, :96]
        bias = jnp.concatenate(
            [
                woven[at[12 + i] // 2, at[12 + i] % 2, :16, 512:].astype(f32)[2:3]
                for i in range(4)
            ],
            axis=1,
        )
        for i in range(8):
            rows = x[i].astype(f32)
            inv = lax.rsqrt(jnp.mean(rows * rows, axis=1, keepdims=True) + eps)
            normed[128 * i : 128 * (i + 1)] = (rows * inv * gains[0:1]).astype(bf16)
        proj[...] = jnp.dot(normed[...], weights[...], preferred_element_type=f32) + bias
        keys[...] = turned(proj[:, 2 * HD : 3 * HD], cos[...], sin[...]).astype(bf16)
        values[...] = proj[:, 3 * HD :].astype(bf16)

    rows = pl.ds(pl.multiple_of(c * 128, 128), 128)
    part = pl.ds(pl.multiple_of(c * 128 + half * 64, 64), 64)
    query = jnp.concatenate(
        [
            turned(proj[rows, :HD], cos[rows], sin[rows]),
            turned(proj[part, HD : 2 * HD], cos[part], sin[part]),
        ],
        axis=0,
    ).astype(bf16)
    queries[...] = query
    scores = nt(query, keys[...]) * SCALE
    seen = jnp.concatenate([pos_col[rows], pos_col[part]], axis=0) >= pos_row[...]
    scores = jnp.where(seen, scores, masked_value)
    row_max = jnp.max(scores, axis=1, keepdims=True)
    exponent = jnp.exp(scores - row_max)
    total = jnp.sum(exponent, axis=1, keepdims=True)
    probability = (exponent / total).astype(bf16)
    att[...] = jnp.dot(probability, values[...], preferred_element_type=f32).astype(bf16)
    lse[...] = jnp.broadcast_to(row_max + jnp.log(total), (192, HD))


def attend(x_got, own, core, half, heads, cos, sin, pos_col, pos_row):
    block = pl.BlockSpec((192, HD), lambda c, at: (c, 0))
    at = [*places_of(x_got, "y", "xl", True), core, half, *heads, lax.axis_index("xh")]
    at = jnp.stack(at).astype(jnp.int32)
    own = own.reshape(8, 96, 640)
    return call(
        attend_kernel,
        [
            shaped((1536, HD), bf16),
            shaped((1536, HD), bf16),
            shaped((1536, HD), f32),
            shaped((1024, HD), bf16),
            shaped((1024, HD), bf16),
            shaped((1024, D), bf16),
            shaped((D, 512), bf16),
            shaped((8, D), f32),
            shaped((8, 128, D), bf16),
        ],
        (8,),
        [(g[3], fixed(g[3].shape[0], D)) for g in x_got]
        + [
            (own, fixed(8, 96, 640)),
            (swap_core(own), fixed(8, 96, 640)),
            (cos, fixed(1024, HD)),
            (sin, fixed(1024, HD)),
            (pos_col, fixed(1024, 1)),
            (pos_row, fixed(1, 1024)),
        ],
        [
            block,
            block,
            block,
            fixed(1024, HD),
            fixed(1024, HD),
            fixed(1024, D),
            fixed(D, 512),
            fixed(8, D),
            fixed(8, 128, D),
        ],
        scalars=(at,),
        scratch=[
            pltpu.VMEM((8, 2, 96, 640), bf16),
            pltpu.VMEM((1024, 512), f32),
        ],
        mib=40,
        flops=4 * 1536 * 1024 * HD + 2 * 1024 * D * 512,
        bytes_accessed=14 * 1024 * 1024,
        exps=1536 * 1024,
    )


def attend_back_kernel(
    half_ref, got, queries, lse, keys, values, cos, sin, pos_col, pos_row, grads, columns, gk, gv
):
    c, half = pl.program_id(0), half_ref[0]

    @pl.when(c == 0)
    def _():
        gk[...] = jnp.zeros_like(gk)
        gv[...] = jnp.zeros_like(gv)

    rows = pl.ds(pl.multiple_of(c * 128, 128), 128)
    part = pl.ds(pl.multiple_of(c * 128 + half * 64, 64), 64)
    rest = pl.ds(pl.multiple_of(c * 128 + (1 - half) * 64, 64), 64)
    out = got[0, :192]
    query = queries[...]
    scores = nt(query, keys[...]) * SCALE
    seen = jnp.concatenate([pos_col[rows], pos_col[part]], axis=0) >= pos_row[...]
    scores = jnp.where(seen, scores, masked_value)
    probs = jnp.exp(scores - lse[:, :1])
    grad_prob = nt(out, values[...])
    inner = jnp.sum(probs * grad_prob, axis=1, keepdims=True)
    grad_scores = (probs * (grad_prob - inner)).astype(bf16)
    grad_query = jnp.dot(grad_scores, keys[...], preferred_element_type=f32) * SCALE
    gk[...] += tn(grad_scores, query)
    gv[...] += tn(probs.astype(bf16), out)
    grads[rows, :HD] = turned(grad_query[:128], cos[rows], -sin[rows]).astype(bf16)
    grads[part, HD : 2 * HD] = turned(grad_query[128:], cos[part], -sin[part]).astype(bf16)
    grads[rest, HD : 2 * HD] = jnp.zeros((64, HD), bf16)
    columns[:, :HD] = got[0, 192:320]
    columns[pl.ds(pl.multiple_of(half * 64, 64), 64), HD:] = got[0, 320:]
    columns[pl.ds(pl.multiple_of((1 - half) * 64, 64), 64), HD:] = jnp.zeros((64, HD), bf16)

    @pl.when(c == 7)
    def _():
        grads[:, 2 * HD : 3 * HD] = turned(gk[...] * SCALE, cos[...], -sin[...]).astype(bf16)
        grads[:, 3 * HD :] = gv[...].astype(bf16)


def attend_back(half, got, queries, lse, keys, values, cos, sin, pos_col, pos_row):
    block = pl.BlockSpec((192, HD), lambda c, half: (c, 0))
    return call(
        attend_back_kernel,
        [shaped((1024, 4 * HD), bf16), shaped((1024, 2 * HD), bf16)],
        (8,),
        [
            (got, pl.BlockSpec((1, 384, HD), lambda c, half: (c, 0, 0))),
            (queries, block),
            (lse, block),
            (keys, fixed(1024, HD)),
            (values, fixed(1024, HD)),
            (cos, fixed(1024, HD)),
            (sin, fixed(1024, HD)),
            (pos_col, fixed(1024, 1)),
            (pos_row, fixed(1, 1024)),
        ],
        [fixed(1024, 4 * HD), pl.BlockSpec((128, 2 * HD), lambda c, half: (c, 0))],
        scalars=(half,),
        scratch=[pltpu.VMEM((1024, HD), f32), pltpu.VMEM((1024, HD), f32)],
        mib=50,
        flops=10 * 1536 * 1024 * HD,
        bytes_accessed=6 * 1024 * 1024,
        exps=1536 * 1024,
    )


def place_kernel(*refs):
    pieces, out = refs[:10], refs[10]
    for i, piece in enumerate(pieces):
        at = 128 * (i if i < 6 else 6 + (i - 6) // 2) + (64 if i in (7, 9) else 0)
        out[at : at + piece.shape[0]] = piece[...]


def placed(got):
    return call(
        place_kernel,
        shaped((1024, D), bf16),
        (1,),
        [(g[3], pl.BlockSpec((g[3].shape[0], D), lambda i: (0, 1))) for g in got],
        fixed(1024, D),
        bytes_accessed=4 * 1024 * D,
    )


def middle_kernel(at, *refs):
    pieces, own, other, x, gains = refs[:10], *refs[10:14]
    attended, normed, middle, inverse, w_out, heads = refs[14:]
    step, core, side = pl.program_id(0), at[10], at[11]

    @pl.when(step == 0)
    def _():
        for i in range(8):
            index = 2 * (4 * (side if i % 2 == 0 else 1 - side) + i // 2)
            w_out[index + core] = own[i]
            w_out[index + 1 - core] = other[i]
        for i, piece in enumerate(pieces):
            first = 768 if i in (7, 9) else 0
            heads[at[i], first : first + piece.shape[0]] = piece[...]

    block = at[12 + step]
    rows = pl.ds(pl.multiple_of(block * 192, 64), 128)
    part = pl.ds(pl.multiple_of(block * 192 + 128, 64), 64)
    for y in range(4):
        for q in range(2):
            whole, split = HD * (3 * y + 2 * q), HD * (3 * y + 1)
            attended[:, whole : whole + HD] = heads[2 * y + q, rows]
            attended[64 * q : 64 * (q + 1), split : split + HD] = heads[2 * y + q, part]
    weights = w_out[...].reshape(D, D)
    mid = x[0].astype(f32) + jnp.dot(attended[...], weights, preferred_element_type=f32)
    inv = lax.rsqrt(jnp.mean(mid * mid, axis=1, keepdims=True) + eps)
    normed[...] = (mid * inv * gains[1:2]).astype(bf16)

    @pl.when(step == 0)
    def _():
        middle[...] = mid
        inverse[...] = jnp.broadcast_to(inv, (128, HD))


def to_middle(got, own, core, side, x, gains):
    own = own.reshape(8, 96, D)
    order = [place("y", "xl", True, step, flip) for step, flip in ORDER]
    *outs, w_out = call(
        middle_kernel,
        [
            shaped((1024, D), bf16),
            shaped((1024, D), bf16),
            shaped((128, D), f32),
            shaped((128, HD), f32),
            shaped((16, 96, D), bf16),
        ],
        (8,),
        [(g[3], fixed(*g[3].shape)) for g in got]
        + [
            (own, fixed(8, 96, D)),
            (swap_core(own), fixed(8, 96, D)),
            (x, pl.BlockSpec((1, 128, D), lambda b, at: (at[12 + b], 0, 0))),
            (gains, fixed(8, D)),
        ],
        [
            pl.BlockSpec((128, D), lambda b, at: (at[12 + b], 0)),
            pl.BlockSpec((128, D), lambda b, at: (b, 0)),
            fixed(128, D),
            fixed(128, HD),
            fixed(16, 96, D),
        ],
        scalars=(
            jnp.stack([*places_of(got, "y", "xl", True), core, side, *order]).astype(jnp.int32),
        ),
        scratch=[pltpu.VMEM((8, 1536, HD), bf16)],
        mib=40,
        flops=2 * 1024 * D * D,
        bytes_accessed=20 * 1024 * 1024,
    )
    return *outs, w_out.reshape(D, D)


def middle_back_kernel(a, b, c, d, middle, inverse, gain, cot, w_out, grad_middle, send):
    grad_hn = a[...].astype(f32) + b[...].astype(f32) + c[...].astype(f32) + d[...].astype(f32)
    inv, mid = inverse[:, :1], middle[...]
    scaled = grad_hn * gain[1:2]
    inner = jnp.mean(mid * scaled, axis=1, keepdims=True)
    grad = cot[...].astype(f32) + inv * scaled - mid * (inv * inv * inv * inner)
    grad_middle[...] = grad
    grad_attn = grad.astype(bf16)
    heads = nt(grad_attn, w_out[...]).astype(bf16)
    for y in range(4):
        for q in range(2):
            whole, split = HD * (3 * y + 2 * q), HD * (3 * y + 1)
            half = slice(64 * q, 64 * (q + 1))
            send[2 * y + q, :128] = heads[:, whole : whole + HD]
            send[2 * y + q, 128:192] = heads[half, split : split + HD]
            send[2 * y + q, 192:320] = grad_attn[:, whole : whole + HD]
            send[2 * y + q, 320:] = grad_attn[half, split : split + HD]


def middle_back(parts, middle, inverse, gain, cot, w_out):
    row = fixed(128, D)
    return call(
        middle_back_kernel,
        [shaped((128, D), f32), shaped((8, 384, HD), bf16)],
        (1,),
        [(p, row) for p in parts]
        + [
            (middle, row),
            (inverse, fixed(128, HD)),
            (gain, fixed(8, D)),
            (cot, row),
            (w_out, fixed(D, D)),
        ],
        [row, fixed(8, 384, HD)],
        mib=50,
        flops=2 * 128 * D * D,
        bytes_accessed=10 * 1024 * 1024,
    )


def down_product_kernel(*refs):
    hidden, cot, out, total = refs[:2], refs[2:4], refs[4], refs[5]
    step = pl.program_id(0)
    product = tn(hidden[0][...], cot[0][...]) + tn(hidden[1][...], cot[1][...])

    for k in range(3):

        @pl.when(step == k)
        def _():
            for s in range(16):
                total[s, :72, 384 * k : 384 * (k + 1)] = product[72 * s : 72 * (s + 1)]

    @pl.when(step == 3)
    def _():
        for s in range(16):
            for k in range(3):
                total[s, 72:, 384 * k : 384 * (k + 1)] = product[
                    72 * s + 24 * k : 72 * s + 24 * (k + 1)
                ]
        for s in range(16):
            out[s % 8, s // 8] = total[s].astype(bf16)


def gate_up_product_kernel(*refs):
    nm, rhs, out = refs[:2], refs[2:6], refs[7]

    def work(right):
        total = tn(nm[0][...], right[0][...]) + tn(nm[1][...], right[1][...])
        for i in range(4):
            out[i, 0] = total[96 * i : 96 * (i + 1)].astype(bf16)

    for j in range(2):
        pl.when(pl.program_id(0) == j)(lambda j=j: work(rhs[2 * j : 2 * j + 2]))


def down_product(cot, hidden):
    return call(
        down_product_kernel,
        shaped((8, 2, 96, 3 * WIDE), bf16),
        (4,),
        [(a, fixed(512, WIDE)) for a in hidden]
        + [
            (cot, pl.BlockSpec((512, 384), lambda t: (0, t))),
            (cot, pl.BlockSpec((512, 384), lambda t: (1, t))),
        ],
        pl.BlockSpec((8, 2, 96, WIDE), lambda t: (0, 0, 0, 2)),
        scratch=[pltpu.VMEM((16, 96, WIDE), f32)],
        mib=56,
        flops=2 * 1024 * D * WIDE,
        bytes_accessed=10 * 1024 * 1024,
    )


def gate_up_product(nm, gate, up, parts):
    return call(
        gate_up_product_kernel,
        shaped((8, 2, 96, 3 * WIDE), bf16),
        (2, 4),
        [
            (nm, pl.BlockSpec((512, 384), lambda j, g: (0, g))),
            (nm, pl.BlockSpec((512, 384), lambda j, g: (1, g))),
        ]
        + [(a, fixed(512, WIDE)) for pair in (gate, up) for a in pair]
        + [(parts, pl.BlockSpec(memory_space=pl.ANY))],
        pl.BlockSpec((4, 1, 96, WIDE), lambda j, g: (g % 2, g // 2, 0, j)),
        aliases={6: 0},
        mib=56,
        flops=2 * 1024 * D * 2 * WIDE,
        bytes_accessed=20 * 1024 * 1024,
    )


def feed_forward_kernel(
    nm, cot, w_gate, w_up, w_dn, hidden, grad_gate, grad_up, hn, total
):
    step = pl.program_id(0)
    gate = jnp.dot(nm[...], w_gate[...], preferred_element_type=f32)
    up = jnp.dot(nm[...], w_up[...], preferred_element_type=f32)
    act = nt(cot[...], w_dn[...])
    sigmoid_gate = jax.nn.sigmoid(gate)
    silu_gate = gate * sigmoid_gate
    hidden[...] = (silu_gate * up).astype(bf16)
    to_gate = (act * up * (sigmoid_gate * (1.0 + gate * (1.0 - sigmoid_gate)))).astype(bf16)
    to_up = (act * silu_gate).astype(bf16)
    grad_gate[...] = to_gate
    grad_up[...] = to_up
    term = nt(to_gate, w_gate[...]) + nt(to_up, w_up[...])

    @pl.when(step == 0)
    def _():
        total[...] = term

    @pl.when(step > 0)
    def _():
        total[...] += term

    @pl.when(step == 2)
    def _():
        hn[...] = total[...].astype(bf16)


def feed_forward(nm, cot, w_ffn, w_dn, half):
    whole, column = fixed(512, D), pl.BlockSpec((512, 384), lambda j: (0, j))
    narrow = shaped((512, WIDE), bf16)
    rows = pl.BlockSpec((512, D), lambda j: (half, 0))
    return call(
        feed_forward_kernel,
        [narrow, narrow, narrow, shaped((512, D), bf16)],
        (3,),
        [
            (nm, rows),
            (cot, rows),
            (w_ffn, pl.BlockSpec((D, 384), lambda j: (0, j))),
            (w_ffn, pl.BlockSpec((D, 384), lambda j: (0, 3 + j))),
            (w_dn, pl.BlockSpec((384, D), lambda j: (j, 0))),
        ],
        [column, column, column, whole],
        scratch=[pltpu.VMEM((512, D), f32)],
        mib=36,
        flops=2 * 512 * D * 5 * WIDE,
        bytes_accessed=20 * 1024 * 1024,
        exps=512 * WIDE,
    )


def add(a, *others):
    total = a.astype(f32)
    for other in others:
        total = total + other.astype(f32)
    return total.astype(bf16)


def scatter_stages(part, ring, pair):
    away = part(2, 1)
    half = halfway(away.shape[0])
    away, from_after, from_before = yield (
        moved(away, ring, pair, 0, 1),
        moved(part(-1, 1), ring, pair, -1, 0),
        moved(part(1, 1), ring, pair, 1, 0),
    )
    away = add(part(2, 0), away)
    away_first, away_second, got_across = yield (
        moved(away[:half], ring, pair, -1, 0),
        moved(away[half:], ring, pair, 1, 0),
        moved(add(part(0, 1), from_after, from_before), ring, pair, 0, 1),
    )
    back, ahead = part(-1, 0), part(1, 0)
    back = jnp.concatenate([add(back[:half], away_first), back[half:]], axis=0)
    ahead = jnp.concatenate([ahead[:half], add(ahead[half:], away_second)], axis=0)
    got = yield moved(back, ring, pair, -1, 0), moved(ahead, ring, pair, 1, 0)
    yield part(0, 0), got_across, *got


def scattered(part, ring, pair):
    stages = scatter_stages(part, ring, pair)
    state = next(stages)
    for _ in range(3):
        state = stages.send(state)
    return state


ORDER = [(0, 0), (0, 1), (-1, 0), (1, 0), (-1, 1), (1, 1), (2, 0), (2, 1)]


def rows_part(array):
    def part(step, flip):
        at = place("y", "xl", True, step, flip)
        return lax.dynamic_slice_in_dim(array, at * 128, 128, 0)

    return part


def ordered_part(near, far):
    def part(step, flip):
        i = ORDER.index((step, flip))
        return (near, far)[i // 4][i % 4 * 128 : (i % 4 + 1) * 128]

    return part


def tied(*values):
    return lax.optimization_barrier(values)


def call(
    kernel,
    out,
    grid,
    ins,
    outs,
    scalars=(),
    scratch=(),
    aliases=None,
    mib=16,
    flops=0,
    bytes_accessed=0,
    exps=0,
):
    return pl.pallas_call(
        kernel,
        grid_spec=pltpu.PrefetchScalarGridSpec(
            num_scalar_prefetch=len(scalars),
            grid=grid,
            in_specs=[spec for _, spec in ins],
            out_specs=outs,
            scratch_shapes=scratch,
        ),
        out_shape=out,
        input_output_aliases=aliases or {},
        compiler_params=pltpu.CompilerParams(vmem_limit_bytes=mib * 1024 * 1024),
        cost_estimate=pl.CostEstimate(
            flops=flops, bytes_accessed=bytes_accessed, transcendentals=exps
        ),
    )(*scalars, *[array for array, _ in ins])


def fixed(*shape):
    return pl.BlockSpec(shape, lambda *_: (0,) * len(shape))


def shaped(shape, dtype):
    return jax.ShapeDtypeStruct(shape, dtype)


def exchanged(blocks, axes):
    return lax.all_to_all(blocks, axes, 0, 0, tiled=True)


def swap_core(block):
    return lax.ppermute(block, "core", [(0, 1), (1, 0)])


def summed(pieces):
    return jnp.sum(pieces.astype(f32), axis=0)


def mm(a, b):
    return jnp.dot(a, b, preferred_element_type=f32)


def mm_nt(a, b):
    return jnp.einsum("ik,jk->ij", a, b, preferred_element_type=f32)


def mm_tn(a, b):
    return jnp.einsum("ki,kj->ij", a, b, preferred_element_type=f32)


def shards(
    hidden_in, block_order, attn_gain, w_qkv, b_qkv, w_out, mlp_gain, w_gate_up, w_down, cotangent
):
    yi, qi = lax.axis_index("y"), lax.axis_index("xl")
    ci = 2 * yi + qi
    fi = lax.axis_index(FSDP)
    core = lax.axis_index("core")
    group = yi // 2
    half = qi.astype(jnp.int32)[None]
    x_own, cot_own = hidden_in[0], cotangent[0]

    heads = [3 * yi + 2 * qi, 3 * yi + 1, H + group, H + KVH + group]
    vectors = [jnp.pad(attn_gain, (0, 32)), jnp.pad(mlp_gain, (0, 32)), b_qkv]
    packed = packed_columns(heads, w_qkv, vectors)

    order = block_order[0]
    positions = (order[:, None] * 64 + jnp.arange(64, dtype=jnp.int32)[None, :]).reshape(1024)
    frequency = jnp.exp(jnp.arange(0, HD, 2, dtype=f32) * (-math.log(rope_base) / HD))
    angles = positions.astype(f32)[:, None] * frequency[None, :]
    cosine, sine = jnp.cos(angles), jnp.sin(angles)
    cosine = jnp.concatenate([cosine, cosine], axis=1)
    sine = jnp.concatenate([-sine, sine], axis=1)
    pos_col, pos_row = positions[:, None], positions[None, :]

    def both_sides(block):
        return jnp.stack([block, lax.ppermute(block, "xh", [(0, 1), (1, 0)])])

    def along_z(sides):
        return exchanged(jnp.broadcast_to(sides, (4,) + sides.shape), ("z",))

    packed = both_sides(packed)
    w_out = both_sides(w_out)
    x_gather = gather_stages(jnp.concatenate([x_own, cot_own], axis=1), "y", "xl", True)
    *x_state, packed, w_down, w_gate_up_later, cosine, sine = tied(
        *next(x_gather), packed, w_down, w_gate_up, cosine, sine
    )
    own = along_z(packed)
    *x_state, own, w_out = tied(*x_gather.send(x_state), own, w_out)
    own_out = along_z(w_out)
    x_got = x_gather.send(x_gather.send(x_state))

    down = lax.dynamic_slice_in_dim(w_down, PART * ci, PART, 0)
    down = folded(jnp.concatenate([down, jnp.zeros((2, D), bf16)], axis=0))
    ffn_own = jnp.concatenate([picked(ci, w_gate_up_later), down], axis=1)
    w_ffn = lax.all_gather(ffn_own, FSDP, axis=0, tiled=True)

    att_mine, queries, lse, keys, values, normed_all, w_mine, gains, x_all = attend(
        x_got, own, core, qi, heads, cosine, sine, pos_col, pos_row
    )
    att_gather = gather_stages(att_mine, "y", "xl")
    *att_state, cot_all = tied(*next(att_gather), placed(x_got))
    *att_state, own_out, w_dn = tied(*att_gather.send(att_state), own_out, down_weights(w_ffn))
    att_got = att_gather.send(att_gather.send(att_state))
    attended_all, nm_all, middle, inv_second, w_out_all = to_middle(
        att_got, own_out, core, lax.axis_index("xh"), x_all, gains
    )

    hidden_far, gate_far, up_far, hn_far = feed_forward(nm_all, cot_all, w_ffn, w_dn, 1)
    hidden_near, gate_near, up_near, hn_near = feed_forward(nm_all, cot_all, w_ffn, w_dn, 0)
    hn_stages = scatter_stages(ordered_part(hn_near, hn_far), "y", "xl")
    *state, cot_all, hidden_near, hidden_far = tied(
        *next(hn_stages), cot_all, hidden_near, hidden_far
    )
    ffn_parts = down_product(cot_all, (hidden_near, hidden_far))
    *state, nm_all, gate_near, gate_far, up_near, up_far = tied(
        *hn_stages.send(state), nm_all, gate_near, gate_far, up_near, up_far
    )
    ffn_parts = gate_up_product(nm_all, (gate_near, gate_far), (up_near, up_far), ffn_parts)
    ffn_sides = lax.psum_scatter(ffn_parts, ("z", "core"), scatter_dimension=0, tiled=True)[0]
    hn_parts = hn_stages.send(hn_stages.send(state))
    *hn_parts, out_near, out_far = tied(
        *hn_parts, mm(hidden_near, w_dn).astype(bf16), mm(hidden_far, w_dn).astype(bf16)
    )

    grad_middle, send = middle_back(hn_parts, middle, inv_second, gains, cot_own, w_out_all)
    got = exchanged(send, CTX)
    gp_mine, columns = attend_back(
        half, got, queries, lse, keys, values, cosine, sine, pos_col, pos_row
    )
    given, kept = attention_products(core, normed_all, attended_all, gp_mine, columns)
    mine_both = add(kept, swap_core(given))
    mine_both, xn_part = tied(mine_both, mm_nt(gp_mine, w_mine).astype(bf16))
    mine_sides = summed(exchanged(mine_both, ("z",))).astype(bf16)
    xn_of, out_of = rows_part(xn_part), ordered_part(out_near, out_far)
    xn_out = scattered(
        lambda step, flip: jnp.concatenate([xn_of(step, flip), out_of(step, flip)], axis=1),
        "y",
        "xl",
    )
    xn_out = sum(term.astype(f32) for term in xn_out)
    grad_xn = xn_out[:, :D]
    hidden_out = middle + xn_out[:, D:]
    sides = jnp.concatenate([ffn_sides, mine_sides], axis=2)
    side = lax.axis_index("xh")
    weight_sum = add(
        lax.dynamic_index_in_dim(sides, side, 0, keepdims=False),
        lax.ppermute(
            lax.dynamic_index_in_dim(sides, 1 - side, 0, keepdims=False), "xh", [(0, 1), (1, 0)]
        ),
    )
    resid = x_own.astype(f32)
    inv_first = lax.rsqrt(jnp.mean(resid * resid, axis=-1, keepdims=True) + eps)
    scaled = grad_xn * gains[:1]
    grad_in = (
        grad_middle
        + inv_first * scaled
        - resid * (inv_first**3) * jnp.mean(resid * scaled, axis=-1, keepdims=True)
    )

    own_gains = jnp.stack([jnp.pad(g.astype(f32), (0, 32)) for g in (mlp_gain, attn_gain)])
    grad_w_gate_up, grad_w_down, grad_w_qkv, grad_w_out, vectors = weight_gradients(
        gather_eight(weight_sum, "y", "xl"),
        w_gate_up,
        w_qkv,
        jnp.pad(own_gains, ((0, 6), (0, 0)), constant_values=1.0),
        fi,
    )
    grad_mlp_gain, grad_attn_gain, grad_b_qkv = vectors[0, :96], vectors[1, :96], vectors[2]

    return (
        hidden_out[None],
        grad_in[None],
        grad_attn_gain,
        grad_w_qkv,
        grad_b_qkv,
        grad_w_out,
        grad_mlp_gain,
        grad_w_gate_up,
        grad_w_down,
    )


def solution(mesh):
    fine = Mesh(mesh.devices.reshape(4, 2, 2, 4, 2), CTX + FSDP)
    rows = P(FSDP, CTX, None)
    vector = P(FSDP)
    matrix = P(FSDP, None)
    return jax.shard_map(
        shards,
        mesh=fine,
        in_specs=(rows, matrix, vector, matrix, vector, matrix, vector, matrix, matrix, rows),
        out_specs=(rows, rows, vector, matrix, vector, matrix, vector, matrix, matrix),
        check_vma=False,
    )
```

```python
import math

import jax
import jax.numpy as jnp
from jax import lax
from jax.experimental import pallas as pl
from jax.experimental.pallas import tpu as pltpu
from jax.sharding import Mesh, PartitionSpec as P

D = 1536
H = 12
KVH = 2
HD = 128
FF = 8960
PART = FF // 128
WIDE = 1152
MINE = 896

CTX = ("y", "xl")
FSDP = ("xh", "z", "core")

eps = 1e-06
rope_base = 1000000.0
masked_value = -1e30
bf16 = jnp.bfloat16
f32 = jnp.float32


def moved(block, ring, pair, step, flip):
    size = lax.axis_size(ring)
    if step == 0:
        return lax.ppermute(block, pair, [(0, 1), (1, 0)])
    return lax.ppermute(block, ring, [(i, (i + step) % size) for i in range(size)])


def halfway(rows):
    return rows // 32 * 16


def gather_stages(block, ring, pair, by_ring=False):
    half = halfway(block.shape[0])
    across, before, after_ = yield (
        moved(block, ring, pair, 0, 1),
        moved(block, ring, pair, 1, 0),
        moved(block, ring, pair, -1, 0),
    )
    far_first, far_second, across_before, across_after = yield (
        moved(before[:half], ring, pair, 1, 0),
        moved(after_[half:], ring, pair, -1, 0),
        moved(across, ring, pair, 1, 0),
        moved(across, ring, pair, -1, 0),
    )
    if by_ring:
        last = (
            moved(across_before[:half], ring, pair, 1, 0),
            moved(across_after[half:], ring, pair, -1, 0),
        )
    else:
        last = (moved(far_first, ring, pair, 0, 1), moved(far_second, ring, pair, 0, 1))
    across_far_first, across_far_second = yield last
    yield [
        (0, 0, 0, block),
        (0, 1, 0, across),
        (-1, 0, 0, before),
        (1, 0, 0, after_),
        (-1, 1, 0, across_before),
        (1, 1, 0, across_after),
        (2, 0, 0, far_first),
        (2, 0, half, far_second),
        (2, 1, 0, across_far_first),
        (2, 1, half, across_far_second),
    ]


def in_step(*gathers):
    states = [next(g) for g in gathers]
    for _ in range(3):
        if len(gathers) > 1:
            states = lax.optimization_barrier(states)
        states = [g.send(state) for g, state in zip(gathers, states)]
    return states


def gather_eight(block, ring, pair):
    return in_step(gather_stages(block, ring, pair))[0]


def place(ring, pair, ring_major, step, flip):
    size = lax.axis_size(ring)
    r = (lax.axis_index(ring) + step) % size
    q = lax.axis_index(pair)
    q = 1 - q if flip else q
    return r * 2 + q if ring_major else q * size + r


def places_of(got, ring, pair, ring_major):
    return [place(ring, pair, ring_major, step, flip) for step, flip, _, _ in got]


def pick_kernel(at_ref, weights, out):
    for c in range(8):

        @pl.when(at_ref[0] == c)
        def _():
            for part in range(2):
                for s in range(16):
                    start, to = part * FF + 560 * s + PART * c, part * WIDE + 72 * s
                    out[:, to : to + PART] = weights[:, start : start + PART]
                    out[:, to + PART : to + 72] = jnp.zeros((96, 2), bf16)


def picked(slice_index, weights):
    return call(
        pick_kernel,
        shaped((96, 2 * WIDE), bf16),
        (1,),
        [(weights, fixed(96, 2 * FF))],
        fixed(96, 2 * WIDE),
        mib=12,
        scalars=(slice_index.astype(jnp.int32)[None],),
        bytes_accessed=4 * 1024 * 1024,
    )


def folded(rows):
    rest = rows[:, WIDE:]
    rest = jnp.concatenate([rest[24 * k : 24 * (k + 1)] for k in range(3)], axis=1)
    return jnp.concatenate([rows[:, :WIDE], rest], axis=0)


def unfolded(rows):
    rest = jnp.concatenate([rows[72:, 384 * k : 384 * (k + 1)] for k in range(3)], axis=0)
    return jnp.concatenate([rows[:72], rest], axis=1)


def unfold_kernel(weights, out):
    out[0] = unfolded(weights[...].astype(f32)).astype(bf16)


def down_weights(w_ffn):
    return call(
        unfold_kernel,
        shaped((16, 72, D), bf16),
        (16,),
        [(w_ffn, pl.BlockSpec((96, WIDE), lambda s: (s, 2)))],
        pl.BlockSpec((1, 72, D), lambda s: (s, 0, 0)),
        bytes_accessed=8 * 1024 * 1024,
    ).reshape(WIDE, D)


def last_kernel(at_ref, *refs):
    pieces, weights, weights_qkv, gains = refs[:10], *refs[10:13]
    out, out_qkv, out_out, vectors, blocks, sums, bias = refs[13:]
    step = pl.program_id(0)
    for i in range(6):
        blocks[at_ref[i]] = pieces[i][...]
    for i in (6, 8):
        blocks[at_ref[i]] = jnp.where(step < 3, pieces[i][...], pieces[i + 1][...])
    total = jnp.zeros((16, 1), f32)
    for part in range(2):
        for shards in range(0, 16, 8):
            row = jnp.concatenate(
                [
                    blocks[c, :, part * WIDE + 72 * s : part * WIDE + 72 * s + PART]
                    for s in range(shards, shards + 8)
                    for c in range(8)
                ],
                axis=1,
            )
            start = part * FF + 560 * shards
            out[:, start : start + 4480] = row.astype(f32)
    for at in range(0, 2 * FF, 1792):
        lanes = slice(at, at + 1792)
        total = total + jnp.sum(
            out[:, lanes] * weights[:, lanes].astype(f32), axis=1, keepdims=True
        )
    rows = pl.ds(pl.multiple_of(step * 16, 16), 16)
    sums[0, rows] = jnp.broadcast_to(total, (16, HD))

    def whole(c, at, rows=slice(0, 16)):
        start = 3 * WIDE + at * HD
        return blocks[c, rows, start : start + HD].astype(f32)

    def heads(term):
        for y in range(4):
            yield 3 * y, term(2 * y, 0)
            yield 3 * y + 1, term(2 * y, 1) + term(2 * y + 1, 1)
            yield 3 * y + 2, term(2 * y + 1, 0)
        for kind in range(2):
            for group in range(2):
                yield 12 + 2 * kind + group, sum(term(4 * group + i, 2 + kind) for i in range(4))

    total = jnp.zeros((16, 1), f32)
    for h, value in heads(whole):
        lanes = slice(h * HD, (h + 1) * HD)
        out_qkv[:, lanes] = value
        total = total + jnp.sum(
            value * weights_qkv[:, lanes].astype(f32), axis=1, keepdims=True
        )
    sums[1, rows] = jnp.broadcast_to(total, (16, HD))
    for y in range(4):
        at = 3 * y * HD
        out_out[:, at : at + HD] = whole(2 * y, 4)
        out_out[:, at + HD : at + 2 * HD] = whole(2 * y, 5) + whole(2 * y + 1, 5)
        out_out[:, at + 2 * HD : at + 3 * HD] = whole(2 * y + 1, 4)

    @pl.when(step == 0)
    def _():
        for h, value in heads(lambda c, kind: whole(c, 6)[kind : kind + 1]):
            bias[h : h + 1] = value

    @pl.when(step == 5)
    def _():
        vectors[...] = jnp.zeros_like(vectors)
        for i in range(2):
            vectors[i : i + 1, :96] = sums[i].T[:1, :96] / gains[i : i + 1, :96]
        vectors[2:3] = bias[pl.ds(at_ref[10], 1)]


def last_down_kernel(at_ref, *refs):
    pieces, out, blocks = refs[:10], refs[10], refs[11]
    for i in range(6):
        blocks[at_ref[i]] = pieces[i][...].astype(f32)
    for i in (6, 8):
        blocks[at_ref[i], :48] = pieces[i][...].astype(f32)
        blocks[at_ref[i], 48:] = pieces[i + 1][...].astype(f32)
    for c in range(8):
        out[PART * c : PART * (c + 1)] = unfolded(blocks[c])[:PART]


def weight_gradients(got, weights, weights_qkv, gains, head):
    pieces = [g[3] for g in got]
    places = jnp.stack([*places_of(got, "y", "xl", True), head]).astype(jnp.int32)
    width = 3 * WIDE + MINE

    def rows(i, at):
        return i, 0

    maps = [rows] * 6 + [
        lambda i, at: (jnp.minimum(i, 2), 0),
        lambda i, at: (jnp.maximum(i - 3, 0), 0),
    ] * 2
    w_gate_up, w_qkv, w_out, vectors = call(
        last_kernel,
        [
            shaped((96, 2 * FF), f32),
            shaped((96, 2048), f32),
            shaped((96, D), f32),
            shaped((8, HD), f32),
        ],
        (6,),
        [(p, pl.BlockSpec((16, width), m)) for p, m in zip(pieces, maps)]
        + [
            (weights, pl.BlockSpec((16, 2 * FF), rows)),
            (weights_qkv, pl.BlockSpec((16, 2048), rows)),
            (gains, fixed(8, HD)),
        ],
        [
            pl.BlockSpec((16, 2 * FF), rows),
            pl.BlockSpec((16, 2048), rows),
            pl.BlockSpec((16, D), rows),
            fixed(8, HD),
        ],
        scalars=(places,),
        scratch=[
            pltpu.VMEM((8, 16, width), bf16),
            pltpu.VMEM((2, 96, HD), f32),
            pltpu.VMEM((16, HD), f32),
        ],
        mib=24,
        bytes_accessed=96 * 2 * FF * 8,
    )
    w_down = call(
        last_down_kernel,
        shaped((560, D), f32),
        (1,),
        [(p, pl.BlockSpec((p.shape[0], WIDE), lambda i, at: (0, 2))) for p in pieces],
        fixed(560, D),
        scalars=(places,),
        scratch=[pltpu.VMEM((8, 96, WIDE), f32)],
        mib=24,
        bytes_accessed=6 * 1024 * 1024,
    )
    return w_gate_up, w_down, w_qkv, w_out, vectors


def mine_kernel(at, normed, attended, grads, columns, given, kept):
    core = at[0]
    left = tn(normed[...], grads[...])
    right = tn(attended[...], columns[...])
    sums = jnp.sum(grads[...].astype(f32), axis=0, keepdims=True)
    bias = jnp.concatenate(
        [sums[:, i * HD : (i + 1) * HD] for i in range(4)] + [jnp.zeros((92, HD), f32)], axis=0
    )
    total = jnp.concatenate([left, right], axis=1).astype(bf16)
    bias = bias.astype(bf16)
    for p in range(2):
        even = total[192 * p : 192 * p + 96]
        odd = total[192 * p + 96 : 192 * (p + 1)]
        kept[p, 0, :, :768] = jnp.where(core == 0, even, odd)
        given[p, 0, :, :768] = jnp.where(core == 0, odd, even)
        kept[p, 0, :, 768:] = bias
        given[p, 0, :, 768:] = bias


def attention_products(core, normed, attended, grads, columns):
    out = pl.BlockSpec((2, 1, 96, MINE), lambda g, at: (g % 2, g // 2, 0, 0))
    return call(
        mine_kernel,
        [shaped((4, 2, 96, MINE), bf16)] * 2,
        (4,),
        [
            (normed, pl.BlockSpec((1024, 384), lambda g, at: (0, g))),
            (attended, pl.BlockSpec((1024, 384), lambda g, at: (0, g))),
            (grads, fixed(1024, 512)),
            (columns, fixed(1024, 256)),
        ],
        [out, out],
        scalars=(core.astype(jnp.int32)[None],),
        mib=24,
        flops=2 * 1024 * D * 768,
        bytes_accessed=10 * 1024 * 1024,
    )


def pack_kernel(at, weights, vectors, out):
    for i in range(4):
        out[:, i * HD : (i + 1) * HD] = weights[:, pl.ds(pl.multiple_of(at[i] * HD, HD), HD)]
    out[:, 4 * HD :] = jnp.concatenate([vectors[...], jnp.zeros((80, HD), bf16)], axis=0)


def packed_columns(heads, weights, vectors):
    rows = jnp.concatenate([jnp.stack(vectors), jnp.zeros((13, HD), bf16)], axis=0)
    return call(
        pack_kernel,
        shaped((96, 640), bf16),
        (1,),
        [(weights, fixed(96, 2048)), (rows, fixed(16, HD))],
        fixed(96, 640),
        scalars=(jnp.stack(heads).astype(jnp.int32),),
        bytes_accessed=2 * 1024 * 1024,
    )


def turned(field, cos_ref, sin_ref):
    return field * cos_ref + pltpu.roll(field, HD // 2, 1) * sin_ref


def nt(a, b):
    return lax.dot_general(a, b, (((1,), (1,)), ((), ())), preferred_element_type=f32)


def tn(a, b):
    return lax.dot_general(a, b, (((0,), (0,)), ((), ())), preferred_element_type=f32)


SCALE = 1.0 / math.sqrt(HD)


def attend_kernel(*refs):
    at, pieces, own, other, cos, sin, pos_col, pos_row = refs[0], refs[1:11], *refs[11:17]
    att, queries, lse, keys, values, normed, weights, gains, x, woven, proj = refs[17:]
    c, core, half = pl.program_id(0), at[10], at[11]

    @pl.when(c == 0)
    def _():
        for i, piece in enumerate(pieces):
            first = 64 if i in (7, 9) else 0
            x[at[i], first : first + piece.shape[0]] = piece[...]
        for i in range(8):
            index = 4 * (at[16] if i % 2 == 0 else 1 - at[16]) + i // 2
            woven[index, core] = own[i]
            woven[index, 1 - core] = other[i]
        gains[...] = jnp.zeros_like(gains)
        for s in range(16):
            weights[96 * s : 96 * (s + 1)] = woven[s // 2, s % 2, :, :512]
            rows = woven[s // 2, s % 2, :16, 512:].astype(f32)
            gains[0:2, 96 * s : 96 * (s + 1)] = rows[0:2, :96]
        bias = jnp.concatenate(
            [
                woven[at[12 + i] // 2, at[12 + i] % 2, :16, 512:].astype(f32)[2:3]
                for i in range(4)
            ],
            axis=1,
        )
        for i in range(8):
            rows = x[i].astype(f32)
            inv = lax.rsqrt(jnp.mean(rows * rows, axis=1, keepdims=True) + eps)
            normed[128 * i : 128 * (i + 1)] = (rows * inv * gains[0:1]).astype(bf16)
        proj[...] = jnp.dot(normed[...], weights[...], preferred_element_type=f32) + bias
        keys[...] = turned(proj[:, 2 * HD : 3 * HD], cos[...], sin[...]).astype(bf16)
        values[...] = proj[:, 3 * HD :].astype(bf16)

    rows = pl.ds(pl.multiple_of(c * 128, 128), 128)
    part = pl.ds(pl.multiple_of(c * 128 + half * 64, 64), 64)
    query = jnp.concatenate(
        [
            turned(proj[rows, :HD], cos[rows], sin[rows]),
            turned(proj[part, HD : 2 * HD], cos[part], sin[part]),
        ],
        axis=0,
    ).astype(bf16)
    queries[...] = query
    scores = nt(query, keys[...]) * SCALE
    seen = jnp.concatenate([pos_col[rows], pos_col[part]], axis=0) >= pos_row[...]
    scores = jnp.where(seen, scores, masked_value)
    row_max = jnp.max(scores, axis=1, keepdims=True)
    exponent = jnp.exp(scores - row_max)
    total = jnp.sum(exponent, axis=1, keepdims=True)
    probability = (exponent / total).astype(bf16)
    att[...] = jnp.dot(probability, values[...], preferred_element_type=f32).astype(bf16)
    lse[...] = jnp.broadcast_to(row_max + jnp.log(total), (192, HD))


def attend(x_got, own, core, half, heads, cos, sin, pos_col, pos_row):
    block = pl.BlockSpec((192, HD), lambda c, at: (c, 0))
    at = [*places_of(x_got, "y", "xl", True), core, half, *heads, lax.axis_index("xh")]
    at = jnp.stack(at).astype(jnp.int32)
    own = own.reshape(8, 96, 640)
    return call(
        attend_kernel,
        [
            shaped((1536, HD), bf16),
            shaped((1536, HD), bf16),
            shaped((1536, HD), f32),
            shaped((1024, HD), bf16),
            shaped((1024, HD), bf16),
            shaped((1024, D), bf16),
            shaped((D, 512), bf16),
            shaped((8, D), f32),
            shaped((8, 128, D), bf16),
        ],
        (8,),
        [(g[3], fixed(g[3].shape[0], D)) for g in x_got]
        + [
            (own, fixed(8, 96, 640)),
            (swap_core(own), fixed(8, 96, 640)),
            (cos, fixed(1024, HD)),
            (sin, fixed(1024, HD)),
            (pos_col, fixed(1024, 1)),
            (pos_row, fixed(1, 1024)),
        ],
        [
            block,
            block,
            block,
            fixed(1024, HD),
            fixed(1024, HD),
            fixed(1024, D),
            fixed(D, 512),
            fixed(8, D),
            fixed(8, 128, D),
        ],
        scalars=(at,),
        scratch=[
            pltpu.VMEM((8, 2, 96, 640), bf16),
            pltpu.VMEM((1024, 512), f32),
        ],
        mib=40,
        flops=4 * 1536 * 1024 * HD + 2 * 1024 * D * 512,
        bytes_accessed=14 * 1024 * 1024,
        exps=1536 * 1024,
    )


def attend_back_kernel(
    half_ref, got, queries, lse, keys, values, cos, sin, pos_col, pos_row, grads, columns, gk, gv
):
    c, half = pl.program_id(0), half_ref[0]

    @pl.when(c == 0)
    def _():
        gk[...] = jnp.zeros_like(gk)
        gv[...] = jnp.zeros_like(gv)

    rows = pl.ds(pl.multiple_of(c * 128, 128), 128)
    part = pl.ds(pl.multiple_of(c * 128 + half * 64, 64), 64)
    rest = pl.ds(pl.multiple_of(c * 128 + (1 - half) * 64, 64), 64)
    out = got[0, :192]
    query = queries[...]
    scores = nt(query, keys[...]) * SCALE
    seen = jnp.concatenate([pos_col[rows], pos_col[part]], axis=0) >= pos_row[...]
    scores = jnp.where(seen, scores, masked_value)
    probs = jnp.exp(scores - lse[:, :1])
    grad_prob = nt(out, values[...])
    inner = jnp.sum(probs * grad_prob, axis=1, keepdims=True)
    grad_scores = (probs * (grad_prob - inner)).astype(bf16)
    grad_query = jnp.dot(grad_scores, keys[...], preferred_element_type=f32) * SCALE
    gk[...] += tn(grad_scores, query)
    gv[...] += tn(probs.astype(bf16), out)
    grads[rows, :HD] = turned(grad_query[:128], cos[rows], -sin[rows]).astype(bf16)
    grads[part, HD : 2 * HD] = turned(grad_query[128:], cos[part], -sin[part]).astype(bf16)
    grads[rest, HD : 2 * HD] = jnp.zeros((64, HD), bf16)
    columns[:, :HD] = got[0, 192:320]
    columns[pl.ds(pl.multiple_of(half * 64, 64), 64), HD:] = got[0, 320:]
    columns[pl.ds(pl.multiple_of((1 - half) * 64, 64), 64), HD:] = jnp.zeros((64, HD), bf16)

    @pl.when(c == 7)
    def _():
        grads[:, 2 * HD : 3 * HD] = turned(gk[...] * SCALE, cos[...], -sin[...]).astype(bf16)
        grads[:, 3 * HD :] = gv[...].astype(bf16)


def attend_back(half, got, queries, lse, keys, values, cos, sin, pos_col, pos_row):
    block = pl.BlockSpec((192, HD), lambda c, half: (c, 0))
    return call(
        attend_back_kernel,
        [shaped((1024, 4 * HD), bf16), shaped((1024, 2 * HD), bf16)],
        (8,),
        [
            (got, pl.BlockSpec((1, 384, HD), lambda c, half: (c, 0, 0))),
            (queries, block),
            (lse, block),
            (keys, fixed(1024, HD)),
            (values, fixed(1024, HD)),
            (cos, fixed(1024, HD)),
            (sin, fixed(1024, HD)),
            (pos_col, fixed(1024, 1)),
            (pos_row, fixed(1, 1024)),
        ],
        [fixed(1024, 4 * HD), pl.BlockSpec((128, 2 * HD), lambda c, half: (c, 0))],
        scalars=(half,),
        scratch=[pltpu.VMEM((1024, HD), f32), pltpu.VMEM((1024, HD), f32)],
        mib=50,
        flops=10 * 1536 * 1024 * HD,
        bytes_accessed=6 * 1024 * 1024,
        exps=1536 * 1024,
    )


def place_kernel(*refs):
    pieces, out = refs[:10], refs[10]
    for i, piece in enumerate(pieces):
        at = 128 * (i if i < 6 else 6 + (i - 6) // 2) + (64 if i in (7, 9) else 0)
        out[at : at + piece.shape[0]] = piece[...]


def placed(got):
    return call(
        place_kernel,
        shaped((1024, D), bf16),
        (1,),
        [(g[3], pl.BlockSpec((g[3].shape[0], D), lambda i: (0, 1))) for g in got],
        fixed(1024, D),
        bytes_accessed=4 * 1024 * D,
    )


def middle_kernel(at, *refs):
    pieces, own, other, x, gains = refs[:10], *refs[10:14]
    attended, normed, middle, inverse, w_out, heads = refs[14:]
    step, core, side = pl.program_id(0), at[10], at[11]

    @pl.when(step == 0)
    def _():
        for i in range(8):
            index = 2 * (4 * (side if i % 2 == 0 else 1 - side) + i // 2)
            w_out[index + core] = own[i]
            w_out[index + 1 - core] = other[i]
        for i, piece in enumerate(pieces):
            first = 768 if i in (7, 9) else 0
            heads[at[i], first : first + piece.shape[0]] = piece[...]

    block = at[12 + step]
    rows = pl.ds(pl.multiple_of(block * 192, 64), 128)
    part = pl.ds(pl.multiple_of(block * 192 + 128, 64), 64)
    for y in range(4):
        for q in range(2):
            whole, split = HD * (3 * y + 2 * q), HD * (3 * y + 1)
            attended[:, whole : whole + HD] = heads[2 * y + q, rows]
            attended[64 * q : 64 * (q + 1), split : split + HD] = heads[2 * y + q, part]
    weights = w_out[...].reshape(D, D)
    mid = x[0].astype(f32) + jnp.dot(attended[...], weights, preferred_element_type=f32)
    inv = lax.rsqrt(jnp.mean(mid * mid, axis=1, keepdims=True) + eps)
    normed[...] = (mid * inv * gains[1:2]).astype(bf16)

    @pl.when(step == 0)
    def _():
        middle[...] = mid
        inverse[...] = jnp.broadcast_to(inv, (128, HD))


def to_middle(got, own, core, side, x, gains):
    own = own.reshape(8, 96, D)
    order = [place("y", "xl", True, step, flip) for step, flip in ORDER]
    *outs, w_out = call(
        middle_kernel,
        [
            shaped((1024, D), bf16),
            shaped((1024, D), bf16),
            shaped((128, D), f32),
            shaped((128, HD), f32),
            shaped((16, 96, D), bf16),
        ],
        (8,),
        [(g[3], fixed(*g[3].shape)) for g in got]
        + [
            (own, fixed(8, 96, D)),
            (swap_core(own), fixed(8, 96, D)),
            (x, pl.BlockSpec((1, 128, D), lambda b, at: (at[12 + b], 0, 0))),
            (gains, fixed(8, D)),
        ],
        [
            pl.BlockSpec((128, D), lambda b, at: (at[12 + b], 0)),
            pl.BlockSpec((128, D), lambda b, at: (b, 0)),
            fixed(128, D),
            fixed(128, HD),
            fixed(16, 96, D),
        ],
        scalars=(
            jnp.stack([*places_of(got, "y", "xl", True), core, side, *order]).astype(jnp.int32),
        ),
        scratch=[pltpu.VMEM((8, 1536, HD), bf16)],
        mib=40,
        flops=2 * 1024 * D * D,
        bytes_accessed=20 * 1024 * 1024,
    )
    return *outs, w_out.reshape(D, D)


def middle_back_kernel(a, b, c, d, middle, inverse, gain, cot, w_out, grad_middle, send):
    grad_hn = a[...].astype(f32) + b[...].astype(f32) + c[...].astype(f32) + d[...].astype(f32)
    inv, mid = inverse[:, :1], middle[...]
    scaled = grad_hn * gain[1:2]
    inner = jnp.mean(mid * scaled, axis=1, keepdims=True)
    grad = cot[...].astype(f32) + inv * scaled - mid * (inv * inv * inv * inner)
    grad_middle[...] = grad
    grad_attn = grad.astype(bf16)
    heads = nt(grad_attn, w_out[...]).astype(bf16)
    for y in range(4):
        for q in range(2):
            whole, split = HD * (3 * y + 2 * q), HD * (3 * y + 1)
            half = slice(64 * q, 64 * (q + 1))
            send[2 * y + q, :128] = heads[:, whole : whole + HD]
            send[2 * y + q, 128:192] = heads[half, split : split + HD]
            send[2 * y + q, 192:320] = grad_attn[:, whole : whole + HD]
            send[2 * y + q, 320:] = grad_attn[half, split : split + HD]


def middle_back(parts, middle, inverse, gain, cot, w_out):
    row = fixed(128, D)
    return call(
        middle_back_kernel,
        [shaped((128, D), f32), shaped((8, 384, HD), bf16)],
        (1,),
        [(p, row) for p in parts]
        + [
            (middle, row),
            (inverse, fixed(128, HD)),
            (gain, fixed(8, D)),
            (cot, row),
            (w_out, fixed(D, D)),
        ],
        [row, fixed(8, 384, HD)],
        mib=50,
        flops=2 * 128 * D * D,
        bytes_accessed=10 * 1024 * 1024,
    )


def down_product_kernel(*refs):
    hidden, cot, out, total = refs[:2], refs[2:4], refs[4], refs[5]
    step = pl.program_id(0)
    product = tn(hidden[0][...], cot[0][...]) + tn(hidden[1][...], cot[1][...])

    for k in range(3):

        @pl.when(step == k)
        def _():
            for s in range(16):
                total[s, :72, 384 * k : 384 * (k + 1)] = product[72 * s : 72 * (s + 1)]

    @pl.when(step == 3)
    def _():
        for s in range(16):
            for k in range(3):
                total[s, 72:, 384 * k : 384 * (k + 1)] = product[
                    72 * s + 24 * k : 72 * s + 24 * (k + 1)
                ]
        for s in range(16):
            out[s % 8, s // 8] = total[s].astype(bf16)


def gate_up_product_kernel(*refs):
    nm, rhs, out = refs[:2], refs[2:6], refs[7]

    def work(right):
        total = tn(nm[0][...], right[0][...]) + tn(nm[1][...], right[1][...])
        for i in range(4):
            out[i, 0] = total[96 * i : 96 * (i + 1)].astype(bf16)

    for j in range(2):
        pl.when(pl.program_id(0) == j)(lambda j=j: work(rhs[2 * j : 2 * j + 2]))


def down_product(cot, hidden):
    return call(
        down_product_kernel,
        shaped((8, 2, 96, 3 * WIDE), bf16),
        (4,),
        [(a, fixed(512, WIDE)) for a in hidden]
        + [
            (cot, pl.BlockSpec((512, 384), lambda t: (0, t))),
            (cot, pl.BlockSpec((512, 384), lambda t: (1, t))),
        ],
        pl.BlockSpec((8, 2, 96, WIDE), lambda t: (0, 0, 0, 2)),
        scratch=[pltpu.VMEM((16, 96, WIDE), f32)],
        mib=56,
        flops=2 * 1024 * D * WIDE,
        bytes_accessed=10 * 1024 * 1024,
    )


def gate_up_product(nm, gate, up, parts):
    return call(
        gate_up_product_kernel,
        shaped((8, 2, 96, 3 * WIDE), bf16),
        (2, 4),
        [
            (nm, pl.BlockSpec((512, 384), lambda j, g: (0, g))),
            (nm, pl.BlockSpec((512, 384), lambda j, g: (1, g))),
        ]
        + [(a, fixed(512, WIDE)) for pair in (gate, up) for a in pair]
        + [(parts, pl.BlockSpec(memory_space=pl.ANY))],
        pl.BlockSpec((4, 1, 96, WIDE), lambda j, g: (g % 2, g // 2, 0, j)),
        aliases={6: 0},
        mib=56,
        flops=2 * 1024 * D * 2 * WIDE,
        bytes_accessed=20 * 1024 * 1024,
    )


def feed_forward_kernel(
    nm, cot, w_gate, w_up, w_dn, hidden, grad_gate, grad_up, hn, total
):
    step = pl.program_id(0)
    gate = jnp.dot(nm[...], w_gate[...], preferred_element_type=f32)
    up = jnp.dot(nm[...], w_up[...], preferred_element_type=f32)
    act = nt(cot[...], w_dn[...])
    sigmoid_gate = jax.nn.sigmoid(gate)
    silu_gate = gate * sigmoid_gate
    hidden[...] = (silu_gate * up).astype(bf16)
    to_gate = (act * up * (sigmoid_gate * (1.0 + gate * (1.0 - sigmoid_gate)))).astype(bf16)
    to_up = (act * silu_gate).astype(bf16)
    grad_gate[...] = to_gate
    grad_up[...] = to_up
    term = nt(to_gate, w_gate[...]) + nt(to_up, w_up[...])

    @pl.when(step == 0)
    def _():
        total[...] = term

    @pl.when(step > 0)
    def _():
        total[...] += term

    @pl.when(step == 2)
    def _():
        hn[...] = total[...].astype(bf16)


def feed_forward(nm, cot, w_ffn, w_dn, half):
    whole, column = fixed(512, D), pl.BlockSpec((512, 384), lambda j: (0, j))
    narrow = shaped((512, WIDE), bf16)
    rows = pl.BlockSpec((512, D), lambda j: (half, 0))
    return call(
        feed_forward_kernel,
        [narrow, narrow, narrow, shaped((512, D), bf16)],
        (3,),
        [
            (nm, rows),
            (cot, rows),
            (w_ffn, pl.BlockSpec((D, 384), lambda j: (0, j))),
            (w_ffn, pl.BlockSpec((D, 384), lambda j: (0, 3 + j))),
            (w_dn, pl.BlockSpec((384, D), lambda j: (j, 0))),
        ],
        [column, column, column, whole],
        scratch=[pltpu.VMEM((512, D), f32)],
        mib=36,
        flops=2 * 512 * D * 5 * WIDE,
        bytes_accessed=20 * 1024 * 1024,
        exps=512 * WIDE,
    )


def add(a, *others):
    total = a.astype(f32)
    for other in others:
        total = total + other.astype(f32)
    return total.astype(bf16)


def scatter_stages(part, ring, pair):
    away = part(2, 1)
    half = halfway(away.shape[0])
    away, from_after, from_before = yield (
        moved(away, ring, pair, 0, 1),
        moved(part(-1, 1), ring, pair, -1, 0),
        moved(part(1, 1), ring, pair, 1, 0),
    )
    away = add(part(2, 0), away)
    away_first, away_second, got_across = yield (
        moved(away[:half], ring, pair, -1, 0),
        moved(away[half:], ring, pair, 1, 0),
        moved(add(part(0, 1), from_after, from_before), ring, pair, 0, 1),
    )
    back, ahead = part(-1, 0), part(1, 0)
    back = jnp.concatenate([add(back[:half], away_first), back[half:]], axis=0)
    ahead = jnp.concatenate([ahead[:half], add(ahead[half:], away_second)], axis=0)
    got = yield moved(back, ring, pair, -1, 0), moved(ahead, ring, pair, 1, 0)
    yield part(0, 0), got_across, *got


def scattered(part, ring, pair):
    stages = scatter_stages(part, ring, pair)
    state = next(stages)
    for _ in range(3):
        state = stages.send(state)
    return state


ORDER = [(0, 0), (0, 1), (-1, 0), (1, 0), (-1, 1), (1, 1), (2, 0), (2, 1)]


def rows_part(array):
    def part(step, flip):
        at = place("y", "xl", True, step, flip)
        return lax.dynamic_slice_in_dim(array, at * 128, 128, 0)

    return part


def ordered_part(near, far):
    def part(step, flip):
        i = ORDER.index((step, flip))
        return (near, far)[i // 4][i % 4 * 128 : (i % 4 + 1) * 128]

    return part


def tied(*values):
    return lax.optimization_barrier(values)


def call(
    kernel,
    out,
    grid,
    ins,
    outs,
    scalars=(),
    scratch=(),
    aliases=None,
    mib=16,
    flops=0,
    bytes_accessed=0,
    exps=0,
):
    return pl.pallas_call(
        kernel,
        grid_spec=pltpu.PrefetchScalarGridSpec(
            num_scalar_prefetch=len(scalars),
            grid=grid,
            in_specs=[spec for _, spec in ins],
            out_specs=outs,
            scratch_shapes=scratch,
        ),
        out_shape=out,
        input_output_aliases=aliases or {},
        compiler_params=pltpu.CompilerParams(vmem_limit_bytes=mib * 1024 * 1024),
        cost_estimate=pl.CostEstimate(
            flops=flops, bytes_accessed=bytes_accessed, transcendentals=exps
        ),
    )(*scalars, *[array for array, _ in ins])


def fixed(*shape):
    return pl.BlockSpec(shape, lambda *_: (0,) * len(shape))


def shaped(shape, dtype):
    return jax.ShapeDtypeStruct(shape, dtype)


def exchanged(blocks, axes):
    return lax.all_to_all(blocks, axes, 0, 0, tiled=True)


def swap_core(block):
    return lax.ppermute(block, "core", [(0, 1), (1, 0)])


def summed(pieces):
    return jnp.sum(pieces.astype(f32), axis=0)


def mm(a, b):
    return jnp.dot(a, b, preferred_element_type=f32)


def mm_nt(a, b):
    return jnp.einsum("ik,jk->ij", a, b, preferred_element_type=f32)


def mm_tn(a, b):
    return jnp.einsum("ki,kj->ij", a, b, preferred_element_type=f32)


def shards(
    hidden_in, block_order, attn_gain, w_qkv, b_qkv, w_out, mlp_gain, w_gate_up, w_down, cotangent
):
    yi, qi = lax.axis_index("y"), lax.axis_index("xl")
    ci = 2 * yi + qi
    fi = lax.axis_index(FSDP)
    core = lax.axis_index("core")
    group = yi // 2
    half = qi.astype(jnp.int32)[None]
    x_own, cot_own = hidden_in[0], cotangent[0]

    heads = [3 * yi + 2 * qi, 3 * yi + 1, H + group, H + KVH + group]
    vectors = [jnp.pad(attn_gain, (0, 32)), jnp.pad(mlp_gain, (0, 32)), b_qkv]
    packed = packed_columns(heads, w_qkv, vectors)

    order = block_order[0]
    positions = (order[:, None] * 64 + jnp.arange(64, dtype=jnp.int32)[None, :]).reshape(1024)
    frequency = jnp.exp(jnp.arange(0, HD, 2, dtype=f32) * (-math.log(rope_base) / HD))
    angles = positions.astype(f32)[:, None] * frequency[None, :]
    cosine, sine = jnp.cos(angles), jnp.sin(angles)
    cosine = jnp.concatenate([cosine, cosine], axis=1)
    sine = jnp.concatenate([-sine, sine], axis=1)
    pos_col, pos_row = positions[:, None], positions[None, :]

    def both_sides(block):
        return jnp.stack([block, lax.ppermute(block, "xh", [(0, 1), (1, 0)])])

    def along_z(sides):
        return exchanged(jnp.broadcast_to(sides, (4,) + sides.shape), ("z",))

    packed = both_sides(packed)
    w_out = both_sides(w_out)
    x_gather = gather_stages(jnp.concatenate([x_own, cot_own], axis=1), "y", "xl", True)
    *x_state, packed, w_down, w_gate_up_later, cosine, sine = tied(
        *next(x_gather), packed, w_down, w_gate_up, cosine, sine
    )
    own = along_z(packed)
    *x_state, own, w_out = tied(*x_gather.send(x_state), own, w_out)
    own_out = along_z(w_out)
    x_got = x_gather.send(x_gather.send(x_state))

    down = lax.dynamic_slice_in_dim(w_down, PART * ci, PART, 0)
    down = folded(jnp.concatenate([down, jnp.zeros((2, D), bf16)], axis=0))
    ffn_own = jnp.concatenate([picked(ci, w_gate_up_later), down], axis=1)
    w_ffn = lax.all_gather(ffn_own, FSDP, axis=0, tiled=True)

    att_mine, queries, lse, keys, values, normed_all, w_mine, gains, x_all = attend(
        x_got, own, core, qi, heads, cosine, sine, pos_col, pos_row
    )
    att_gather = gather_stages(att_mine, "y", "xl")
    *att_state, cot_all = tied(*next(att_gather), placed(x_got))
    *att_state, own_out, w_dn = tied(*att_gather.send(att_state), own_out, down_weights(w_ffn))
    att_got = att_gather.send(att_gather.send(att_state))
    attended_all, nm_all, middle, inv_second, w_out_all = to_middle(
        att_got, own_out, core, lax.axis_index("xh"), x_all, gains
    )

    hidden_far, gate_far, up_far, hn_far = feed_forward(nm_all, cot_all, w_ffn, w_dn, 1)
    hidden_near, gate_near, up_near, hn_near = feed_forward(nm_all, cot_all, w_ffn, w_dn, 0)
    hn_stages = scatter_stages(ordered_part(hn_near, hn_far), "y", "xl")
    *state, cot_all, hidden_near, hidden_far = tied(
        *next(hn_stages), cot_all, hidden_near, hidden_far
    )
    ffn_parts = down_product(cot_all, (hidden_near, hidden_far))
    *state, nm_all, gate_near, gate_far, up_near, up_far = tied(
        *hn_stages.send(state), nm_all, gate_near, gate_far, up_near, up_far
    )
    ffn_parts = gate_up_product(nm_all, (gate_near, gate_far), (up_near, up_far), ffn_parts)
    ffn_sides = lax.psum_scatter(ffn_parts, ("z", "core"), scatter_dimension=0, tiled=True)[0]
    hn_parts = hn_stages.send(hn_stages.send(state))
    *hn_parts, out_near, out_far = tied(
        *hn_parts, mm(hidden_near, w_dn).astype(bf16), mm(hidden_far, w_dn).astype(bf16)
    )

    grad_middle, send = middle_back(hn_parts, middle, inv_second, gains, cot_own, w_out_all)
    got = exchanged(send, CTX)
    gp_mine, columns = attend_back(
        half, got, queries, lse, keys, values, cosine, sine, pos_col, pos_row
    )
    given, kept = attention_products(core, normed_all, attended_all, gp_mine, columns)
    mine_both = add(kept, swap_core(given))
    mine_both, xn_part = tied(mine_both, mm_nt(gp_mine, w_mine).astype(bf16))
    mine_sides = summed(exchanged(mine_both, ("z",))).astype(bf16)
    xn_of, out_of = rows_part(xn_part), ordered_part(out_near, out_far)
    xn_out = scattered(
        lambda step, flip: jnp.concatenate([xn_of(step, flip), out_of(step, flip)], axis=1),
        "y",
        "xl",
    )
    xn_out = sum(term.astype(f32) for term in xn_out)
    grad_xn = xn_out[:, :D]
    hidden_out = middle + xn_out[:, D:]
    sides = jnp.concatenate([ffn_sides, mine_sides], axis=2)
    side = lax.axis_index("xh")
    weight_sum = add(
        lax.dynamic_index_in_dim(sides, side, 0, keepdims=False),
        lax.ppermute(
            lax.dynamic_index_in_dim(sides, 1 - side, 0, keepdims=False), "xh", [(0, 1), (1, 0)]
        ),
    )
    resid = x_own.astype(f32)
    inv_first = lax.rsqrt(jnp.mean(resid * resid, axis=-1, keepdims=True) + eps)
    scaled = grad_xn * gains[:1]
    grad_in = (
        grad_middle
        + inv_first * scaled
        - resid * (inv_first**3) * jnp.mean(resid * scaled, axis=-1, keepdims=True)
    )

    own_gains = jnp.stack([jnp.pad(g.astype(f32), (0, 32)) for g in (mlp_gain, attn_gain)])
    grad_w_gate_up, grad_w_down, grad_w_qkv, grad_w_out, vectors = weight_gradients(
        gather_eight(weight_sum, "y", "xl"),
        w_gate_up,
        w_qkv,
        jnp.pad(own_gains, ((0, 6), (0, 0)), constant_values=1.0),
        fi,
    )
    grad_mlp_gain, grad_attn_gain, grad_b_qkv = vectors[0, :96], vectors[1, :96], vectors[2]

    return (
        hidden_out[None],
        grad_in[None],
        grad_attn_gain,
        grad_w_qkv,
        grad_b_qkv,
        grad_w_out,
        grad_mlp_gain,
        grad_w_gate_up,
        grad_w_down,
    )


def solution(mesh):
    fine = Mesh(mesh.devices.reshape(4, 2, 2, 4, 2), CTX + FSDP)
    rows = P(FSDP, CTX, None)
    vector = P(FSDP)
    matrix = P(FSDP, None)
    return jax.shard_map(
        shards,
        mesh=fine,
        in_specs=(rows, matrix, vector, matrix, vector, matrix, vector, matrix, matrix, rows),
        out_specs=(rows, rows, vector, matrix, vector, matrix, vector, matrix, matrix),
        check_vma=False,
    )
```

```python
import math

import jax
import jax.numpy as jnp
from jax import lax
from jax.experimental import pallas as pl
from jax.experimental.pallas import tpu as pltpu
from jax.sharding import Mesh, PartitionSpec as P

D = 1536
H = 12
KVH = 2
HD = 128
FF = 8960
PART = FF // 128
WIDE = 1152
MINE = 896

CTX = ("y", "xl")
FSDP = ("xh", "z", "core")

eps = 1e-06
rope_base = 1000000.0
masked_value = -1e30
bf16 = jnp.bfloat16
f32 = jnp.float32


def moved(block, ring, pair, step, flip):
    size = lax.axis_size(ring)
    if step == 0:
        return lax.ppermute(block, pair, [(0, 1), (1, 0)])
    return lax.ppermute(block, ring, [(i, (i + step) % size) for i in range(size)])


def halfway(rows):
    return rows // 32 * 16


def gather_stages(block, ring, pair, by_ring=False):
    half = halfway(block.shape[0])
    across, before, after_ = yield (
        moved(block, ring, pair, 0, 1),
        moved(block, ring, pair, 1, 0),
        moved(block, ring, pair, -1, 0),
    )
    far_first, far_second, across_before, across_after = yield (
        moved(before[:half], ring, pair, 1, 0),
        moved(after_[half:], ring, pair, -1, 0),
        moved(across, ring, pair, 1, 0),
        moved(across, ring, pair, -1, 0),
    )
    if by_ring:
        last = (
            moved(across_before[:half], ring, pair, 1, 0),
            moved(across_after[half:], ring, pair, -1, 0),
        )
    else:
        last = (moved(far_first, ring, pair, 0, 1), moved(far_second, ring, pair, 0, 1))
    across_far_first, across_far_second = yield last
    yield [
        (0, 0, 0, block),
        (0, 1, 0, across),
        (-1, 0, 0, before),
        (1, 0, 0, after_),
        (-1, 1, 0, across_before),
        (1, 1, 0, across_after),
        (2, 0, 0, far_first),
        (2, 0, half, far_second),
        (2, 1, 0, across_far_first),
        (2, 1, half, across_far_second),
    ]


def in_step(*gathers):
    states = [next(g) for g in gathers]
    for _ in range(3):
        if len(gathers) > 1:
            states = lax.optimization_barrier(states)
        states = [g.send(state) for g, state in zip(gathers, states)]
    return states


def gather_eight(block, ring, pair):
    return in_step(gather_stages(block, ring, pair))[0]


def place(ring, pair, ring_major, step, flip):
    size = lax.axis_size(ring)
    r = (lax.axis_index(ring) + step) % size
    q = lax.axis_index(pair)
    q = 1 - q if flip else q
    return r * 2 + q if ring_major else q * size + r


def places_of(got, ring, pair, ring_major):
    return [place(ring, pair, ring_major, step, flip) for step, flip, _, _ in got]


def pick_kernel(at_ref, weights, out):
    for c in range(8):

        @pl.when(at_ref[0] == c)
        def _():
            for part in range(2):
                for s in range(16):
                    start, to = part * FF + 560 * s + PART * c, part * WIDE + 72 * s
                    out[:, to : to + PART] = weights[:, start : start + PART]
                    out[:, to + PART : to + 72] = jnp.zeros((96, 2), bf16)


def picked(slice_index, weights):
    return call(
        pick_kernel,
        shaped((96, 2 * WIDE), bf16),
        (1,),
        [(weights, fixed(96, 2 * FF))],
        fixed(96, 2 * WIDE),
        mib=12,
        scalars=(slice_index.astype(jnp.int32)[None],),
        bytes_accessed=4 * 1024 * 1024,
    )


def folded(rows):
    rest = rows[:, WIDE:]
    rest = jnp.concatenate([rest[24 * k : 24 * (k + 1)] for k in range(3)], axis=1)
    return jnp.concatenate([rows[:, :WIDE], rest], axis=0)


def unfolded(rows):
    rest = jnp.concatenate([rows[72:, 384 * k : 384 * (k + 1)] for k in range(3)], axis=0)
    return jnp.concatenate([rows[:72], rest], axis=1)


def unfold_kernel(weights, out):
    out[0] = unfolded(weights[...].astype(f32)).astype(bf16)


def down_weights(w_ffn):
    return call(
        unfold_kernel,
        shaped((16, 72, D), bf16),
        (16,),
        [(w_ffn, pl.BlockSpec((96, WIDE), lambda s: (s, 2)))],
        pl.BlockSpec((1, 72, D), lambda s: (s, 0, 0)),
        bytes_accessed=8 * 1024 * 1024,
    ).reshape(WIDE, D)


def last_kernel(at_ref, *refs):
    pieces, weights, weights_qkv, gains = refs[:10], *refs[10:13]
    out, out_qkv, out_out, vectors, blocks, sums, bias = refs[13:]
    step = pl.program_id(0)
    for i in range(6):
        blocks[at_ref[i]] = pieces[i][...]
    for i in (6, 8):
        blocks[at_ref[i]] = jnp.where(step < 3, pieces[i][...], pieces[i + 1][...])
    total = jnp.zeros((16, 1), f32)
    for part in range(2):
        for shards in range(0, 16, 8):
            row = jnp.concatenate(
                [
                    blocks[c, :, part * WIDE + 72 * s : part * WIDE + 72 * s + PART]
                    for s in range(shards, shards + 8)
                    for c in range(8)
                ],
                axis=1,
            )
            start = part * FF + 560 * shards
            out[:, start : start + 4480] = row.astype(f32)
    for at in range(0, 2 * FF, 1792):
        lanes = slice(at, at + 1792)
        total = total + jnp.sum(
            out[:, lanes] * weights[:, lanes].astype(f32), axis=1, keepdims=True
        )
    rows = pl.ds(pl.multiple_of(step * 16, 16), 16)
    sums[0, rows] = jnp.broadcast_to(total, (16, HD))

    def whole(c, at, rows=slice(0, 16)):
        start = 3 * WIDE + at * HD
        return blocks[c, rows, start : start + HD].astype(f32)

    def heads(term):
        for y in range(4):
            yield 3 * y, term(2 * y, 0)
            yield 3 * y + 1, term(2 * y, 1) + term(2 * y + 1, 1)
            yield 3 * y + 2, term(2 * y + 1, 0)
        for kind in range(2):
            for group in range(2):
                yield 12 + 2 * kind + group, sum(term(4 * group + i, 2 + kind) for i in range(4))

    total = jnp.zeros((16, 1), f32)
    for h, value in heads(whole):
        lanes = slice(h * HD, (h + 1) * HD)
        out_qkv[:, lanes] = value
        total = total + jnp.sum(
            value * weights_qkv[:, lanes].astype(f32), axis=1, keepdims=True
        )
    sums[1, rows] = jnp.broadcast_to(total, (16, HD))
    for y in range(4):
        at = 3 * y * HD
        out_out[:, at : at + HD] = whole(2 * y, 4)
        out_out[:, at + HD : at + 2 * HD] = whole(2 * y, 5) + whole(2 * y + 1, 5)
        out_out[:, at + 2 * HD : at + 3 * HD] = whole(2 * y + 1, 4)

    @pl.when(step == 0)
    def _():
        for h, value in heads(lambda c, kind: whole(c, 6)[kind : kind + 1]):
            bias[h : h + 1] = value

    @pl.when(step == 5)
    def _():
        vectors[...] = jnp.zeros_like(vectors)
        for i in range(2):
            vectors[i : i + 1, :96] = sums[i].T[:1, :96] / gains[i : i + 1, :96]
        vectors[2:3] = bias[pl.ds(at_ref[10], 1)]


def last_down_kernel(at_ref, *refs):
    pieces, out, blocks = refs[:10], refs[10], refs[11]
    for i in range(6):
        blocks[at_ref[i]] = pieces[i][...].astype(f32)
    for i in (6, 8):
        blocks[at_ref[i], :48] = pieces[i][...].astype(f32)
        blocks[at_ref[i], 48:] = pieces[i + 1][...].astype(f32)
    for c in range(8):
        out[PART * c : PART * (c + 1)] = unfolded(blocks[c])[:PART]


def weight_gradients(got, weights, weights_qkv, gains, head):
    pieces = [g[3] for g in got]
    places = jnp.stack([*places_of(got, "y", "xl", True), head]).astype(jnp.int32)
    width = 3 * WIDE + MINE

    def rows(i, at):
        return i, 0

    maps = [rows] * 6 + [
        lambda i, at: (jnp.minimum(i, 2), 0),
        lambda i, at: (jnp.maximum(i - 3, 0), 0),
    ] * 2
    w_gate_up, w_qkv, w_out, vectors = call(
        last_kernel,
        [
            shaped((96, 2 * FF), f32),
            shaped((96, 2048), f32),
            shaped((96, D), f32),
            shaped((8, HD), f32),
        ],
        (6,),
        [(p, pl.BlockSpec((16, width), m)) for p, m in zip(pieces, maps)]
        + [
            (weights, pl.BlockSpec((16, 2 * FF), rows)),
            (weights_qkv, pl.BlockSpec((16, 2048), rows)),
            (gains, fixed(8, HD)),
        ],
        [
            pl.BlockSpec((16, 2 * FF), rows),
            pl.BlockSpec((16, 2048), rows),
            pl.BlockSpec((16, D), rows),
            fixed(8, HD),
        ],
        scalars=(places,),
        scratch=[
            pltpu.VMEM((8, 16, width), bf16),
            pltpu.VMEM((2, 96, HD), f32),
            pltpu.VMEM((16, HD), f32),
        ],
        mib=24,
        bytes_accessed=96 * 2 * FF * 8,
    )
    w_down = call(
        last_down_kernel,
        shaped((560, D), f32),
        (1,),
        [(p, pl.BlockSpec((p.shape[0], WIDE), lambda i, at: (0, 2))) for p in pieces],
        fixed(560, D),
        scalars=(places,),
        scratch=[pltpu.VMEM((8, 96, WIDE), f32)],
        mib=24,
        bytes_accessed=6 * 1024 * 1024,
    )
    return w_gate_up, w_down, w_qkv, w_out, vectors


def mine_kernel(at, normed, attended, grads, columns, given, kept):
    core = at[0]
    left = tn(normed[...], grads[...])
    right = tn(attended[...], columns[...])
    sums = jnp.sum(grads[...].astype(f32), axis=0, keepdims=True)
    bias = jnp.concatenate(
        [sums[:, i * HD : (i + 1) * HD] for i in range(4)] + [jnp.zeros((92, HD), f32)], axis=0
    )
    total = jnp.concatenate([left, right], axis=1).astype(bf16)
    bias = bias.astype(bf16)
    for p in range(2):
        even = total[192 * p : 192 * p + 96]
        odd = total[192 * p + 96 : 192 * (p + 1)]
        kept[p, 0, :, :768] = jnp.where(core == 0, even, odd)
        given[p, 0, :, :768] = jnp.where(core == 0, odd, even)
        kept[p, 0, :, 768:] = bias
        given[p, 0, :, 768:] = bias


def attention_products(core, normed, attended, grads, columns):
    out = pl.BlockSpec((2, 1, 96, MINE), lambda g, at: (g % 2, g // 2, 0, 0))
    return call(
        mine_kernel,
        [shaped((4, 2, 96, MINE), bf16)] * 2,
        (4,),
        [
            (normed, pl.BlockSpec((1024, 384), lambda g, at: (0, g))),
            (attended, pl.BlockSpec((1024, 384), lambda g, at: (0, g))),
            (grads, fixed(1024, 512)),
            (columns, fixed(1024, 256)),
        ],
        [out, out],
        scalars=(core.astype(jnp.int32)[None],),
        mib=24,
        flops=2 * 1024 * D * 768,
        bytes_accessed=10 * 1024 * 1024,
    )


def pack_kernel(at, weights, vectors, out):
    for i in range(4):
        out[:, i * HD : (i + 1) * HD] = weights[:, pl.ds(pl.multiple_of(at[i] * HD, HD), HD)]
    out[:, 4 * HD :] = jnp.concatenate([vectors[...], jnp.zeros((80, HD), bf16)], axis=0)


def packed_columns(heads, weights, vectors):
    rows = jnp.concatenate([jnp.stack(vectors), jnp.zeros((13, HD), bf16)], axis=0)
    return call(
        pack_kernel,
        shaped((96, 640), bf16),
        (1,),
        [(weights, fixed(96, 2048)), (rows, fixed(16, HD))],
        fixed(96, 640),
        scalars=(jnp.stack(heads).astype(jnp.int32),),
        bytes_accessed=2 * 1024 * 1024,
    )


def turned(field, cos_ref, sin_ref):
    return field * cos_ref + pltpu.roll(field, HD // 2, 1) * sin_ref


def nt(a, b):
    return lax.dot_general(a, b, (((1,), (1,)), ((), ())), preferred_element_type=f32)


def tn(a, b):
    return lax.dot_general(a, b, (((0,), (0,)), ((), ())), preferred_element_type=f32)


SCALE = 1.0 / math.sqrt(HD)


def attend_kernel(*refs):
    at, pieces, own, other, cos, sin, pos_col, pos_row = refs[0], refs[1:11], *refs[11:17]
    att, queries, lse, keys, values, normed, weights, gains, x, woven, proj = refs[17:]
    c, core, half = pl.program_id(0), at[10], at[11]

    @pl.when(c == 0)
    def _():
        for i, piece in enumerate(pieces):
            first = 64 if i in (7, 9) else 0
            x[at[i], first : first + piece.shape[0]] = piece[...]
        for i in range(8):
            index = 4 * (at[16] if i % 2 == 0 else 1 - at[16]) + i // 2
            woven[index, core] = own[i]
            woven[index, 1 - core] = other[i]
        gains[...] = jnp.zeros_like(gains)
        for s in range(16):
            weights[96 * s : 96 * (s + 1)] = woven[s // 2, s % 2, :, :512]
            rows = woven[s // 2, s % 2, :16, 512:].astype(f32)
            gains[0:2, 96 * s : 96 * (s + 1)] = rows[0:2, :96]
        bias = jnp.concatenate(
            [
                woven[at[12 + i] // 2, at[12 + i] % 2, :16, 512:].astype(f32)[2:3]
                for i in range(4)
            ],
            axis=1,
        )
        for i in range(8):
            rows = x[i].astype(f32)
            inv = lax.rsqrt(jnp.mean(rows * rows, axis=1, keepdims=True) + eps)
            normed[128 * i : 128 * (i + 1)] = (rows * inv * gains[0:1]).astype(bf16)
        proj[...] = jnp.dot(normed[...], weights[...], preferred_element_type=f32) + bias
        keys[...] = turned(proj[:, 2 * HD : 3 * HD], cos[...], sin[...]).astype(bf16)
        values[...] = proj[:, 3 * HD :].astype(bf16)

    rows = pl.ds(pl.multiple_of(c * 128, 128), 128)
    part = pl.ds(pl.multiple_of(c * 128 + half * 64, 64), 64)
    query = jnp.concatenate(
        [
            turned(proj[rows, :HD], cos[rows], sin[rows]),
            turned(proj[part, HD : 2 * HD], cos[part], sin[part]),
        ],
        axis=0,
    ).astype(bf16)
    queries[...] = query
    scores = nt(query, keys[...]) * SCALE
    seen = jnp.concatenate([pos_col[rows], pos_col[part]], axis=0) >= pos_row[...]
    scores = jnp.where(seen, scores, masked_value)
    row_max = jnp.max(scores, axis=1, keepdims=True)
    exponent = jnp.exp(scores - row_max)
    total = jnp.sum(exponent, axis=1, keepdims=True)
    probability = (exponent / total).astype(bf16)
    att[...] = jnp.dot(probability, values[...], preferred_element_type=f32).astype(bf16)
    lse[...] = jnp.broadcast_to(row_max + jnp.log(total), (192, HD))


def attend(x_got, own, core, half, heads, cos, sin, pos_col, pos_row):
    block = pl.BlockSpec((192, HD), lambda c, at: (c, 0))
    at = [*places_of(x_got, "y", "xl", True), core, half, *heads, lax.axis_index("xh")]
    at = jnp.stack(at).astype(jnp.int32)
    own = own.reshape(8, 96, 640)
    return call(
        attend_kernel,
        [
            shaped((1536, HD), bf16),
            shaped((1536, HD), bf16),
            shaped((1536, HD), f32),
            shaped((1024, HD), bf16),
            shaped((1024, HD), bf16),
            shaped((1024, D), bf16),
            shaped((D, 512), bf16),
            shaped((8, D), f32),
            shaped((8, 128, D), bf16),
        ],
        (8,),
        [(g[3], fixed(g[3].shape[0], D)) for g in x_got]
        + [
            (own, fixed(8, 96, 640)),
            (swap_core(own), fixed(8, 96, 640)),
            (cos, fixed(1024, HD)),
            (sin, fixed(1024, HD)),
            (pos_col, fixed(1024, 1)),
            (pos_row, fixed(1, 1024)),
        ],
        [
            block,
            block,
            block,
            fixed(1024, HD),
            fixed(1024, HD),
            fixed(1024, D),
            fixed(D, 512),
            fixed(8, D),
            fixed(8, 128, D),
        ],
        scalars=(at,),
        scratch=[
            pltpu.VMEM((8, 2, 96, 640), bf16),
            pltpu.VMEM((1024, 512), f32),
        ],
        mib=58,
        flops=4 * 1536 * 1024 * HD + 2 * 1024 * D * 512,
        bytes_accessed=14 * 1024 * 1024,
        exps=1536 * 1024,
    )


def attend_back_kernel(
    half_ref, got, queries, lse, keys, values, cos, sin, pos_col, pos_row, grads, columns, gk, gv
):
    c, half = pl.program_id(0), half_ref[0]

    @pl.when(c == 0)
    def _():
        gk[...] = jnp.zeros_like(gk)
        gv[...] = jnp.zeros_like(gv)

    rows = pl.ds(pl.multiple_of(c * 128, 128), 128)
    part = pl.ds(pl.multiple_of(c * 128 + half * 64, 64), 64)
    rest = pl.ds(pl.multiple_of(c * 128 + (1 - half) * 64, 64), 64)
    out = got[0, :192]
    query = queries[...]
    scores = nt(query, keys[...]) * SCALE
    seen = jnp.concatenate([pos_col[rows], pos_col[part]], axis=0) >= pos_row[...]
    scores = jnp.where(seen, scores, masked_value)
    probs = jnp.exp(scores - lse[:, :1])
    grad_prob = nt(out, values[...])
    inner = jnp.sum(probs * grad_prob, axis=1, keepdims=True)
    grad_scores = (probs * (grad_prob - inner)).astype(bf16)
    grad_query = jnp.dot(grad_scores, keys[...], preferred_element_type=f32) * SCALE
    gk[...] += tn(grad_scores, query)
    gv[...] += tn(probs.astype(bf16), out)
    grads[rows, :HD] = turned(grad_query[:128], cos[rows], -sin[rows]).astype(bf16)
    grads[part, HD : 2 * HD] = turned(grad_query[128:], cos[part], -sin[part]).astype(bf16)
    grads[rest, HD : 2 * HD] = jnp.zeros((64, HD), bf16)
    columns[:, :HD] = got[0, 192:320]
    columns[pl.ds(pl.multiple_of(half * 64, 64), 64), HD:] = got[0, 320:]
    columns[pl.ds(pl.multiple_of((1 - half) * 64, 64), 64), HD:] = jnp.zeros((64, HD), bf16)

    @pl.when(c == 7)
    def _():
        grads[:, 2 * HD : 3 * HD] = turned(gk[...] * SCALE, cos[...], -sin[...]).astype(bf16)
        grads[:, 3 * HD :] = gv[...].astype(bf16)


def attend_back(half, got, queries, lse, keys, values, cos, sin, pos_col, pos_row):
    block = pl.BlockSpec((192, HD), lambda c, half: (c, 0))
    return call(
        attend_back_kernel,
        [shaped((1024, 4 * HD), bf16), shaped((1024, 2 * HD), bf16)],
        (8,),
        [
            (got, pl.BlockSpec((1, 384, HD), lambda c, half: (c, 0, 0))),
            (queries, block),
            (lse, block),
            (keys, fixed(1024, HD)),
            (values, fixed(1024, HD)),
            (cos, fixed(1024, HD)),
            (sin, fixed(1024, HD)),
            (pos_col, fixed(1024, 1)),
            (pos_row, fixed(1, 1024)),
        ],
        [fixed(1024, 4 * HD), pl.BlockSpec((128, 2 * HD), lambda c, half: (c, 0))],
        scalars=(half,),
        scratch=[pltpu.VMEM((1024, HD), f32), pltpu.VMEM((1024, HD), f32)],
        mib=50,
        flops=10 * 1536 * 1024 * HD,
        bytes_accessed=6 * 1024 * 1024,
        exps=1536 * 1024,
    )


def place_kernel(*refs):
    pieces, out = refs[:10], refs[10]
    for i, piece in enumerate(pieces):
        at = 128 * (i if i < 6 else 6 + (i - 6) // 2) + (64 if i in (7, 9) else 0)
        out[at : at + piece.shape[0]] = piece[...]


def placed(got):
    return call(
        place_kernel,
        shaped((1024, D), bf16),
        (1,),
        [(g[3], pl.BlockSpec((g[3].shape[0], D), lambda i: (0, 1))) for g in got],
        fixed(1024, D),
        bytes_accessed=4 * 1024 * D,
    )


def middle_kernel(at, *refs):
    pieces, own, other, x_first, x_second, gains = refs[:10], *refs[10:15]
    attended, normed, middle, inverse, w_out, heads, both = refs[15:]
    step, core, side = pl.program_id(0), at[10], at[11]

    @pl.when(step == 0)
    def _():
        for i in range(8):
            index = 2 * (4 * (side if i % 2 == 0 else 1 - side) + i // 2)
            w_out[index + core] = own[i]
            w_out[index + 1 - core] = other[i]
        for i, piece in enumerate(pieces):
            first = 768 if i in (7, 9) else 0
            heads[at[i], first : first + piece.shape[0]] = piece[...]

    for k in range(2):
        block = at[12 + 2 * step + k]
        rows = pl.ds(pl.multiple_of(block * 192, 64), 128)
        part = pl.ds(pl.multiple_of(block * 192 + 128, 64), 64)
        for y in range(4):
            for q in range(2):
                whole, split = HD * (3 * y + 2 * q), HD * (3 * y + 1)
                half = slice(128 * k + 64 * q, 128 * k + 64 * (q + 1))
                both[128 * k : 128 * (k + 1), whole : whole + HD] = heads[2 * y + q, rows]
                both[half, split : split + HD] = heads[2 * y + q, part]
        attended[block] = both[128 * k : 128 * (k + 1)]
    weights = w_out[...].reshape(D, D)
    x = jnp.concatenate([x_first[0], x_second[0]], axis=0).astype(f32)
    mid = x + jnp.dot(both[...], weights, preferred_element_type=f32)
    inv = lax.rsqrt(jnp.mean(mid * mid, axis=1, keepdims=True) + eps)
    normed[...] = (mid * inv * gains[1:2]).astype(bf16)

    @pl.when(step == 0)
    def _():
        middle[...] = mid[:128]
        inverse[...] = jnp.broadcast_to(inv[:128], (128, HD))


def to_middle(got, own, core, side, x, gains):
    own = own.reshape(8, 96, D)
    order = [place("y", "xl", True, step, flip) for step, flip in ORDER]
    attended, *outs, w_out = call(
        middle_kernel,
        [
            shaped((8, 128, D), bf16),
            shaped((1024, D), bf16),
            shaped((128, D), f32),
            shaped((128, HD), f32),
            shaped((16, 96, D), bf16),
        ],
        (4,),
        [(g[3], fixed(*g[3].shape)) for g in got]
        + [
            (own, fixed(8, 96, D)),
            (swap_core(own), fixed(8, 96, D)),
            (x, pl.BlockSpec((1, 128, D), lambda b, at: (at[12 + 2 * b], 0, 0))),
            (x, pl.BlockSpec((1, 128, D), lambda b, at: (at[13 + 2 * b], 0, 0))),
            (gains, fixed(8, D)),
        ],
        [
            fixed(8, 128, D),
            pl.BlockSpec((256, D), lambda b, at: (b, 0)),
            fixed(128, D),
            fixed(128, HD),
            fixed(16, 96, D),
        ],
        scalars=(
            jnp.stack([*places_of(got, "y", "xl", True), core, side, *order]).astype(jnp.int32),
        ),
        scratch=[pltpu.VMEM((8, 1536, HD), bf16), pltpu.VMEM((256, D), bf16)],
        mib=48,
        flops=2 * 1024 * D * D,
        bytes_accessed=20 * 1024 * 1024,
    )
    return attended.reshape(1024, D), *outs, w_out.reshape(D, D)


def middle_back_kernel(a, b, c, d, middle, inverse, gain, cot, w_out, grad_middle, send):
    grad_hn = a[...].astype(f32) + b[...].astype(f32) + c[...].astype(f32) + d[...].astype(f32)
    inv, mid = inverse[:, :1], middle[...]
    scaled = grad_hn * gain[1:2]
    inner = jnp.mean(mid * scaled, axis=1, keepdims=True)
    grad = cot[...].astype(f32) + inv * scaled - mid * (inv * inv * inv * inner)
    grad_middle[...] = grad
    grad_attn = grad.astype(bf16)
    heads = nt(grad_attn, w_out[...]).astype(bf16)
    for y in range(4):
        for q in range(2):
            whole, split = HD * (3 * y + 2 * q), HD * (3 * y + 1)
            half = slice(64 * q, 64 * (q + 1))
            send[2 * y + q, :128] = heads[:, whole : whole + HD]
            send[2 * y + q, 128:192] = heads[half, split : split + HD]
            send[2 * y + q, 192:320] = grad_attn[:, whole : whole + HD]
            send[2 * y + q, 320:] = grad_attn[half, split : split + HD]


def middle_back(parts, middle, inverse, gain, cot, w_out):
    row = fixed(128, D)
    return call(
        middle_back_kernel,
        [shaped((128, D), f32), shaped((8, 384, HD), bf16)],
        (1,),
        [(p, row) for p in parts]
        + [
            (middle, row),
            (inverse, fixed(128, HD)),
            (gain, fixed(8, D)),
            (cot, row),
            (w_out, fixed(D, D)),
        ],
        [row, fixed(8, 384, HD)],
        mib=50,
        flops=2 * 128 * D * D,
        bytes_accessed=10 * 1024 * 1024,
    )


def down_product_kernel(hidden_near, hidden_far, cot_near, cot_far, out):
    product = tn(hidden_near[...], cot_near[...]) + tn(hidden_far[...], cot_far[...])
    for s in range(16):
        out[s % 8, s // 8] = folded(product[72 * s : 72 * (s + 1)]).astype(bf16)


def gate_up_product_kernel(nm_near, nm_far, gate_near, gate_far, up_near, up_far, _, out):
    near, far = nm_near[...].T, nm_far[...].T
    for j, (a, b) in enumerate(((gate_near, gate_far), (up_near, up_far))):
        total = jnp.dot(near, a[...], preferred_element_type=f32)
        total = total + jnp.dot(far, b[...], preferred_element_type=f32)
        for i in range(4):
            rows = total[96 * i : 96 * (i + 1)]
            out[i, 0, :, j * WIDE : (j + 1) * WIDE] = rows.astype(bf16)


def down_product(cot, hidden):
    return call(
        down_product_kernel,
        shaped((8, 2, 96, 3 * WIDE), bf16),
        (1,),
        [(a, fixed(512, WIDE)) for a in hidden]
        + [
            (cot, pl.BlockSpec((512, D), lambda t: (0, 0))),
            (cot, pl.BlockSpec((512, D), lambda t: (1, 0))),
        ],
        pl.BlockSpec((8, 2, 96, WIDE), lambda t: (0, 0, 0, 2)),
        mib=56,
        flops=2 * 1024 * D * WIDE,
        bytes_accessed=10 * 1024 * 1024,
    )


def gate_up_product(nm, gate, up, parts):
    return call(
        gate_up_product_kernel,
        shaped((8, 2, 96, 3 * WIDE), bf16),
        (4,),
        [
            (nm, pl.BlockSpec((512, 384), lambda g: (0, g))),
            (nm, pl.BlockSpec((512, 384), lambda g: (1, g))),
        ]
        + [(a, fixed(512, WIDE)) for pair in (gate, up) for a in pair]
        + [(parts, pl.BlockSpec(memory_space=pl.ANY))],
        pl.BlockSpec((4, 1, 96, 2 * WIDE), lambda g: (g % 2, g // 2, 0, 0)),
        aliases={6: 0},
        mib=56,
        flops=2 * 1024 * D * 2 * WIDE,
        bytes_accessed=20 * 1024 * 1024,
    )


def feed_forward_kernel(
    nm, cot, w_gate, w_up, w_dn, hidden, grad_gate, grad_up, hn, total
):
    step = pl.program_id(0)
    gate = jnp.dot(nm[...], w_gate[...], preferred_element_type=f32)
    up = jnp.dot(nm[...], w_up[...], preferred_element_type=f32)
    act = nt(cot[...], w_dn[...])
    sigmoid_gate = jax.nn.sigmoid(gate)
    silu_gate = gate * sigmoid_gate
    hidden[...] = (silu_gate * up).astype(bf16)
    to_gate = (act * up * (sigmoid_gate * (1.0 + gate * (1.0 - sigmoid_gate)))).astype(bf16)
    to_up = (act * silu_gate).astype(bf16)
    grad_gate[...] = to_gate
    grad_up[...] = to_up
    term = nt(to_gate, w_gate[...]) + nt(to_up, w_up[...])

    @pl.when(step == 0)
    def _():
        total[...] = term

    @pl.when(step > 0)
    def _():
        total[...] += term

    @pl.when(step == 2)
    def _():
        hn[...] = total[...].astype(bf16)


def feed_forward(nm, cot, w_ffn, w_dn, half):
    whole, column = fixed(512, D), pl.BlockSpec((512, 384), lambda j: (0, j))
    narrow = shaped((512, WIDE), bf16)
    rows = pl.BlockSpec((512, D), lambda j: (half, 0))
    return call(
        feed_forward_kernel,
        [narrow, narrow, narrow, shaped((512, D), bf16)],
        (3,),
        [
            (nm, rows),
            (cot, rows),
            (w_ffn, pl.BlockSpec((D, 384), lambda j: (0, j))),
            (w_ffn, pl.BlockSpec((D, 384), lambda j: (0, 3 + j))),
            (w_dn, pl.BlockSpec((384, D), lambda j: (j, 0))),
        ],
        [column, column, column, whole],
        scratch=[pltpu.VMEM((512, D), f32)],
        mib=36,
        flops=2 * 512 * D * 5 * WIDE,
        bytes_accessed=20 * 1024 * 1024,
        exps=512 * WIDE,
    )


def add(a, *others):
    total = a.astype(f32)
    for other in others:
        total = total + other.astype(f32)
    return total.astype(bf16)


def scatter_stages(part, ring, pair):
    away = part(2, 1)
    half = halfway(away.shape[0])
    away, from_after, from_before = yield (
        moved(away, ring, pair, 0, 1),
        moved(part(-1, 1), ring, pair, -1, 0),
        moved(part(1, 1), ring, pair, 1, 0),
    )
    away = add(part(2, 0), away)
    away_first, away_second, got_across = yield (
        moved(away[:half], ring, pair, -1, 0),
        moved(away[half:], ring, pair, 1, 0),
        moved(add(part(0, 1), from_after, from_before), ring, pair, 0, 1),
    )
    back, ahead = part(-1, 0), part(1, 0)
    back = jnp.concatenate([add(back[:half], away_first), back[half:]], axis=0)
    ahead = jnp.concatenate([ahead[:half], add(ahead[half:], away_second)], axis=0)
    got = yield moved(back, ring, pair, -1, 0), moved(ahead, ring, pair, 1, 0)
    yield part(0, 0), got_across, *got


def scattered(part, ring, pair):
    stages = scatter_stages(part, ring, pair)
    state = next(stages)
    for _ in range(3):
        state = stages.send(state)
    return state


ORDER = [(0, 0), (0, 1), (-1, 0), (1, 0), (-1, 1), (1, 1), (2, 0), (2, 1)]


def rows_part(array):
    def part(step, flip):
        at = place("y", "xl", True, step, flip)
        return lax.dynamic_slice_in_dim(array, at * 128, 128, 0)

    return part


def ordered_part(near, far):
    def part(step, flip):
        i = ORDER.index((step, flip))
        return (near, far)[i // 4][i % 4 * 128 : (i % 4 + 1) * 128]

    return part


def tied(*values):
    return lax.optimization_barrier(values)


def call(
    kernel,
    out,
    grid,
    ins,
    outs,
    scalars=(),
    scratch=(),
    aliases=None,
    mib=16,
    flops=0,
    bytes_accessed=0,
    exps=0,
):
    return pl.pallas_call(
        kernel,
        grid_spec=pltpu.PrefetchScalarGridSpec(
            num_scalar_prefetch=len(scalars),
            grid=grid,
            in_specs=[spec for _, spec in ins],
            out_specs=outs,
            scratch_shapes=scratch,
        ),
        out_shape=out,
        input_output_aliases=aliases or {},
        compiler_params=pltpu.CompilerParams(vmem_limit_bytes=mib * 1024 * 1024),
        cost_estimate=pl.CostEstimate(
            flops=flops, bytes_accessed=bytes_accessed, transcendentals=exps
        ),
    )(*scalars, *[array for array, _ in ins])


def fixed(*shape):
    return pl.BlockSpec(shape, lambda *_: (0,) * len(shape))


def shaped(shape, dtype):
    return jax.ShapeDtypeStruct(shape, dtype)


def exchanged(blocks, axes):
    return lax.all_to_all(blocks, axes, 0, 0, tiled=True)


def swap_core(block):
    return lax.ppermute(block, "core", [(0, 1), (1, 0)])


def summed(pieces):
    return jnp.sum(pieces.astype(f32), axis=0)


def mm(a, b):
    return jnp.dot(a, b, preferred_element_type=f32)


def mm_nt(a, b):
    return jnp.einsum("ik,jk->ij", a, b, preferred_element_type=f32)


def mm_tn(a, b):
    return jnp.einsum("ki,kj->ij", a, b, preferred_element_type=f32)


def shards(
    hidden_in, block_order, attn_gain, w_qkv, b_qkv, w_out, mlp_gain, w_gate_up, w_down, cotangent
):
    yi, qi = lax.axis_index("y"), lax.axis_index("xl")
    ci = 2 * yi + qi
    fi = lax.axis_index(FSDP)
    core = lax.axis_index("core")
    group = yi // 2
    half = qi.astype(jnp.int32)[None]
    x_own, cot_own = hidden_in[0], cotangent[0]

    heads = [3 * yi + 2 * qi, 3 * yi + 1, H + group, H + KVH + group]
    vectors = [jnp.pad(attn_gain, (0, 32)), jnp.pad(mlp_gain, (0, 32)), b_qkv]
    packed = packed_columns(heads, w_qkv, vectors)

    order = block_order[0]
    positions = (order[:, None] * 64 + jnp.arange(64, dtype=jnp.int32)[None, :]).reshape(1024)
    frequency = jnp.exp(jnp.arange(0, HD, 2, dtype=f32) * (-math.log(rope_base) / HD))
    angles = positions.astype(f32)[:, None] * frequency[None, :]
    cosine, sine = jnp.cos(angles), jnp.sin(angles)
    cosine = jnp.concatenate([cosine, cosine], axis=1)
    sine = jnp.concatenate([-sine, sine], axis=1)
    pos_col, pos_row = positions[:, None], positions[None, :]

    def both_sides(block):
        return jnp.stack([block, lax.ppermute(block, "xh", [(0, 1), (1, 0)])])

    def along_z(sides):
        return exchanged(jnp.broadcast_to(sides, (4,) + sides.shape), ("z",))

    packed = both_sides(packed)
    w_out = both_sides(w_out)
    x_gather = gather_stages(jnp.concatenate([x_own, cot_own], axis=1), "y", "xl", True)
    *x_state, packed, w_down, w_gate_up_later, cosine, sine = tied(
        *next(x_gather), packed, w_down, w_gate_up, cosine, sine
    )
    own = along_z(packed)
    *x_state, own, w_out = tied(*x_gather.send(x_state), own, w_out)
    own_out = along_z(w_out)
    x_got = x_gather.send(x_gather.send(x_state))

    down = lax.dynamic_slice_in_dim(w_down, PART * ci, PART, 0)
    down = folded(jnp.concatenate([down, jnp.zeros((2, D), bf16)], axis=0))
    ffn_own = jnp.concatenate([picked(ci, w_gate_up_later), down], axis=1)
    w_ffn = lax.all_gather(ffn_own, FSDP, axis=0, tiled=True)

    att_mine, queries, lse, keys, values, normed_all, w_mine, gains, x_all = attend(
        x_got, own, core, qi, heads, cosine, sine, pos_col, pos_row
    )
    att_gather = gather_stages(att_mine, "y", "xl")
    *att_state, cot_all = tied(*next(att_gather), placed(x_got))
    *att_state, own_out, w_dn = tied(*att_gather.send(att_state), own_out, down_weights(w_ffn))
    att_got = att_gather.send(att_gather.send(att_state))
    attended_all, nm_all, middle, inv_second, w_out_all = to_middle(
        att_got, own_out, core, lax.axis_index("xh"), x_all, gains
    )

    hidden_far, gate_far, up_far, hn_far = feed_forward(nm_all, cot_all, w_ffn, w_dn, 1)
    hidden_near, gate_near, up_near, hn_near = feed_forward(nm_all, cot_all, w_ffn, w_dn, 0)
    hn_stages = scatter_stages(ordered_part(hn_near, hn_far), "y", "xl")
    *state, cot_all, hidden_near, hidden_far = tied(
        *next(hn_stages), cot_all, hidden_near, hidden_far
    )
    ffn_parts = down_product(cot_all, (hidden_near, hidden_far))
    *state, nm_all, gate_near, gate_far, up_near, up_far = tied(
        *hn_stages.send(state), nm_all, gate_near, gate_far, up_near, up_far
    )
    ffn_parts = gate_up_product(nm_all, (gate_near, gate_far), (up_near, up_far), ffn_parts)
    ffn_sides = lax.psum_scatter(ffn_parts, ("z", "core"), scatter_dimension=0, tiled=True)[0]
    hn_parts = hn_stages.send(hn_stages.send(state))
    *hn_parts, out_near, out_far = tied(
        *hn_parts, mm(hidden_near, w_dn).astype(bf16), mm(hidden_far, w_dn).astype(bf16)
    )

    grad_middle, send = middle_back(hn_parts, middle, inv_second, gains, cot_own, w_out_all)
    got = exchanged(send, CTX)
    gp_mine, columns = attend_back(
        half, got, queries, lse, keys, values, cosine, sine, pos_col, pos_row
    )
    given, kept = attention_products(core, normed_all, attended_all, gp_mine, columns)
    mine_both = add(kept, swap_core(given))
    mine_both, xn_part = tied(mine_both, mm_nt(gp_mine, w_mine).astype(bf16))
    mine_sides = summed(exchanged(mine_both, ("z",))).astype(bf16)
    xn_of, out_of = rows_part(xn_part), ordered_part(out_near, out_far)
    xn_out = scattered(
        lambda step, flip: jnp.concatenate([xn_of(step, flip), out_of(step, flip)], axis=1),
        "y",
        "xl",
    )
    xn_out = sum(term.astype(f32) for term in xn_out)
    grad_xn = xn_out[:, :D]
    hidden_out = middle + xn_out[:, D:]
    sides = jnp.concatenate([ffn_sides, mine_sides], axis=2)
    side = lax.axis_index("xh")
    weight_sum = add(
        lax.dynamic_index_in_dim(sides, side, 0, keepdims=False),
        lax.ppermute(
            lax.dynamic_index_in_dim(sides, 1 - side, 0, keepdims=False), "xh", [(0, 1), (1, 0)]
        ),
    )
    resid = x_own.astype(f32)
    inv_first = lax.rsqrt(jnp.mean(resid * resid, axis=-1, keepdims=True) + eps)
    scaled = grad_xn * gains[:1]
    grad_in = (
        grad_middle
        + inv_first * scaled
        - resid * (inv_first**3) * jnp.mean(resid * scaled, axis=-1, keepdims=True)
    )

    own_gains = jnp.stack([jnp.pad(g.astype(f32), (0, 32)) for g in (mlp_gain, attn_gain)])
    grad_w_gate_up, grad_w_down, grad_w_qkv, grad_w_out, vectors = weight_gradients(
        gather_eight(weight_sum, "y", "xl"),
        w_gate_up,
        w_qkv,
        jnp.pad(own_gains, ((0, 6), (0, 0)), constant_values=1.0),
        fi,
    )
    grad_mlp_gain, grad_attn_gain, grad_b_qkv = vectors[0, :96], vectors[1, :96], vectors[2]

    return (
        hidden_out[None],
        grad_in[None],
        grad_attn_gain,
        grad_w_qkv,
        grad_b_qkv,
        grad_w_out,
        grad_mlp_gain,
        grad_w_gate_up,
        grad_w_down,
    )


def solution(mesh):
    fine = Mesh(mesh.devices.reshape(4, 2, 2, 4, 2), CTX + FSDP)
    rows = P(FSDP, CTX, None)
    vector = P(FSDP)
    matrix = P(FSDP, None)
    return jax.shard_map(
        shards,
        mesh=fine,
        in_specs=(rows, matrix, vector, matrix, vector, matrix, vector, matrix, matrix, rows),
        out_specs=(rows, rows, vector, matrix, vector, matrix, vector, matrix, matrix),
        check_vma=False,
    )
```

```python
import math

import jax
import jax.numpy as jnp
from jax import lax
from jax.experimental import pallas as pl
from jax.experimental.pallas import tpu as pltpu
from jax.sharding import Mesh, PartitionSpec as P

D = 1536
H = 12
KVH = 2
HD = 128
FF = 8960
PART = FF // 128
WIDE = 1152
MINE = 896

CTX = ("y", "xl")
FSDP = ("xh", "z", "core")

eps = 1e-06
rope_base = 1000000.0
masked_value = -1e30
bf16 = jnp.bfloat16
f32 = jnp.float32


def moved(block, ring, pair, step, flip):
    size = lax.axis_size(ring)
    if step == 0:
        return lax.ppermute(block, pair, [(0, 1), (1, 0)])
    return lax.ppermute(block, ring, [(i, (i + step) % size) for i in range(size)])


def halfway(rows):
    return rows // 32 * 16


def gather_stages(block, ring, pair, by_ring=False):
    half = halfway(block.shape[0])
    across, before, after_ = yield (
        moved(block, ring, pair, 0, 1),
        moved(block, ring, pair, 1, 0),
        moved(block, ring, pair, -1, 0),
    )
    far_first, far_second, across_before, across_after = yield (
        moved(before[:half], ring, pair, 1, 0),
        moved(after_[half:], ring, pair, -1, 0),
        moved(across, ring, pair, 1, 0),
        moved(across, ring, pair, -1, 0),
    )
    if by_ring:
        last = (
            moved(across_before[:half], ring, pair, 1, 0),
            moved(across_after[half:], ring, pair, -1, 0),
        )
    else:
        last = (moved(far_first, ring, pair, 0, 1), moved(far_second, ring, pair, 0, 1))
    across_far_first, across_far_second = yield last
    yield [
        (0, 0, 0, block),
        (0, 1, 0, across),
        (-1, 0, 0, before),
        (1, 0, 0, after_),
        (-1, 1, 0, across_before),
        (1, 1, 0, across_after),
        (2, 0, 0, far_first),
        (2, 0, half, far_second),
        (2, 1, 0, across_far_first),
        (2, 1, half, across_far_second),
    ]


def in_step(*gathers):
    states = [next(g) for g in gathers]
    for _ in range(3):
        if len(gathers) > 1:
            states = lax.optimization_barrier(states)
        states = [g.send(state) for g, state in zip(gathers, states)]
    return states


def gather_eight(block, ring, pair):
    return in_step(gather_stages(block, ring, pair))[0]


def place(ring, pair, ring_major, step, flip):
    size = lax.axis_size(ring)
    r = (lax.axis_index(ring) + step) % size
    q = lax.axis_index(pair)
    q = 1 - q if flip else q
    return r * 2 + q if ring_major else q * size + r


def places_of(got, ring, pair, ring_major):
    return [place(ring, pair, ring_major, step, flip) for step, flip, _, _ in got]


def pick_kernel(at_ref, weights, out):
    for c in range(8):

        @pl.when(at_ref[0] == c)
        def _():
            for part in range(2):
                for s in range(16):
                    start, to = part * FF + 560 * s + PART * c, part * WIDE + 72 * s
                    out[:, to : to + PART] = weights[:, start : start + PART]
                    out[:, to + PART : to + 72] = jnp.zeros((96, 2), bf16)


def picked(slice_index, weights):
    return call(
        pick_kernel,
        shaped((96, 2 * WIDE), bf16),
        (1,),
        [(weights, fixed(96, 2 * FF))],
        fixed(96, 2 * WIDE),
        mib=12,
        scalars=(slice_index.astype(jnp.int32)[None],),
        bytes_accessed=4 * 1024 * 1024,
    )


def folded(rows):
    rest = rows[:, WIDE:]
    rest = jnp.concatenate([rest[24 * k : 24 * (k + 1)] for k in range(3)], axis=1)
    return jnp.concatenate([rows[:, :WIDE], rest], axis=0)


def unfolded(rows):
    rest = jnp.concatenate([rows[72:, 384 * k : 384 * (k + 1)] for k in range(3)], axis=0)
    return jnp.concatenate([rows[:72], rest], axis=1)


def unfold_kernel(weights, out):
    out[0] = unfolded(weights[...].astype(f32)).astype(bf16)


def down_weights(w_ffn):
    return call(
        unfold_kernel,
        shaped((16, 72, D), bf16),
        (16,),
        [(w_ffn, pl.BlockSpec((96, WIDE), lambda s: (s, 2)))],
        pl.BlockSpec((1, 72, D), lambda s: (s, 0, 0)),
        bytes_accessed=8 * 1024 * 1024,
    ).reshape(WIDE, D)


def last_kernel(at_ref, *refs):
    pieces, weights, weights_qkv, gains = refs[:10], *refs[10:13]
    out, out_qkv, out_out, vectors, blocks, sums, bias = refs[13:]
    step = pl.program_id(0)
    for i in range(6):
        blocks[at_ref[i]] = pieces[i][...]
    for i in (6, 8):
        blocks[at_ref[i]] = jnp.where(step < 3, pieces[i][...], pieces[i + 1][...])
    total = jnp.zeros((16, 1), f32)
    for part in range(2):
        for shards in range(0, 16, 8):
            row = jnp.concatenate(
                [
                    blocks[c, :, part * WIDE + 72 * s : part * WIDE + 72 * s + PART]
                    for s in range(shards, shards + 8)
                    for c in range(8)
                ],
                axis=1,
            )
            start = part * FF + 560 * shards
            out[:, start : start + 4480] = row.astype(f32)
    for at in range(0, 2 * FF, 1792):
        lanes = slice(at, at + 1792)
        total = total + jnp.sum(
            out[:, lanes] * weights[:, lanes].astype(f32), axis=1, keepdims=True
        )
    rows = pl.ds(pl.multiple_of(step * 16, 16), 16)
    sums[0, rows] = jnp.broadcast_to(total, (16, HD))

    def whole(c, at, rows=slice(0, 16)):
        start = 3 * WIDE + at * HD
        return blocks[c, rows, start : start + HD].astype(f32)

    def heads(term):
        for y in range(4):
            yield 3 * y, term(2 * y, 0)
            yield 3 * y + 1, term(2 * y, 1) + term(2 * y + 1, 1)
            yield 3 * y + 2, term(2 * y + 1, 0)
        for kind in range(2):
            for group in range(2):
                yield 12 + 2 * kind + group, sum(term(4 * group + i, 2 + kind) for i in range(4))

    total = jnp.zeros((16, 1), f32)
    for h, value in heads(whole):
        lanes = slice(h * HD, (h + 1) * HD)
        out_qkv[:, lanes] = value
        total = total + jnp.sum(
            value * weights_qkv[:, lanes].astype(f32), axis=1, keepdims=True
        )
    sums[1, rows] = jnp.broadcast_to(total, (16, HD))
    for y in range(4):
        at = 3 * y * HD
        out_out[:, at : at + HD] = whole(2 * y, 4)
        out_out[:, at + HD : at + 2 * HD] = whole(2 * y, 5) + whole(2 * y + 1, 5)
        out_out[:, at + 2 * HD : at + 3 * HD] = whole(2 * y + 1, 4)

    @pl.when(step == 0)
    def _():
        for h, value in heads(lambda c, kind: whole(c, 6)[kind : kind + 1]):
            bias[h : h + 1] = value

    @pl.when(step == 5)
    def _():
        vectors[...] = jnp.zeros_like(vectors)
        for i in range(2):
            vectors[i : i + 1, :96] = sums[i].T[:1, :96] / gains[i : i + 1, :96]
        vectors[2:3] = bias[pl.ds(at_ref[10], 1)]


def last_down_kernel(at_ref, *refs):
    pieces, out, blocks = refs[:10], refs[10], refs[11]
    for i in range(6):
        blocks[at_ref[i]] = pieces[i][...].astype(f32)
    for i in (6, 8):
        blocks[at_ref[i], :48] = pieces[i][...].astype(f32)
        blocks[at_ref[i], 48:] = pieces[i + 1][...].astype(f32)
    for c in range(8):
        out[PART * c : PART * (c + 1)] = unfolded(blocks[c])[:PART]


def weight_gradients(got, weights, weights_qkv, gains, head):
    pieces = [g[3] for g in got]
    places = jnp.stack([*places_of(got, "y", "xl", True), head]).astype(jnp.int32)
    width = 3 * WIDE + MINE

    def rows(i, at):
        return i, 0

    maps = [rows] * 6 + [
        lambda i, at: (jnp.minimum(i, 2), 0),
        lambda i, at: (jnp.maximum(i - 3, 0), 0),
    ] * 2
    w_gate_up, w_qkv, w_out, vectors = call(
        last_kernel,
        [
            shaped((96, 2 * FF), f32),
            shaped((96, 2048), f32),
            shaped((96, D), f32),
            shaped((8, HD), f32),
        ],
        (6,),
        [(p, pl.BlockSpec((16, width), m)) for p, m in zip(pieces, maps)]
        + [
            (weights, pl.BlockSpec((16, 2 * FF), rows)),
            (weights_qkv, pl.BlockSpec((16, 2048), rows)),
            (gains, fixed(8, HD)),
        ],
        [
            pl.BlockSpec((16, 2 * FF), rows),
            pl.BlockSpec((16, 2048), rows),
            pl.BlockSpec((16, D), rows),
            fixed(8, HD),
        ],
        scalars=(places,),
        scratch=[
            pltpu.VMEM((8, 16, width), bf16),
            pltpu.VMEM((2, 96, HD), f32),
            pltpu.VMEM((16, HD), f32),
        ],
        mib=24,
        bytes_accessed=96 * 2 * FF * 8,
    )
    w_down = call(
        last_down_kernel,
        shaped((560, D), f32),
        (1,),
        [(p, pl.BlockSpec((p.shape[0], WIDE), lambda i, at: (0, 2))) for p in pieces],
        fixed(560, D),
        scalars=(places,),
        scratch=[pltpu.VMEM((8, 96, WIDE), f32)],
        mib=24,
        bytes_accessed=6 * 1024 * 1024,
    )
    return w_gate_up, w_down, w_qkv, w_out, vectors


def mine_kernel(at, normed, attended, grads, columns, given, kept):
    core = at[0]
    left = tn(normed[...], grads[...])
    right = tn(attended[...], columns[...])
    sums = jnp.sum(grads[...].astype(f32), axis=0, keepdims=True)
    bias = jnp.concatenate(
        [sums[:, i * HD : (i + 1) * HD] for i in range(4)] + [jnp.zeros((92, HD), f32)], axis=0
    )
    total = jnp.concatenate([left, right], axis=1).astype(bf16)
    bias = bias.astype(bf16)
    for p in range(2):
        even = total[192 * p : 192 * p + 96]
        odd = total[192 * p + 96 : 192 * (p + 1)]
        kept[p, 0, :, :768] = jnp.where(core == 0, even, odd)
        given[p, 0, :, :768] = jnp.where(core == 0, odd, even)
        kept[p, 0, :, 768:] = bias
        given[p, 0, :, 768:] = bias


def attention_products(core, normed, attended, grads, columns):
    out = pl.BlockSpec((2, 1, 96, MINE), lambda g, at: (g % 2, g // 2, 0, 0))
    return call(
        mine_kernel,
        [shaped((4, 2, 96, MINE), bf16)] * 2,
        (4,),
        [
            (normed, pl.BlockSpec((1024, 384), lambda g, at: (0, g))),
            (attended, pl.BlockSpec((1024, 384), lambda g, at: (0, g))),
            (grads, fixed(1024, 512)),
            (columns, fixed(1024, 256)),
        ],
        [out, out],
        scalars=(core.astype(jnp.int32)[None],),
        mib=24,
        flops=2 * 1024 * D * 768,
        bytes_accessed=10 * 1024 * 1024,
    )


def pack_kernel(at, weights, vectors, out):
    for i in range(4):
        out[:, i * HD : (i + 1) * HD] = weights[:, pl.ds(pl.multiple_of(at[i] * HD, HD), HD)]
    out[:, 4 * HD :] = jnp.concatenate([vectors[...], jnp.zeros((80, HD), bf16)], axis=0)


def packed_columns(heads, weights, vectors):
    rows = jnp.concatenate([jnp.stack(vectors), jnp.zeros((13, HD), bf16)], axis=0)
    return call(
        pack_kernel,
        shaped((96, 640), bf16),
        (1,),
        [(weights, fixed(96, 2048)), (rows, fixed(16, HD))],
        fixed(96, 640),
        scalars=(jnp.stack(heads).astype(jnp.int32),),
        bytes_accessed=2 * 1024 * 1024,
    )


def turned(field, cos_ref, sin_ref):
    return field * cos_ref + pltpu.roll(field, HD // 2, 1) * sin_ref


def nt(a, b):
    return lax.dot_general(a, b, (((1,), (1,)), ((), ())), preferred_element_type=f32)


def tn(a, b):
    return lax.dot_general(a, b, (((0,), (0,)), ((), ())), preferred_element_type=f32)


SCALE = 1.0 / math.sqrt(HD)


def attend_kernel(*refs):
    at, pieces, own, other, cos, sin, pos_col, pos_row = refs[0], refs[1:11], *refs[11:17]
    att, queries, lse, keys, values, normed, weights, gains, x, woven, proj = refs[17:]
    c, core, half = pl.program_id(0), at[10], at[11]

    @pl.when(c == 0)
    def _():
        for i, piece in enumerate(pieces):
            first = 64 if i in (7, 9) else 0
            x[at[i], first : first + piece.shape[0]] = piece[...]
        for i in range(8):
            index = 4 * (at[16] if i % 2 == 0 else 1 - at[16]) + i // 2
            woven[index, core] = own[i]
            woven[index, 1 - core] = other[i]
        gains[...] = jnp.zeros_like(gains)
        for s in range(16):
            weights[96 * s : 96 * (s + 1)] = woven[s // 2, s % 2, :, :512]
            rows = woven[s // 2, s % 2, :16, 512:].astype(f32)
            gains[0:2, 96 * s : 96 * (s + 1)] = rows[0:2, :96]
        bias = jnp.concatenate(
            [
                woven[at[12 + i] // 2, at[12 + i] % 2, :16, 512:].astype(f32)[2:3]
                for i in range(4)
            ],
            axis=1,
        )
        for i in range(8):
            rows = x[i].astype(f32)
            inv = lax.rsqrt(jnp.mean(rows * rows, axis=1, keepdims=True) + eps)
            normed[128 * i : 128 * (i + 1)] = (rows * inv * gains[0:1]).astype(bf16)
        proj[...] = jnp.dot(normed[...], weights[...], preferred_element_type=f32) + bias
        keys[...] = turned(proj[:, 2 * HD : 3 * HD], cos[...], sin[...]).astype(bf16)
        values[...] = proj[:, 3 * HD :].astype(bf16)

    rows = pl.ds(pl.multiple_of(c * 128, 128), 128)
    part = pl.ds(pl.multiple_of(c * 128 + half * 64, 64), 64)
    query = jnp.concatenate(
        [
            turned(proj[rows, :HD], cos[rows], sin[rows]),
            turned(proj[part, HD : 2 * HD], cos[part], sin[part]),
        ],
        axis=0,
    ).astype(bf16)
    queries[...] = query
    scores = nt(query, keys[...]) * SCALE
    seen = jnp.concatenate([pos_col[rows], pos_col[part]], axis=0) >= pos_row[...]
    scores = jnp.where(seen, scores, masked_value)
    row_max = jnp.max(scores, axis=1, keepdims=True)
    exponent = jnp.exp(scores - row_max)
    total = jnp.sum(exponent, axis=1, keepdims=True)
    probability = (exponent / total).astype(bf16)
    att[...] = jnp.dot(probability, values[...], preferred_element_type=f32).astype(bf16)
    lse[...] = jnp.broadcast_to(row_max + jnp.log(total), (192, HD))


def attend(x_got, own, core, half, heads, cos, sin, pos_col, pos_row):
    block = pl.BlockSpec((192, HD), lambda c, at: (c, 0))
    at = [*places_of(x_got, "y", "xl", True), core, half, *heads, lax.axis_index("xh")]
    at = jnp.stack(at).astype(jnp.int32)
    own = own.reshape(8, 96, 640)
    return call(
        attend_kernel,
        [
            shaped((1536, HD), bf16),
            shaped((1536, HD), bf16),
            shaped((1536, HD), f32),
            shaped((1024, HD), bf16),
            shaped((1024, HD), bf16),
            shaped((1024, D), bf16),
            shaped((D, 512), bf16),
            shaped((8, D), f32),
            shaped((8, 128, D), bf16),
        ],
        (8,),
        [(g[3], fixed(g[3].shape[0], D)) for g in x_got]
        + [
            (own, fixed(8, 96, 640)),
            (swap_core(own), fixed(8, 96, 640)),
            (cos, fixed(1024, HD)),
            (sin, fixed(1024, HD)),
            (pos_col, fixed(1024, 1)),
            (pos_row, fixed(1, 1024)),
        ],
        [
            block,
            block,
            block,
            fixed(1024, HD),
            fixed(1024, HD),
            fixed(1024, D),
            fixed(D, 512),
            fixed(8, D),
            fixed(8, 128, D),
        ],
        scalars=(at,),
        scratch=[
            pltpu.VMEM((8, 2, 96, 640), bf16),
            pltpu.VMEM((1024, 512), f32),
        ],
        mib=58,
        flops=4 * 1536 * 1024 * HD + 2 * 1024 * D * 512,
        bytes_accessed=14 * 1024 * 1024,
        exps=1536 * 1024,
    )


def attend_back_kernel(
    half_ref, got, queries, lse, keys, values, cos, sin, pos_col, pos_row, grads, columns, gk, gv
):
    c, half = pl.program_id(0), half_ref[0]

    @pl.when(c == 0)
    def _():
        gk[...] = jnp.zeros_like(gk)
        gv[...] = jnp.zeros_like(gv)

    rows = pl.ds(pl.multiple_of(c * 128, 128), 128)
    part = pl.ds(pl.multiple_of(c * 128 + half * 64, 64), 64)
    rest = pl.ds(pl.multiple_of(c * 128 + (1 - half) * 64, 64), 64)
    out = got[0, :192]
    query = queries[...]
    scores = nt(query, keys[...]) * SCALE
    seen = jnp.concatenate([pos_col[rows], pos_col[part]], axis=0) >= pos_row[...]
    scores = jnp.where(seen, scores, masked_value)
    probs = jnp.exp(scores - lse[:, :1])
    grad_prob = nt(out, values[...])
    inner = jnp.sum(probs * grad_prob, axis=1, keepdims=True)
    grad_scores = (probs * (grad_prob - inner)).astype(bf16)
    grad_query = jnp.dot(grad_scores, keys[...], preferred_element_type=f32) * SCALE
    gk[...] += tn(grad_scores, query)
    gv[...] += tn(probs.astype(bf16), out)
    grads[rows, :HD] = turned(grad_query[:128], cos[rows], -sin[rows]).astype(bf16)
    grads[part, HD : 2 * HD] = turned(grad_query[128:], cos[part], -sin[part]).astype(bf16)
    grads[rest, HD : 2 * HD] = jnp.zeros((64, HD), bf16)
    columns[:, :HD] = got[0, 192:320]
    columns[pl.ds(pl.multiple_of(half * 64, 64), 64), HD:] = got[0, 320:]
    columns[pl.ds(pl.multiple_of((1 - half) * 64, 64), 64), HD:] = jnp.zeros((64, HD), bf16)

    @pl.when(c == 7)
    def _():
        grads[:, 2 * HD : 3 * HD] = turned(gk[...] * SCALE, cos[...], -sin[...]).astype(bf16)
        grads[:, 3 * HD :] = gv[...].astype(bf16)


def attend_back(half, got, queries, lse, keys, values, cos, sin, pos_col, pos_row):
    block = pl.BlockSpec((192, HD), lambda c, half: (c, 0))
    return call(
        attend_back_kernel,
        [shaped((1024, 4 * HD), bf16), shaped((1024, 2 * HD), bf16)],
        (8,),
        [
            (got, pl.BlockSpec((1, 384, HD), lambda c, half: (c, 0, 0))),
            (queries, block),
            (lse, block),
            (keys, fixed(1024, HD)),
            (values, fixed(1024, HD)),
            (cos, fixed(1024, HD)),
            (sin, fixed(1024, HD)),
            (pos_col, fixed(1024, 1)),
            (pos_row, fixed(1, 1024)),
        ],
        [fixed(1024, 4 * HD), pl.BlockSpec((128, 2 * HD), lambda c, half: (c, 0))],
        scalars=(half,),
        scratch=[pltpu.VMEM((1024, HD), f32), pltpu.VMEM((1024, HD), f32)],
        mib=58,
        flops=10 * 1536 * 1024 * HD,
        bytes_accessed=6 * 1024 * 1024,
        exps=1536 * 1024,
    )


def place_kernel(*refs):
    pieces, out = refs[:10], refs[10]
    for i, piece in enumerate(pieces):
        at = 128 * (i if i < 6 else 6 + (i - 6) // 2) + (64 if i in (7, 9) else 0)
        out[at : at + piece.shape[0]] = piece[...]


def placed(got):
    return call(
        place_kernel,
        shaped((1024, D), bf16),
        (1,),
        [(g[3], pl.BlockSpec((g[3].shape[0], D), lambda i: (0, 1))) for g in got],
        fixed(1024, D),
        bytes_accessed=4 * 1024 * D,
    )


def middle_kernel(at, *refs):
    pieces, own, other, x_first, x_second, gains = refs[:10], *refs[10:15]
    attended, normed, middle, inverse, w_out, heads, both = refs[15:]
    step, core, side = pl.program_id(0), at[10], at[11]

    @pl.when(step == 0)
    def _():
        for i in range(8):
            index = 2 * (4 * (side if i % 2 == 0 else 1 - side) + i // 2)
            w_out[index + core] = own[i]
            w_out[index + 1 - core] = other[i]
        for i, piece in enumerate(pieces):
            first = 768 if i in (7, 9) else 0
            heads[at[i], first : first + piece.shape[0]] = piece[...]

    for k in range(2):
        block = at[12 + 2 * step + k]
        rows = pl.ds(pl.multiple_of(block * 192, 64), 128)
        part = pl.ds(pl.multiple_of(block * 192 + 128, 64), 64)
        for y in range(4):
            for q in range(2):
                whole, split = HD * (3 * y + 2 * q), HD * (3 * y + 1)
                half = slice(128 * k + 64 * q, 128 * k + 64 * (q + 1))
                both[128 * k : 128 * (k + 1), whole : whole + HD] = heads[2 * y + q, rows]
                both[half, split : split + HD] = heads[2 * y + q, part]
        attended[block] = both[128 * k : 128 * (k + 1)]
    weights = w_out[...].reshape(D, D)
    x = jnp.concatenate([x_first[0], x_second[0]], axis=0).astype(f32)
    mid = x + jnp.dot(both[...], weights, preferred_element_type=f32)
    inv = lax.rsqrt(jnp.mean(mid * mid, axis=1, keepdims=True) + eps)
    normed[...] = (mid * inv * gains[1:2]).astype(bf16)

    @pl.when(step == 0)
    def _():
        middle[...] = mid[:128]
        inverse[...] = jnp.broadcast_to(inv[:128], (128, HD))


def to_middle(got, own, core, side, x, gains):
    own = own.reshape(8, 96, D)
    order = [place("y", "xl", True, step, flip) for step, flip in ORDER]
    attended, *outs, w_out = call(
        middle_kernel,
        [
            shaped((8, 128, D), bf16),
            shaped((1024, D), bf16),
            shaped((128, D), f32),
            shaped((128, HD), f32),
            shaped((16, 96, D), bf16),
        ],
        (4,),
        [(g[3], fixed(*g[3].shape)) for g in got]
        + [
            (own, fixed(8, 96, D)),
            (swap_core(own), fixed(8, 96, D)),
            (x, pl.BlockSpec((1, 128, D), lambda b, at: (at[12 + 2 * b], 0, 0))),
            (x, pl.BlockSpec((1, 128, D), lambda b, at: (at[13 + 2 * b], 0, 0))),
            (gains, fixed(8, D)),
        ],
        [
            fixed(8, 128, D),
            pl.BlockSpec((256, D), lambda b, at: (b, 0)),
            fixed(128, D),
            fixed(128, HD),
            fixed(16, 96, D),
        ],
        scalars=(
            jnp.stack([*places_of(got, "y", "xl", True), core, side, *order]).astype(jnp.int32),
        ),
        scratch=[pltpu.VMEM((8, 1536, HD), bf16), pltpu.VMEM((256, D), bf16)],
        mib=58,
        flops=2 * 1024 * D * D,
        bytes_accessed=20 * 1024 * 1024,
    )
    return attended.reshape(1024, D), *outs, w_out.reshape(D, D)


def middle_back_kernel(a, b, c, d, middle, inverse, gain, cot, w_out, grad_middle, send):
    grad_hn = a[...].astype(f32) + b[...].astype(f32) + c[...].astype(f32) + d[...].astype(f32)
    inv, mid = inverse[:, :1], middle[...]
    scaled = grad_hn * gain[1:2]
    inner = jnp.mean(mid * scaled, axis=1, keepdims=True)
    grad = cot[...].astype(f32) + inv * scaled - mid * (inv * inv * inv * inner)
    grad_middle[...] = grad
    grad_attn = grad.astype(bf16)
    heads = nt(grad_attn, w_out[...]).astype(bf16)
    for y in range(4):
        for q in range(2):
            whole, split = HD * (3 * y + 2 * q), HD * (3 * y + 1)
            half = slice(64 * q, 64 * (q + 1))
            send[2 * y + q, :128] = heads[:, whole : whole + HD]
            send[2 * y + q, 128:192] = heads[half, split : split + HD]
            send[2 * y + q, 192:320] = grad_attn[:, whole : whole + HD]
            send[2 * y + q, 320:] = grad_attn[half, split : split + HD]


def middle_back(parts, middle, inverse, gain, cot, w_out):
    row = fixed(128, D)
    return call(
        middle_back_kernel,
        [shaped((128, D), f32), shaped((8, 384, HD), bf16)],
        (1,),
        [(p, row) for p in parts]
        + [
            (middle, row),
            (inverse, fixed(128, HD)),
            (gain, fixed(8, D)),
            (cot, row),
            (w_out, fixed(D, D)),
        ],
        [row, fixed(8, 384, HD)],
        mib=50,
        flops=2 * 128 * D * D,
        bytes_accessed=10 * 1024 * 1024,
    )


def down_product_kernel(hidden_near, hidden_far, cot_near, cot_far, out):
    product = tn(hidden_near[...], cot_near[...]) + tn(hidden_far[...], cot_far[...])
    for s in range(16):
        out[s % 8, s // 8] = folded(product[72 * s : 72 * (s + 1)]).astype(bf16)


def gate_up_product_kernel(nm_near, nm_far, gate_near, gate_far, up_near, up_far, _, out):
    near, far = nm_near[...].T, nm_far[...].T
    for j, (a, b) in enumerate(((gate_near, gate_far), (up_near, up_far))):
        total = jnp.dot(near, a[...], preferred_element_type=f32)
        total = total + jnp.dot(far, b[...], preferred_element_type=f32)
        for i in range(4):
            rows = total[96 * i : 96 * (i + 1)]
            out[i, 0, :, j * WIDE : (j + 1) * WIDE] = rows.astype(bf16)


def down_product(cot, hidden):
    return call(
        down_product_kernel,
        shaped((8, 2, 96, 3 * WIDE), bf16),
        (1,),
        [(a, fixed(512, WIDE)) for a in hidden]
        + [
            (cot, pl.BlockSpec((512, D), lambda t: (0, 0))),
            (cot, pl.BlockSpec((512, D), lambda t: (1, 0))),
        ],
        pl.BlockSpec((8, 2, 96, WIDE), lambda t: (0, 0, 0, 2)),
        mib=56,
        flops=2 * 1024 * D * WIDE,
        bytes_accessed=10 * 1024 * 1024,
    )


def gate_up_product(nm, gate, up, parts):
    return call(
        gate_up_product_kernel,
        shaped((8, 2, 96, 3 * WIDE), bf16),
        (4,),
        [
            (nm, pl.BlockSpec((512, 384), lambda g: (0, g))),
            (nm, pl.BlockSpec((512, 384), lambda g: (1, g))),
        ]
        + [(a, fixed(512, WIDE)) for pair in (gate, up) for a in pair]
        + [(parts, pl.BlockSpec(memory_space=pl.ANY))],
        pl.BlockSpec((4, 1, 96, 2 * WIDE), lambda g: (g % 2, g // 2, 0, 0)),
        aliases={6: 0},
        mib=56,
        flops=2 * 1024 * D * 2 * WIDE,
        bytes_accessed=20 * 1024 * 1024,
    )


def feed_forward_kernel(
    nm, cot, w_gate, w_up, w_dn, hidden, grad_gate, grad_up, hn, total
):
    step = pl.program_id(0)
    gate = jnp.dot(nm[...], w_gate[...], preferred_element_type=f32)
    up = jnp.dot(nm[...], w_up[...], preferred_element_type=f32)
    act = nt(cot[...], w_dn[...])
    sigmoid_gate = jax.nn.sigmoid(gate)
    silu_gate = gate * sigmoid_gate
    hidden[...] = (silu_gate * up).astype(bf16)
    to_gate = (act * up * (sigmoid_gate * (1.0 + gate * (1.0 - sigmoid_gate)))).astype(bf16)
    to_up = (act * silu_gate).astype(bf16)
    grad_gate[...] = to_gate
    grad_up[...] = to_up
    term = nt(to_gate, w_gate[...]) + nt(to_up, w_up[...])

    @pl.when(step == 0)
    def _():
        total[...] = term

    @pl.when(step > 0)
    def _():
        total[...] += term

    @pl.when(step == 2)
    def _():
        hn[...] = total[...].astype(bf16)


def feed_forward(nm, cot, w_ffn, w_dn, half):
    whole, column = fixed(512, D), pl.BlockSpec((512, 384), lambda j: (0, j))
    narrow = shaped((512, WIDE), bf16)
    rows = pl.BlockSpec((512, D), lambda j: (half, 0))
    return call(
        feed_forward_kernel,
        [narrow, narrow, narrow, shaped((512, D), bf16)],
        (3,),
        [
            (nm, rows),
            (cot, rows),
            (w_ffn, pl.BlockSpec((D, 384), lambda j: (0, j))),
            (w_ffn, pl.BlockSpec((D, 384), lambda j: (0, 3 + j))),
            (w_dn, pl.BlockSpec((384, D), lambda j: (j, 0))),
        ],
        [column, column, column, whole],
        scratch=[pltpu.VMEM((512, D), f32)],
        mib=36,
        flops=2 * 512 * D * 5 * WIDE,
        bytes_accessed=20 * 1024 * 1024,
        exps=512 * WIDE,
    )


def add(a, *others):
    total = a.astype(f32)
    for other in others:
        total = total + other.astype(f32)
    return total.astype(bf16)


def scatter_stages(part, ring, pair):
    away = part(2, 1)
    half = halfway(away.shape[0])
    away, from_after, from_before = yield (
        moved(away, ring, pair, 0, 1),
        moved(part(-1, 1), ring, pair, -1, 0),
        moved(part(1, 1), ring, pair, 1, 0),
    )
    away = add(part(2, 0), away)
    away_first, away_second, got_across = yield (
        moved(away[:half], ring, pair, -1, 0),
        moved(away[half:], ring, pair, 1, 0),
        moved(add(part(0, 1), from_after, from_before), ring, pair, 0, 1),
    )
    back, ahead = part(-1, 0), part(1, 0)
    back = jnp.concatenate([add(back[:half], away_first), back[half:]], axis=0)
    ahead = jnp.concatenate([ahead[:half], add(ahead[half:], away_second)], axis=0)
    got = yield moved(back, ring, pair, -1, 0), moved(ahead, ring, pair, 1, 0)
    yield part(0, 0), got_across, *got


def scattered(part, ring, pair):
    stages = scatter_stages(part, ring, pair)
    state = next(stages)
    for _ in range(3):
        state = stages.send(state)
    return state


ORDER = [(0, 0), (0, 1), (-1, 0), (1, 0), (-1, 1), (1, 1), (2, 0), (2, 1)]


def rows_part(array):
    def part(step, flip):
        at = place("y", "xl", True, step, flip)
        return lax.dynamic_slice_in_dim(array, at * 128, 128, 0)

    return part


def ordered_part(near, far):
    def part(step, flip):
        i = ORDER.index((step, flip))
        return (near, far)[i // 4][i % 4 * 128 : (i % 4 + 1) * 128]

    return part


def tied(*values):
    return lax.optimization_barrier(values)


def call(
    kernel,
    out,
    grid,
    ins,
    outs,
    scalars=(),
    scratch=(),
    aliases=None,
    mib=16,
    flops=0,
    bytes_accessed=0,
    exps=0,
):
    return pl.pallas_call(
        kernel,
        grid_spec=pltpu.PrefetchScalarGridSpec(
            num_scalar_prefetch=len(scalars),
            grid=grid,
            in_specs=[spec for _, spec in ins],
            out_specs=outs,
            scratch_shapes=scratch,
        ),
        out_shape=out,
        input_output_aliases=aliases or {},
        compiler_params=pltpu.CompilerParams(vmem_limit_bytes=mib * 1024 * 1024),
        cost_estimate=pl.CostEstimate(
            flops=flops, bytes_accessed=bytes_accessed, transcendentals=exps
        ),
    )(*scalars, *[array for array, _ in ins])


def fixed(*shape):
    return pl.BlockSpec(shape, lambda *_: (0,) * len(shape))


def shaped(shape, dtype):
    return jax.ShapeDtypeStruct(shape, dtype)


def exchanged(blocks, axes):
    return lax.all_to_all(blocks, axes, 0, 0, tiled=True)


def swap_core(block):
    return lax.ppermute(block, "core", [(0, 1), (1, 0)])


def summed(pieces):
    return jnp.sum(pieces.astype(f32), axis=0)


def mm(a, b):
    return jnp.dot(a, b, preferred_element_type=f32)


def mm_nt(a, b):
    return jnp.einsum("ik,jk->ij", a, b, preferred_element_type=f32)


def mm_tn(a, b):
    return jnp.einsum("ki,kj->ij", a, b, preferred_element_type=f32)


def shards(
    hidden_in, block_order, attn_gain, w_qkv, b_qkv, w_out, mlp_gain, w_gate_up, w_down, cotangent
):
    yi, qi = lax.axis_index("y"), lax.axis_index("xl")
    ci = 2 * yi + qi
    fi = lax.axis_index(FSDP)
    core = lax.axis_index("core")
    group = yi // 2
    half = qi.astype(jnp.int32)[None]
    x_own, cot_own = hidden_in[0], cotangent[0]

    heads = [3 * yi + 2 * qi, 3 * yi + 1, H + group, H + KVH + group]
    vectors = [jnp.pad(attn_gain, (0, 32)), jnp.pad(mlp_gain, (0, 32)), b_qkv]
    packed = packed_columns(heads, w_qkv, vectors)

    order = block_order[0]
    positions = (order[:, None] * 64 + jnp.arange(64, dtype=jnp.int32)[None, :]).reshape(1024)
    frequency = jnp.exp(jnp.arange(0, HD, 2, dtype=f32) * (-math.log(rope_base) / HD))
    angles = positions.astype(f32)[:, None] * frequency[None, :]
    cosine, sine = jnp.cos(angles), jnp.sin(angles)
    cosine = jnp.concatenate([cosine, cosine], axis=1)
    sine = jnp.concatenate([-sine, sine], axis=1)
    pos_col, pos_row = positions[:, None], positions[None, :]

    def both_sides(block):
        return jnp.stack([block, lax.ppermute(block, "xh", [(0, 1), (1, 0)])])

    def along_z(sides):
        return exchanged(jnp.broadcast_to(sides, (4,) + sides.shape), ("z",))

    packed = both_sides(packed)
    w_out = both_sides(w_out)
    x_gather = gather_stages(jnp.concatenate([x_own, cot_own], axis=1), "y", "xl", True)
    *x_state, packed, w_down, w_gate_up_later, cosine, sine = tied(
        *next(x_gather), packed, w_down, w_gate_up, cosine, sine
    )
    own = along_z(packed)
    *x_state, own, w_out = tied(*x_gather.send(x_state), own, w_out)
    own_out = along_z(w_out)
    x_got = x_gather.send(x_gather.send(x_state))

    down = lax.dynamic_slice_in_dim(w_down, PART * ci, PART, 0)
    down = folded(jnp.concatenate([down, jnp.zeros((2, D), bf16)], axis=0))
    ffn_own = jnp.concatenate([picked(ci, w_gate_up_later), down], axis=1)
    w_ffn = lax.all_gather(ffn_own, FSDP, axis=0, tiled=True)

    att_mine, queries, lse, keys, values, normed_all, w_mine, gains, x_all = attend(
        x_got, own, core, qi, heads, cosine, sine, pos_col, pos_row
    )
    att_gather = gather_stages(att_mine, "y", "xl")
    *att_state, cot_all = tied(*next(att_gather), placed(x_got))
    *att_state, own_out, w_dn = tied(*att_gather.send(att_state), own_out, down_weights(w_ffn))
    att_got = att_gather.send(att_gather.send(att_state))
    attended_all, nm_all, middle, inv_second, w_out_all = to_middle(
        att_got, own_out, core, lax.axis_index("xh"), x_all, gains
    )

    hidden_far, gate_far, up_far, hn_far = feed_forward(nm_all, cot_all, w_ffn, w_dn, 1)
    hidden_near, gate_near, up_near, hn_near = feed_forward(nm_all, cot_all, w_ffn, w_dn, 0)
    hn_stages = scatter_stages(ordered_part(hn_near, hn_far), "y", "xl")
    *state, cot_all, hidden_near, hidden_far = tied(
        *next(hn_stages), cot_all, hidden_near, hidden_far
    )
    ffn_parts = down_product(cot_all, (hidden_near, hidden_far))
    *state, nm_all, gate_near, gate_far, up_near, up_far = tied(
        *hn_stages.send(state), nm_all, gate_near, gate_far, up_near, up_far
    )
    ffn_parts = gate_up_product(nm_all, (gate_near, gate_far), (up_near, up_far), ffn_parts)
    ffn_sides = lax.psum_scatter(ffn_parts, ("z", "core"), scatter_dimension=0, tiled=True)[0]
    hn_parts = hn_stages.send(hn_stages.send(state))
    *hn_parts, out_near, out_far = tied(
        *hn_parts, mm(hidden_near, w_dn).astype(bf16), mm(hidden_far, w_dn).astype(bf16)
    )

    grad_middle, send = middle_back(hn_parts, middle, inv_second, gains, cot_own, w_out_all)
    got = exchanged(send, CTX)
    gp_mine, columns = attend_back(
        half, got, queries, lse, keys, values, cosine, sine, pos_col, pos_row
    )
    given, kept = attention_products(core, normed_all, attended_all, gp_mine, columns)
    mine_both = add(kept, swap_core(given))
    mine_both, xn_part = tied(mine_both, mm_nt(gp_mine, w_mine).astype(bf16))
    mine_sides = summed(exchanged(mine_both, ("z",))).astype(bf16)
    xn_of, out_of = rows_part(xn_part), ordered_part(out_near, out_far)
    xn_out = scattered(
        lambda step, flip: jnp.concatenate([xn_of(step, flip), out_of(step, flip)], axis=1),
        "y",
        "xl",
    )
    xn_out = sum(term.astype(f32) for term in xn_out)
    grad_xn = xn_out[:, :D]
    hidden_out = middle + xn_out[:, D:]
    sides = jnp.concatenate([ffn_sides, mine_sides], axis=2)
    side = lax.axis_index("xh")
    weight_sum = add(
        lax.dynamic_index_in_dim(sides, side, 0, keepdims=False),
        lax.ppermute(
            lax.dynamic_index_in_dim(sides, 1 - side, 0, keepdims=False), "xh", [(0, 1), (1, 0)]
        ),
    )
    resid = x_own.astype(f32)
    inv_first = lax.rsqrt(jnp.mean(resid * resid, axis=-1, keepdims=True) + eps)
    scaled = grad_xn * gains[:1]
    grad_in = (
        grad_middle
        + inv_first * scaled
        - resid * (inv_first**3) * jnp.mean(resid * scaled, axis=-1, keepdims=True)
    )

    own_gains = jnp.stack([jnp.pad(g.astype(f32), (0, 32)) for g in (mlp_gain, attn_gain)])
    grad_w_gate_up, grad_w_down, grad_w_qkv, grad_w_out, vectors = weight_gradients(
        gather_eight(weight_sum, "y", "xl"),
        w_gate_up,
        w_qkv,
        jnp.pad(own_gains, ((0, 6), (0, 0)), constant_values=1.0),
        fi,
    )
    grad_mlp_gain, grad_attn_gain, grad_b_qkv = vectors[0, :96], vectors[1, :96], vectors[2]

    return (
        hidden_out[None],
        grad_in[None],
        grad_attn_gain,
        grad_w_qkv,
        grad_b_qkv,
        grad_w_out,
        grad_mlp_gain,
        grad_w_gate_up,
        grad_w_down,
    )


def solution(mesh):
    fine = Mesh(mesh.devices.reshape(4, 2, 2, 4, 2), CTX + FSDP)
    rows = P(FSDP, CTX, None)
    vector = P(FSDP)
    matrix = P(FSDP, None)
    return jax.shard_map(
        shards,
        mesh=fine,
        in_specs=(rows, matrix, vector, matrix, vector, matrix, vector, matrix, matrix, rows),
        out_specs=(rows, rows, vector, matrix, vector, matrix, vector, matrix, matrix),
        check_vma=False,
    )
```
